32 devices in a mesh: expert: 8 (over z, y), tensor: 4 (over x, core).
Axes of the slice: x: 2, y: 2, z: 4, core: 2. Of those that a mesh axis runs over, the one named last changes fastest.
Arguments:
- tokens: bfloat16 [4096, 2048], P('expert'), may hold values from -6 to 6
- lengths: int32 [8], P('expert'), may hold values from 256 to 512, as said below
- routes: int32 [4096, 6], P('expert'), may hold values from 0 to 15, all different within a row; in each aligned block of 512 rows (0 to 511, 512 to 1023, ...) at most 288 rows name the same one
- gain_attn: float32 [2048], replicated, may hold values from 0.1 to 1.9
- w_query: bfloat16 [2048, 3072], P('expert', 'tensor'), may hold values from -0.125 to 0.125
- w_latent: bfloat16 [2048, 576], replicated, may hold values from -0.125 to 0.125
- gain_latent: float32 [512], replicated, may hold values from 0.1 to 1.9
- w_kv: bfloat16 [512, 4096], P('expert', 'tensor'), may hold values from -0.25 to 0.25
- w_out: bfloat16 [2048, 2048], P('tensor', 'expert'), may hold values from -0.5 to 0.5
- gain_ffn: float32 [2048], replicated, may hold values from 0.1 to 1.9
- w_router: bfloat16 [2048, 16], replicated, may hold values from -0.0625 to 0.0625
- w_shared_gate: bfloat16 [2048, 2816], P('expert', 'tensor'), may hold values from -0.125 to 0.125
- w_shared_up: bfloat16 [2048, 2816], P('expert', 'tensor'), may hold values from -0.125 to 0.125
- w_shared_down: bfloat16 [2816, 2048], P('tensor', 'expert'), may hold values from -0.109375 to 0.109375
- w_gate: bfloat16 [16, 2048, 1408], P('expert', None, 'tensor'), may hold values from -0.125 to 0.125
- w_up: bfloat16 [16, 2048, 1408], P('expert', None, 'tensor'), may hold values from -0.125 to 0.125
- w_down: bfloat16 [16, 1408, 2048], P('expert', 'tensor'), may hold values from -6 to 6
- cotangent: bfloat16 [4096, 2048], P('expert'), may hold values from -6 to 6
Outputs:
- output: bfloat16 [4096, 2048], P('expert')
- grad_tokens: bfloat16 [4096, 2048], P('expert')
- grad_gain_attn: float32 [2048], replicated
- grad_query: float32 [2048, 3072], P('expert', 'tensor')
- grad_latent: float32 [2048, 576], replicated
- grad_gain_latent: float32 [512], replicated
- grad_kv: float32 [512, 4096], P('expert', 'tensor')
- grad_out: float32 [2048, 2048], P('tensor', 'expert')
- grad_gain_ffn: float32 [2048], replicated
- grad_router: float32 [2048, 16], replicated
- grad_shared_gate: float32 [2048, 2816], P('expert', 'tensor')
- grad_shared_up: float32 [2048, 2816], P('expert', 'tensor')
- grad_shared_down: float32 [2816, 2048], P('tensor', 'expert')
- grad_gate: float32 [16, 2048, 1408], P('expert', None, 'tensor')
- grad_up: float32 [16, 2048, 1408], P('expert', None, 'tensor')
- grad_down: float32 [16, 1408, 2048], P('expert', 'tensor')
The draws below stay inside these ranges and needn't reach their ends.
Inputs may be any that keep to these rules, and one draw needn't show every extreme that they name: Group g of the expert axis holds one causal sequence in its first lengths[g] rows; the rest of its 512 rows is padding; some group's sequence fills all 512 rows. `routes`: each row names 6 different experts; within the rows of one group no expert is named more than 288 times, a bound that some block reaches.
All inputs are finite; a program needn't handle non-finite values.
Results may differ from the reference program's by a relative error of at most 0.028.
Values may be sent and summed in bfloat16 or wider, within the bound.
A program may use at most 384 MiB of HBM per device.

```python
import math
import jax
import jax.numpy as jnp
import numpy as np
from jax import lax

D = 2048
HEADS = 16
NOPE = 128
ROPE = 64
VD = 128
KVR = 512
FF = 1408
SFF = 2816
TOP = 6
ROWS = 512
EXPERTS = 16
GROUPS = 8
TOKENS = 4096
CAP = 288
MIN_LEN = 256
FF_DEV = 352
N_TENSOR = 4


def draw_lengths(key, part):
    key = jax.random.fold_in(key, 11)
    first, second = jax.random.split(key)
    values = jax.random.randint(first, (GROUPS,), MIN_LEN, ROWS + 1)
    longest = jax.random.randint(second, (), 0, GROUPS)
    return jnp.where(jnp.arange(GROUPS) == longest, ROWS, values).astype(jnp.int32)


def levels(rng, extent, cuts, low, largest):
    factor_of = 1.0
    for axis_at, shards_of in cuts:
        heights = jax.random.uniform(jax.random.fold_in(jax.random.fold_in(rng, 6), axis_at), (shards_of,), jnp.float32, low / len(cuts), largest / len(cuts))
        factor_of = factor_of * jnp.repeat(jnp.exp(heights), extent[axis_at] // shards_of).reshape((-1,) + (1,) * (len(extent) - 1 - axis_at))
    return factor_of


def routed_block(own_key, own, number, rows, count, top, most, slope):
    ranking = jax.random.permutation(own_key, count)
    heavy_load, usual = portions_of(count, rows * top, most, slope, True), portions_of(count, rows * top, most, slope, False)
    places = jnp.arange(count)

    def named(tallies, rotation):
        used = int((tallies > 0).sum())
        fixed = max(1, used // 4)
        moved = fixed + (places - fixed + rotation * (used - fixed)) % max(1, count - fixed)
        return jnp.zeros((count,), jnp.int32).at[ranking[jnp.where(places < fixed, places, moved)]].set(jnp.asarray(tallies, jnp.int32))

    tallies = jnp.where(number % 4 == 0, named(heavy_load, number // 4), named(usual, number - number // 4 - 1))
    mixed = jax.random.permutation(jax.random.fold_in(own, 3), count)
    source_of, receiver = mixed[0:count // 2 * 2:2], mixed[1:count // 2 * 2:2]
    room = jnp.minimum(tallies[source_of] - 1, most - tallies[receiver]) // 2
    room = jnp.where((source_of == ranking[0]) | (receiver == ranking[0]) | (tallies[receiver] == 0), 0, jnp.maximum(room, 0))
    moved = jax.random.randint(jax.random.fold_in(own, 4), (count // 2,), 0, 1 << 20) % (room + 1)
    tallies = tallies.at[source_of].add(-moved).at[receiver].add(moved)
    members = jnp.searchsorted(jnp.cumsum(tallies), jnp.arange(rows * top), side="right").astype(jnp.int32)
    listing = members.reshape(top, rows).T
    listing = listing[jax.random.permutation(jax.random.fold_in(own, 1), rows)]
    rotation = jax.random.randint(jax.random.fold_in(own, 2), (rows, 1), 0, top)
    return jnp.take_along_axis(listing, (jnp.arange(top)[None, :] + rotation) % top, axis=1)


def portions_of(amount, total, limit, slope, full):
    loads = [(1 << 20) // math.isqrt(rank ** slope) + 1 for rank in range(1, amount + 1)]
    largest = limit if full else min(limit, max(-(-total // amount), total * loads[0] // sum(loads)))
    least = 1 if total - largest >= amount - 1 else 0
    given, rest = [largest] + [least] * (amount - 1), total - largest - least * (amount - 1)
    while rest > 0:
        free = [i for i in range(1, amount) if given[i] < largest] or [i for i in range(1, amount) if given[i] < limit]
        whole, budget = sum([loads[i] for i in free]), rest
        for i in free:
            extra = min(limit - given[i], max(1, budget * loads[i] // whole), rest)
            given[i] = given[i] + extra
            rest = rest - extra
    return np.array(given)


def centred(key, dims, scale, most, pieces=(), held_as=jnp.bfloat16):
    values = scale * jax.random.normal(key, dims, jnp.float32)
    if pieces:
        values = values * levels(key, dims, pieces, -0.22, 0.18)
    return jnp.clip(values, -most, most).astype(held_as)


def setup_inputs(seed: int = 0) -> dict:
    seeds = jax.random.split(jax.random.key(seed), 19)
    tokens = centred(seeds[0], (TOKENS, D), 1.0, 6.0, ((0, 8),))
    lengths = draw_lengths(jax.random.fold_in(seeds[18], 71), 0)
    routes_keys = jax.random.split(jax.random.fold_in(seeds[2], 1), TOKENS // ROWS)
    routes_turns = jax.random.permutation(jax.random.fold_in(seeds[2], 3), TOKENS // ROWS)
    routes = jax.vmap(lambda own, number: routed_block(jax.random.fold_in(seeds[2], 2), own, number, ROWS, EXPERTS, TOP, CAP, 2))(routes_keys, routes_turns).reshape((TOKENS, TOP))
    gain_attn = jnp.clip(1.0 + 0.18 * jax.random.normal(seeds[3], (D,), jnp.float32), 0.1, 1.9)
    w_query = centred(seeds[4], (D, HEADS * (NOPE + ROPE)), D ** -0.5, 0.125, ((0, 8), (1, 4)))
    w_latent = centred(seeds[5], (D, KVR + ROPE), D ** -0.5, 0.125)
    gain_latent = jnp.clip(1.0 + 0.18 * jax.random.normal(seeds[6], (KVR,), jnp.float32), 0.1, 1.9)
    w_kv = centred(seeds[7], (KVR, HEADS * (NOPE + VD)), KVR ** -0.5, 0.25, ((0, 8), (1, 4)))
    w_out = centred(seeds[8], (HEADS * VD, D), (HEADS * VD // 16) ** -0.5, 0.5, ((0, 4), (1, 8)))
    gain_ffn = jnp.clip(1.0 + 0.18 * jax.random.normal(seeds[9], (D,), jnp.float32), 0.1, 1.9)
    w_router = centred(seeds[10], (D, EXPERTS), (4 * D) ** -0.5, 0.0625)
    w_shared_gate = centred(seeds[11], (D, SFF), D ** -0.5, 0.125, ((0, 8), (1, 4)))
    w_shared_up = centred(seeds[12], (D, SFF), D ** -0.5, 0.125, ((0, 8), (1, 4)))
    w_shared_down = centred(seeds[13], (SFF, D), SFF ** -0.5, 0.109375, ((0, 4), (1, 8)))
    w_gate = centred(seeds[14], (EXPERTS, D, FF), D ** -0.5, 0.125, ((0, 8), (2, 4)))
    w_up = centred(seeds[15], (EXPERTS, D, FF), D ** -0.5, 0.125, ((0, 8), (2, 4)))
    w_down = centred(seeds[16], (EXPERTS, FF, D), (max(FF // 1024, 1)) ** -0.5, 6.0, ((0, 8), (1, 4)))
    cotangent = centred(seeds[17], (TOKENS, D), 1.0, 6.0, ((0, 8),))
    return dict(tokens=tokens, lengths=lengths, routes=routes, gain_attn=gain_attn, w_query=w_query, w_latent=w_latent, gain_latent=gain_latent, w_kv=w_kv, w_out=w_out, gain_ffn=gain_ffn, w_router=w_router, w_shared_gate=w_shared_gate, w_shared_up=w_shared_up, w_shared_down=w_shared_down, w_gate=w_gate, w_up=w_up, w_down=w_down, cotangent=cotangent)


@jax.custom_vjp
def low(v):
    return lax.optimization_barrier(v.astype(jnp.bfloat16)).astype(jnp.float32)

@jax.custom_vjp
def low_back(v):
    return v

def low_keep(v):
    return (low(v), None)

def low_pass(kept, grad):
    return (grad,)

def back_keep(v):
    return (v, None)

def back_low(kept, grad):
    return (low(grad),)
low.defvjp(low_keep, low_pass)
low_back.defvjp(back_keep, back_low)
EPS = 1e-06
ROPE_BASE = 10000.0
HIGH = lax.Precision.HIGHEST

def mult(a, b):
    return jnp.dot(a, b, precision=HIGH, preferred_element_type=jnp.float32)

def inv_rms(v):
    return lax.rsqrt(lax.optimization_barrier(jnp.mean(v * v, axis=-1, keepdims=True)) + EPS)

def rope_tables(count, width):
    half = width // 2
    freq = ROPE_BASE ** (-(jnp.arange(half, dtype=jnp.float32) * 2.0 / width))
    angle = jnp.arange(count, dtype=jnp.float32)[:, None] * freq[None, :]
    return (jnp.cos(angle), jnp.sin(angle))

def rotate(v, cosine, sine):
    half = v.shape[-1] // 2
    first = v[..., :half]
    second = v[..., half:]
    return jnp.concatenate([first * cosine - second * sine, second * cosine + first * sine], axis=-1)

def reference(tokens, lengths, routes, gain_attn, w_query, w_latent, gain_latent, w_kv, w_out, gain_ffn, w_router, w_shared_gate, w_shared_up, w_shared_down, w_gate, w_up, w_down, cotangent):
    live_int = (jnp.arange(ROWS)[None, :] < lengths[:, None]).astype(jnp.int32)
    live = live_int.astype(jnp.float32)[..., None]
    entries = ROWS * TOP
    marks = (routes.reshape(GROUPS, ROWS, TOP)[..., None] == jnp.arange(EXPERTS)[None, None, None, :]).astype(jnp.int32)
    marks = (marks * live_int[:, :, None, None]).reshape(GROUPS, entries, EXPERTS)
    rank = lax.optimization_barrier(jnp.sum((jnp.cumsum(marks, axis=1) - marks) * marks, axis=-1))
    flat_ids = routes.reshape(GROUPS, entries)
    valid = jnp.repeat(live_int, TOP, axis=1) > 0
    group_ids = jnp.arange(GROUPS)[:, None]
    span = GROUPS * CAP
    slot = jnp.where(valid, flat_ids * span + group_ids * CAP + rank, EXPERTS * span).astype(jnp.int32)
    token_of_entry = (group_ids * ROWS + jnp.arange(entries)[None, :] // TOP).astype(jnp.int32)
    table = jnp.full((EXPERTS * span + 1,), TOKENS, jnp.int32).at[slot.reshape(-1)].set(token_of_entry.reshape(-1))
    table = table[:EXPERTS * span].reshape(EXPERTS, span)
    slot_rows = slot.reshape(TOKENS, TOP)
    cosine, sine = rope_tables(ROWS, ROPE)
    causal = jnp.arange(ROWS)[:, None] >= jnp.arange(ROWS)[None, :]
    score_scale = (NOPE + ROPE) ** (-0.5)

    def forward(xf, g1, wq, wkva, gkv, wkvb, wo, g2, wr, wsg, wsu, wsd, weg, weu, wed):

        def attend(xn):
            qraw = low_back(mult(xn, wq)).reshape(ROWS, HEADS, NOPE + ROPE)
            query = low(jnp.concatenate([qraw[..., :NOPE], rotate(qraw[..., NOPE:], cosine[:, None, :], sine[:, None, :])], axis=-1))
            latent = mult(xn, wkva)
            comp = latent[:, :KVR]
            compressed = low(comp * inv_rms(comp) * gkv)
            key_rope = low(rotate(latent[:, KVR:], cosine, sine))
            key_value = low_back(low(mult(compressed, wkvb))).reshape(ROWS, HEADS, NOPE + VD)
            keys = jnp.concatenate([key_value[..., :NOPE], jnp.broadcast_to(key_rope[:, None, :], (ROWS, HEADS, ROPE))], axis=-1)
            raw = jnp.einsum('qhd,khd->hqk', query, keys, precision=HIGH)
            scores = jnp.where(causal[None], low_back(raw) * score_scale, -1e+30)
            probs = low(jax.nn.softmax(scores, axis=-1))
            attended = jnp.einsum('hqk,khd->qhd', probs, key_value[..., NOPE:], precision=HIGH)
            attended = low_back(low(attended)).reshape(ROWS, HEADS * VD)
            return low_back(mult(attended, wo))
        xg = xf.reshape(GROUPS, ROWS, D)
        xn1 = low(xg * inv_rms(xg) * g1)
        attn = lax.map(jax.checkpoint(attend), xn1)
        resid = xg + live * attn
        xn2 = low(resid * inv_rms(resid) * g2).reshape(TOKENS, D)
        router = jax.nn.softmax(mult(xn2, wr), axis=-1)
        choose = (routes[..., None] == jnp.arange(EXPERTS)[None, None, :]).astype(jnp.float32)
        gates = lax.optimization_barrier(jnp.sum(choose * router[:, None, :], axis=-1)) * live.reshape(TOKENS, 1)
        shared_h = low(jax.nn.silu(low_back(mult(xn2, wsg))) * low_back(mult(xn2, wsu)))
        shared = mult(shared_h, wsd)
        padded = jnp.concatenate([xn2, jnp.zeros((1, D), jnp.float32)], axis=0)

        def expert(item):
            index, wg, wu, wd = item
            copy = low_back(padded[index])
            hidden = low(jax.nn.silu(low_back(mult(copy, wg))) * low_back(mult(copy, wu)))
            parts = jnp.einsum('ntf,tfd->tnd', hidden.reshape(span, N_TENSOR, FF_DEV), wd.reshape(N_TENSOR, FF_DEV, D), precision=HIGH)
            return low_back(lax.optimization_barrier(jnp.sum(low(parts), axis=0)))
        expert_rows = lax.map(jax.checkpoint(expert), (table, weg, weu, wed))
        outs = jnp.concatenate([expert_rows.reshape(EXPERTS * span, D), jnp.zeros((1, D), jnp.float32)], axis=0)
        picked = outs[slot_rows]
        routed = lax.optimization_barrier(jnp.sum(picked * gates[..., None], axis=1))
        ffn = low_back(routed + shared)
        return resid.reshape(TOKENS, D) + live.reshape(TOKENS, 1) * ffn
    primals = (tokens.astype(jnp.float32), gain_attn, w_query.astype(jnp.float32), w_latent.astype(jnp.float32), gain_latent, w_kv.astype(jnp.float32), w_out.astype(jnp.float32), gain_ffn, w_router.astype(jnp.float32), w_shared_gate.astype(jnp.float32), w_shared_up.astype(jnp.float32), w_shared_down.astype(jnp.float32), w_gate.astype(jnp.float32), w_up.astype(jnp.float32), w_down.astype(jnp.float32))
    result, pullback = jax.vjp(forward, *primals)
    grads = pullback(cotangent.astype(jnp.float32))
    return (result.astype(jnp.bfloat16), grads[0].astype(jnp.bfloat16), grads[1], grads[2], grads[3], grads[4], grads[5], grads[6], grads[7], grads[8], grads[9], grads[10], grads[11], grads[12], grads[13], grads[14])
```

```python
import functools

import jax
import jax.numpy as jnp
from jax import lax
from jax.experimental import pallas as pl
from jax.experimental.pallas import tpu as pltpu
from jax.sharding import PartitionSpec as P

F32, BF16 = jnp.float32, jnp.bfloat16

NOPE = 128
ROPE = 64
VD = 128
KVR = 512


EPS = 1e-06
ROPE_BASE = 10000.0


def inv_rms(v):
    return lax.rsqrt(jnp.mean(v * v, axis=-1, keepdims=True) + EPS)


def rope_tables(count, width):
    half = width // 2
    freq = ROPE_BASE ** (-(jnp.arange(half, dtype=jnp.float32) * 2.0 / width))
    angle = jnp.arange(count, dtype=jnp.float32)[:, None] * freq[None, :]
    return (jnp.cos(angle), jnp.sin(angle))


def rotate(v, cosine, sine):
    half = v.shape[-1] // 2
    first = v[..., :half]
    second = v[..., half:]
    return jnp.concatenate(
        [first * cosine - second * sine, second * cosine + first * sine], axis=-1
    )


def rotate_back(grad, cosine, sine):
    half = grad.shape[-1] // 2
    first = grad[..., :half]
    second = grad[..., half:]
    return jnp.concatenate(
        [first * cosine + second * sine, second * cosine - first * sine], axis=-1
    )


def norm_back(grad, normed, scale_row, gain):
    weighted = grad * gain
    return scale_row * (weighted - normed * jnp.mean(weighted * normed, axis=-1, keepdims=True))


def silu_parts(gate):
    sig = jax.nn.sigmoid(gate)
    return (gate * sig, sig * (1.0 + gate * (1.0 - sig)))


def mat(left, right):
    return jnp.dot(left, right, preferred_element_type=jnp.float32)


def mat_tn(left, right):
    return lax.dot_general(
        left, right, (((0,), (0,)), ((), ())), preferred_element_type=jnp.float32
    )


def mat_nt(left, right):
    return lax.dot_general(
        left, right, (((1,), (1,)), ((), ())), preferred_element_type=jnp.float32
    )


MESH = pl.DeviceIdType.MESH


def places():
    e, t = lax.axis_index("expert"), lax.axis_index("tensor")
    return e // 2, e % 2, t // 2, t % 2


def device(e1, e0, t1, t0):
    return (e1 * 2 + e0, t1 * 2 + t0)


def slot_of(e1, e0, t1, t0):
    return ((e1 * 2 + e0) * 2 + t1) * 2 + t0


def greet(peers):
    barrier = pltpu.get_barrier_semaphore()
    for peer in peers:
        pl.semaphore_signal(barrier, inc=1, device_id=peer, device_id_type=MESH)
    pl.semaphore_wait(barrier, len(peers))


def all_peers(far):
    e1, e0, t1, t0 = places()
    peers = [device((e1 + r) % far, e0, t1, t0) for r in range(1, far)]
    peers += [device(e1, 1 - e0, t1, t0), device(e1, e0, 1 - t1, t0), device(e1, e0, t1, 1 - t0)]
    return peers


def gather_kernel(far, x_ref, out_ref, send, recv, own):
    e1, e0, t1, t0 = places()
    m = x_ref.shape[0]
    half = m // 2
    greet(all_peers(far))
    mine = pltpu.make_async_copy(x_ref, out_ref.at[slot_of(e1, e0, t1, t0)], own)
    mine.start()
    ylink, xlink, core = (
        device(e1, 1 - e0, t1, t0),
        device(e1, e0, 1 - t1, t0),
        device(e1, e0, t1, 1 - t0),
    )

    def rel(r, b, c):
        return slot_of((e1 - r) % far, (e0 + b) % 2, (t1 + c) % 2, t0)

    def at_z(p, r):
        return p * 8 * far + r

    def at_1(p, r):
        return p * 8 * far + far + r

    def at_2(p, r, k):
        return p * 8 * far + 2 * far + 2 * r + k

    def at_c(p, r, k):
        return p * 8 * far + 4 * far + 4 * r + k

    started = []

    def send_piece(p, r, b, c, sem, to):
        rows = pl.ds(p * half, half)
        place = rel(r, b, c)
        src = x_ref.at[rows] if (r, b, c) == (0, 0, 0) else out_ref.at[place, rows]
        copy = pltpu.make_async_remote_copy(
            src_ref=src,
            dst_ref=out_ref.at[place, rows],
            send_sem=send.at[sem],
            recv_sem=recv.at[sem],
            device_id=to,
            device_id_type=MESH,
        )
        copy.start()
        started.append(copy)

    def wait_piece(p, sem):
        rows = pl.ds(p * half, half)
        pltpu.make_async_copy(x_ref.at[rows], out_ref.at[0, rows], recv.at[sem]).wait()

    for r in range(1, far):
        for p in range(2):
            send_piece(p, 0, 0, 0, at_z(p, r), device((e1 + r) % far, e0, t1, t0))
    firsts, seconds = (ylink, xlink), (xlink, ylink)

    def stage_a(r):
        for p in range(2):
            if r:
                wait_piece(p, at_z(p, r))
            send_piece(p, r, 0, 0, at_1(p, r), firsts[p])
            send_piece(p, r, 0, 0, at_2(p, r, 0), seconds[p])
        for p in range(2):
            send_piece(p, r, 0, 0, at_c(p, r, 0), core)

    def stage_b(r):
        for p in range(2):
            b, c = (1, 0) if p == 0 else (0, 1)
            wait_piece(p, at_1(p, r))
            send_piece(p, r, b, c, at_2(p, r, 1), seconds[p])
            send_piece(p, r, b, c, at_c(p, r, 1), core)

    def stage_c(r):
        for p in range(2):
            b, c = (0, 1) if p == 0 else (1, 0)
            wait_piece(p, at_2(p, r, 0))
            send_piece(p, r, b, c, at_c(p, r, 2), core)
            wait_piece(p, at_2(p, r, 1))
            send_piece(p, r, 1, 1, at_c(p, r, 3), core)

    for step in range(far + 2):
        if step < far:
            stage_a(step)
        if 0 <= step - 1 < far:
            stage_b(step - 1)
        if 0 <= step - 2 < far:
            stage_c(step - 2)
    for r in range(far):
        for p in range(2):
            for k in range(4):
                wait_piece(p, at_c(p, r, k))
    for copy in started:
        copy.wait_send()
    mine.wait()


def gather_all(x, groups, tensors, ident):
    m, width = x.shape
    far = groups // 2
    n = groups * tensors
    return pl.pallas_call(
        functools.partial(gather_kernel, far),
        out_shape=jax.ShapeDtypeStruct((n, m, width), x.dtype),
        in_specs=[pl.BlockSpec(memory_space=pl.ANY)],
        out_specs=pl.BlockSpec(memory_space=pl.ANY),
        scratch_shapes=[
            pltpu.SemaphoreType.DMA((16 * far,)),
            pltpu.SemaphoreType.DMA((16 * far,)),
            pltpu.SemaphoreType.DMA,
        ],
        compiler_params=pltpu.CompilerParams(collective_id=ident, has_side_effects=True),
    )(x)


def reduce_kernel(far, p_ref, out_ref, acc, rc, r1, r2, rz, load_sem, send, recv):
    e1, e0, t1, t0 = places()
    m = out_ref.shape[0]
    half = m // 2
    ylink, xlink, core = (
        device(e1, 1 - e0, t1, t0),
        device(e1, e0, 1 - t1, t0),
        device(e1, e0, t1, 1 - t0),
    )

    def dest(r, b, c, d):
        return slot_of((e1 + r) % far, (e0 + b) % 2, (t1 + c) % 2, (t0 + d) % 2)

    def plane(r, b, c):
        return r * 4 + b * 2 + c

    places_in_turn = [(1, 1), (0, 1), (1, 0), (0, 0)]
    turn = list(range(far - 1, -1, -1))
    loads = {}
    for r in turn:
        for b, c in places_in_turn:
            k = plane(r, b, c)
            copy = pltpu.make_async_copy(p_ref.at[dest(r, b, c, 0)], acc.at[k], load_sem.at[k])
            copy.start()
            loads[k] = copy
    greet(all_peers(far))
    started = []

    def push(src, dst, sem, to):
        copy = pltpu.make_async_remote_copy(
            src_ref=src,
            dst_ref=dst,
            send_sem=send.at[sem],
            recv_sem=recv.at[sem],
            device_id=to,
            device_id_type=MESH,
        )
        copy.start()
        started.append(copy)

    def arrived(ref, sem):
        pltpu.make_async_copy(ref, ref, recv.at[sem]).wait()

    def add(k, base, count, ref):
        @pl.loop(0, count // 16)
        def _(i):
            rows = pl.ds(pl.multiple_of(base + i * 16, 16), 16)
            there = pl.ds(pl.multiple_of(i * 16, 16), 16)
            acc[k, rows, :] = acc[k, rows, :] + ref[there, :]

    c_base, s1_base, s2_base, z_base = 0, 4 * far, 8 * far, 10 * far
    for r in turn:
        for b, c in places_in_turn:
            k = plane(r, b, c)
            push(p_ref.at[dest(r, b, c, 1)], rc.at[k], c_base + k, core)

    rows_of = (pl.ds(0, half), pl.ds(half, half))

    def stage_a(r):
        for b, c in places_in_turn:
            k = plane(r, b, c)
            loads[k].wait()
            arrived(rc.at[k], c_base + k)
            add(k, 0, m, rc.at[k])
            if c == 1:
                at = r * 2 + b
                push(acc.at[k, rows_of[0]], r1.at[0, at], s1_base + at, xlink)
            if b == 1:
                at = r * 2 + c
                push(acc.at[k, rows_of[1]], r1.at[1, at], s1_base + 2 * far + at, ylink)

    def stage_b(r):
        for j in (1, 0):
            at = r * 2 + j
            k = plane(r, j, 0)
            arrived(r1.at[0, at], s1_base + at)
            add(k, 0, half, r1.at[0, at])
            if j == 1:
                push(acc.at[k, rows_of[0]], r2.at[0, r], s2_base + r, ylink)
            k = plane(r, 0, j)
            arrived(r1.at[1, at], s1_base + 2 * far + at)
            add(k, half, half, r1.at[1, at])
            if j == 1:
                push(acc.at[k, rows_of[1]], r2.at[1, r], s2_base + far + r, xlink)

    def stage_c(r):
        k = plane(r, 0, 0)
        for p in range(2):
            arrived(r2.at[p, r], s2_base + p * far + r)
            add(k, p * half, half, r2.at[p, r])
        if r:
            push(acc.at[k], rz.at[r - 1], z_base + r, device((e1 + r) % far, e0, t1, t0))

    for step in range(far + 2):
        if step < far:
            stage_a(turn[step])
        if 0 <= step - 1 < far:
            stage_b(turn[step - 1])
        if 0 <= step - 2 < far:
            stage_c(turn[step - 2])
    for r in range(1, far):
        arrived(rz.at[r - 1], z_base + r)

    @pl.loop(0, m // 16)
    def _(i):
        rows = pl.ds(pl.multiple_of(i * 16, 16), 16)
        total = acc[0, rows, :].astype(F32)
        for r in range(1, far):
            total = total + rz[r - 1, rows, :].astype(F32)
        out_ref[rows, :] = total

    for copy in started:
        copy.wait_send()


def reduce_all(p, groups, tensors, ident):
    n, m, width = p.shape
    far = groups // 2
    return pl.pallas_call(
        functools.partial(reduce_kernel, far),
        out_shape=jax.ShapeDtypeStruct((m, width), F32),
        in_specs=[pl.BlockSpec(memory_space=pl.ANY)],
        out_specs=pl.BlockSpec(memory_space=pltpu.VMEM),
        scratch_shapes=[
            pltpu.VMEM((4 * far, m, width), BF16),
            pltpu.VMEM((4 * far, m, width), BF16),
            pltpu.VMEM((2, 2 * far, m // 2, width), BF16),
            pltpu.VMEM((2, far, m // 2, width), BF16),
            pltpu.VMEM((far - 1, m, width), BF16),
            pltpu.SemaphoreType.DMA((4 * far,)),
            pltpu.SemaphoreType.DMA((11 * far,)),
            pltpu.SemaphoreType.DMA((11 * far,)),
        ],
        compiler_params=pltpu.CompilerParams(
            collective_id=ident, has_side_effects=True, vmem_limit_bytes=56 * 2**20
        ),
    )(p)


TILE = 32


def dot_nt(left, right):
    return lax.dot_general(left, right, (((1,), (1,)), ((), ())), preferred_element_type=F32)


def dot_nn(left, right):
    return lax.dot_general(left, right, (((1,), (0,)), ((), ())), preferred_element_type=F32)


def ffn_kernel(
    counts,
    x_ref, dy_ref, picks_ref, wg_hbm, wu_hbm, wd_hbm, ws_hbm, wr_hbm,
    ffn_ref, dx_ref, dgates_ref, gg_hbm, gu_hbm, gd_hbm, gs_hbm,
    w_in, w_down, h, dh, hs, dgu, hsn, dgun, acc_in, acc_down, sem,
):
    experts, hidden, shared, total = counts
    routed = experts * hidden
    units = routed + shared
    step = pl.program_id(0)
    last = pl.num_programs(0) - 1
    block, width = x_ref.shape

    def loads():
        pairs = []
        for e in range(experts):
            at = pl.ds(e * hidden, hidden)
            pairs.append((wg_hbm.at[e], w_in.at[at]))
            pairs.append((wu_hbm.at[e], w_in.at[pl.ds(units + e * hidden, hidden)]))
            pairs.append((wd_hbm.at[e], w_down.at[at]))
        pairs.append((ws_hbm.at[0], w_in.at[pl.ds(routed, shared)]))
        pairs.append((ws_hbm.at[1], w_in.at[pl.ds(units + routed, shared)]))
        pairs.append((ws_hbm.at[2], w_down.at[pl.ds(routed, shared)]))
        pairs.append((wr_hbm, w_in.at[pl.ds(2 * units, total)]))
        return [pltpu.make_async_copy(a, b, sem.at[i]) for i, (a, b) in enumerate(pairs)]

    @pl.when(step == 0)
    def _():
        for c in loads():
            c.start()
        acc_in[...] = jnp.zeros_like(acc_in)
        acc_down[...] = jnp.zeros_like(acc_down)
        dgu[2 * units :, :] = jnp.zeros((dgu.shape[0] - 2 * units, block), BF16)
        hs[units:, :] = jnp.zeros((hs.shape[0] - units, block), BF16)
        for c in loads():
            c.wait()

    @pl.loop(0, block // 256)
    def _(n):
        at = pl.ds(pl.multiple_of(n * 256, 256), 256)
        h[:, at] = dot_nt(w_in[: 2 * units + total, :], x_ref[at, :])
        dh[:, at] = dot_nt(w_down[:units, :], dy_ref[at, :])

    logits = h[2 * units : 2 * units + total, :]
    expo = jnp.exp(logits - jnp.max(logits, axis=0, keepdims=True))
    gates = expo / jnp.sum(expo, axis=0, keepdims=True) * picks_ref[...]
    rows = []
    for s in range(experts + 1):
        base, count = (s * hidden, hidden) if s < experts else (routed, shared)
        gate = gates[s : s + 1, :] if s < experts else jnp.ones((1, block), F32)

        def body(i, total_):
            a = pl.multiple_of(base + i * TILE, TILE)
            here = pl.ds(a, TILE)
            there = pl.ds(pl.multiple_of(units + a, TILE), TILE)
            hg, hu, d = h[here, :], h[there, :], dh[here, :]
            sig = 1.0 / (1.0 + jnp.exp(-hg))
            act = hg * sig
            dact = sig + act * (1.0 - sig)
            hid = act * hu
            hs[here, :] = (hid * gate).astype(BF16)
            ds = d * gate
            dgu[here, :] = (ds * hu * dact).astype(BF16)
            dgu[there, :] = (ds * act).astype(BF16)
            return total_ + jnp.sum(hid * d, axis=0, keepdims=True)

        rows.append(lax.fori_loop(0, count // TILE, body, jnp.zeros((1, block), F32)))
    rows = rows[:experts]
    dgates_ref[...] = jnp.concatenate(rows + [jnp.zeros((8 - experts, block), F32)], axis=0)
    hsn[...] = hs[...].T
    dgun[...] = dgu[...].T

    @pl.loop(0, width // 256)
    def _(c):
        at = pl.ds(pl.multiple_of(c * 256, 256), 256)
        acc_in[:, at] += dot_nn(dgu[: 2 * units, :], x_ref[:, at])
        acc_down[:, at] += dot_nn(hs[:units, :], dy_ref[:, at])
        dx_ref[:, at] = dot_nn(dgun[:, : 2 * units], w_in[: 2 * units, at]).astype(BF16)
        ffn_ref[:, at] = dot_nn(hsn[:, :units], w_down[:, at]).astype(BF16)

    def stores():
        pairs = []
        for e in range(experts):
            at = pl.ds(e * hidden, hidden)
            pairs.append((acc_in.at[at], gg_hbm.at[e]))
            pairs.append((acc_in.at[pl.ds(units + e * hidden, hidden)], gu_hbm.at[e]))
            pairs.append((acc_down.at[at], gd_hbm.at[e]))
        pairs.append((acc_in.at[pl.ds(routed, shared)], gs_hbm.at[0]))
        pairs.append((acc_in.at[pl.ds(units + routed, shared)], gs_hbm.at[1]))
        pairs.append((acc_down.at[pl.ds(routed, shared)], gs_hbm.at[2]))
        return [pltpu.make_async_copy(a, b, sem.at[i]) for i, (a, b) in enumerate(pairs)]

    @pl.when(step == last)
    def _():
        for c in stores():
            c.start()
        for c in stores():
            c.wait()


def ffn_local(x, dy, picks, wg, wu, wd, ws, wr, block=512):
    n, width = x.shape
    experts, hidden, _ = wg.shape
    shared, total = ws.shape[1], wr.shape[0]
    units = experts * hidden + shared
    up = lambda v: -(-v // 128) * 128
    any_ = pl.BlockSpec(memory_space=pl.ANY)
    return pl.pallas_call(
        functools.partial(ffn_kernel, (experts, hidden, shared, total)),
        grid=(n // block,),
        in_specs=[
            pl.BlockSpec((block, width), lambda i: (i, 0)),
            pl.BlockSpec((block, width), lambda i: (i, 0)),
            pl.BlockSpec((total, block), lambda i: (0, i)),
            any_, any_, any_, any_, any_,
        ],
        out_specs=[
            pl.BlockSpec((block, width), lambda i: (i, 0)),
            pl.BlockSpec((block, width), lambda i: (i, 0)),
            pl.BlockSpec((8, block), lambda i: (0, i)),
            any_, any_, any_, any_,
        ],
        out_shape=[
            jax.ShapeDtypeStruct((n, width), BF16),
            jax.ShapeDtypeStruct((n, width), BF16),
            jax.ShapeDtypeStruct((8, n), F32),
            jax.ShapeDtypeStruct(wg.shape, F32),
            jax.ShapeDtypeStruct(wu.shape, F32),
            jax.ShapeDtypeStruct(wd.shape, F32),
            jax.ShapeDtypeStruct(ws.shape, F32),
        ],
        scratch_shapes=[
            pltpu.VMEM((2 * units + total, width), BF16),
            pltpu.VMEM((units, width), BF16),
            pltpu.VMEM((2 * units + total, block), F32),
            pltpu.VMEM((units, block), F32),
            pltpu.VMEM((up(units), block), BF16),
            pltpu.VMEM((up(2 * units), block), BF16),
            pltpu.VMEM((block, up(units)), BF16),
            pltpu.VMEM((block, up(2 * units)), BF16),
            pltpu.VMEM((2 * units, width), F32),
            pltpu.VMEM((units, width), F32),
            pltpu.SemaphoreType.DMA((3 * experts + 4,)),
        ],
        compiler_params=pltpu.CompilerParams(vmem_limit_bytes=63 * 2**20),
        cost_estimate=pl.CostEstimate(flops=18 * n * units * width, bytes_accessed=n * width * 8, transcendentals=0),
    )(x, dy, picks, wg, wu, wd, ws, wr)


BOTH = ("expert", "tensor")


def shards(
    tokens,
    lengths,
    routes,
    gain_attn,
    w_query,
    w_latent,
    gain_latent,
    w_kv,
    w_out,
    gain_ffn,
    w_router,
    w_shared_gate,
    w_shared_up,
    w_shared_down,
    w_gate,
    w_up,
    w_down,
    cotangent,
):
    groups = lax.axis_size("expert")
    tensors = lax.axis_size("tensor")
    eindex = lax.axis_index("expert")
    tindex = lax.axis_index("tensor")
    rows, width = tokens.shape
    quarter = rows // tensors
    experts_local, _, hidden_units = w_gate.shape
    total_experts = experts_local * groups
    every = groups * rows
    bf16, f32 = jnp.bfloat16, jnp.float32

    def own(v):
        return lax.dynamic_slice_in_dim(v, tindex * quarter, quarter, 0)

    live_int = (jnp.arange(rows) < lengths[0]).astype(jnp.int32)
    live = live_int.astype(f32)[:, None]
    live_own = own(live)
    cot_own = own(cotangent).astype(f32)
    dffn_own = (cot_own * live_own).astype(bf16)

    query_w = lax.all_gather(w_query, "expert", axis=0, tiled=True)
    kv_up = lax.all_gather(w_kv, "expert", axis=0, tiled=True)
    out_proj = lax.all_gather(w_out, "expert", axis=1, tiled=True)

    part = w_shared_down.shape[0] // groups
    spare = -part % TILE

    def shared_units(v):
        v = jnp.pad(v.reshape(groups, part, v.shape[1]), ((0, 0), (0, spare), (0, 0)))
        return v

    shared_w = jnp.stack(
        [shared_units(v) for v in (w_shared_gate.T, w_shared_up.T, w_shared_down)], axis=1
    )
    shared_w = lax.all_to_all(shared_w, "expert", split_axis=0, concat_axis=0, tiled=True)
    shared_w = shared_w.transpose(1, 2, 0, 3).reshape(3, part + spare, width)
    gate_t, up_t = w_gate.transpose(0, 2, 1), w_up.transpose(0, 2, 1)
    router_t = jnp.roll(w_router.T, -eindex * experts_local, axis=0)
    parts = max(1, every // 4096)
    some = quarter // parts

    def split(v):
        return v.reshape(parts, some, v.shape[1])

    choose = jnp.any(own(routes)[..., None] == jnp.arange(total_experts), axis=1).astype(F32)
    picks = choose * live_own
    picks_all = lax.all_gather(split(picks), BOTH, axis=1, tiled=True)
    picks_all = jnp.roll(picks_all.transpose(0, 2, 1), -eindex * experts_local, axis=1)
    dffn = [lax.all_gather(v, BOTH, axis=0, tiled=True) for v in split(dffn_own)]

    heads = out_proj.shape[0] // VD
    xf = tokens.astype(f32)
    scale_one = inv_rms(xf)
    normed_one = xf * scale_one
    xn1 = (normed_one * gain_attn).astype(bf16)
    cosine, sine = rope_tables(rows, ROPE)
    qfull = mat(xn1, query_w).reshape(rows, heads, NOPE + ROPE)
    qcat = jnp.concatenate(
        [qfull[..., :NOPE], rotate(qfull[..., NOPE:], cosine[:, None, :], sine[:, None, :])],
        axis=-1,
    ).astype(bf16)
    latent = mat(xn1, w_latent)
    comp = latent[:, :KVR]
    scale_lat = inv_rms(comp)
    normed_lat = comp * scale_lat
    compressed = (normed_lat * gain_latent).astype(bf16)
    key_rope = rotate(latent[:, KVR:], cosine, sine).astype(bf16)
    key_value = mat(compressed, kv_up).astype(bf16).reshape(rows, heads, NOPE + VD)
    keys = jnp.concatenate(
        [key_value[..., :NOPE], jnp.broadcast_to(key_rope[:, None, :], (rows, heads, ROPE))],
        axis=-1,
    )
    values = key_value[..., NOPE:]
    causal = jnp.arange(rows)[:, None] >= jnp.arange(rows)[None, :]
    score_scale = (NOPE + ROPE) ** (-0.5)
    raw = jnp.einsum("qhd,khd->hqk", qcat, keys, preferred_element_type=f32) * score_scale
    score_now = jnp.where(causal[None], raw, -jnp.inf)
    peak = jnp.max(score_now, axis=-1, keepdims=True)
    expo = jnp.exp(score_now - peak)
    pfull = expo / jnp.sum(expo, axis=-1, keepdims=True)
    probs = pfull.astype(bf16)
    attended = (
        jnp.einsum("hqk,khd->qhd", probs, values, preferred_element_type=f32)
        .astype(bf16)
        .reshape(rows, heads * VD)
    )
    attn = lax.psum_scatter(
        mat(attended, out_proj).astype(bf16), "tensor", scatter_dimension=0, tiled=True
    ).astype(f32)
    resid = own(xf) + live_own * attn
    scale_two = inv_rms(resid)
    normed_two = resid * scale_two
    xn2_own = (normed_two * gain_ffn).astype(bf16)
    router = jax.nn.softmax(mat(xn2_own, w_router), axis=-1)
    outs = []
    for k in range(parts):
        xn2 = gather_all(split(xn2_own)[k], groups, tensors, 3 * k).reshape(-1, width)
        ffn, dx, dgates, *grads = ffn_local(
            xn2, dffn[k], picks_all[k], gate_t, up_t, w_down, shared_w, router_t
        )
        dgates = lax.dynamic_update_slice_in_dim(
            jnp.zeros((xn2.shape[0], total_experts), F32),
            dgates[:experts_local].T,
            eindex * experts_local,
            1,
        )
        dgates = lax.psum_scatter(dgates, BOTH, scatter_dimension=0, tiled=True)
        dx = reduce_all(dx.reshape(-1, some, width), groups, tensors, 3 * k + 1)
        ffn = reduce_all(ffn.reshape(-1, some, width), groups, tensors, 3 * k + 2)
        outs.append((ffn, dx, dgates, *grads))
    ffn, dx, dgates = (jnp.concatenate(v, axis=0) for v in list(zip(*outs))[:3])
    grads = [functools.reduce(jnp.add, v) for v in list(zip(*outs))[3:]]
    drouter = picks * dgates
    output = lax.all_gather(
        (resid + live_own * ffn).astype(bf16), "tensor", axis=0, tiled=True
    )
    grad_gate, grad_up = (v.transpose(0, 2, 1) for v in grads[:2])
    grad_down = grads[2]
    shared_g = grads[3][:, :part].astype(BF16).reshape(3, part, groups, width // groups)
    shared_g = lax.all_to_all(
        shared_g.transpose(2, 0, 1, 3), "expert", split_axis=0, concat_axis=0, tiled=True
    )
    shared_g = shared_g.transpose(1, 0, 2, 3).reshape(3, groups * part, width // groups)
    grad_sgate, grad_sup, grad_sdown = shared_g[0].T, shared_g[1].T, shared_g[2]
    grad_sgate, grad_sup, grad_sdown = (
        v.astype(F32) for v in (grad_sgate, grad_sup, grad_sdown)
    )
    dlogit = router * (drouter - jnp.sum(router * drouter, axis=-1, keepdims=True))
    grad_router = mat_tn(xn2_own, dlogit.astype(bf16))
    dnorm_two = dx + mat_nt(dlogit.astype(bf16), w_router)
    grad_gain_ffn = jnp.sum(dnorm_two * normed_two, axis=0)
    dresid = cot_own + norm_back(dnorm_two, normed_two, scale_two, gain_ffn)
    dattn = lax.all_gather((dresid * live_own).astype(bf16), "tensor", axis=0, tiled=True)
    grad_out = mat_tn(attended, dattn)
    dattended = mat_nt(dattn, out_proj).astype(bf16).reshape(rows, heads, VD)
    dvalues = jnp.einsum("hqk,qhd->khd", probs, dattended, preferred_element_type=f32)
    dprobs = jnp.einsum("qhd,khd->hqk", dattended, values, preferred_element_type=f32)
    dscore = (
        pfull * (dprobs - jnp.sum(pfull * dprobs, axis=-1, keepdims=True)) * score_scale
    ).astype(bf16)
    dquery = jnp.einsum("hqk,khd->qhd", dscore, keys, preferred_element_type=f32)
    dkeys = jnp.einsum("hqk,qhd->khd", dscore, qcat, preferred_element_type=f32)
    dkv = (
        jnp.concatenate([dkeys[..., :NOPE], dvalues], axis=-1)
        .astype(bf16)
        .reshape(rows, heads * (NOPE + VD))
    )
    grad_kv = mat_tn(compressed, dkv)
    dcomp = mat_nt(dkv, kv_up)
    grad_gain_latent = jnp.sum(dcomp * normed_lat, axis=0)
    dlatent = jnp.concatenate(
        [
            norm_back(dcomp, normed_lat, scale_lat, gain_latent),
            rotate_back(jnp.sum(dkeys[..., NOPE:], axis=1), cosine, sine),
        ],
        axis=-1,
    ).astype(bf16)
    dqfull = jnp.concatenate(
        [dquery[..., :NOPE], rotate_back(dquery[..., NOPE:], cosine[:, None, :], sine[:, None, :])],
        axis=-1,
    )
    dqfull = dqfull.astype(bf16).reshape(rows, heads * (NOPE + ROPE))
    grad_query = mat_tn(xn1, dqfull)
    grad_latent = mat_tn(xn1, dlatent)
    dnorm_one = mat_nt(dqfull, query_w) + mat_nt(dlatent, w_latent)
    dnorm_one = lax.psum_scatter(
        dnorm_one.astype(bf16), "tensor", scatter_dimension=0, tiled=True
    ).astype(f32)
    normed_own = own(normed_one)
    grad_gain_attn = jnp.sum(dnorm_one * normed_own, axis=0)
    grad_tokens = (dresid + norm_back(dnorm_one, normed_own, own(scale_one), gain_attn)).astype(bf16)
    grad_tokens = lax.all_gather(grad_tokens, "tensor", axis=0, tiled=True)
    small = jnp.concatenate(
        [
            grad_latent,
            grad_router,
            grad_gain_attn[:, None],
            grad_gain_ffn[:, None],
            jnp.pad(grad_gain_latent, (0, width - KVR))[:, None],
        ],
        axis=1,
    ).astype(bf16)
    pad = -small.shape[1] % 128
    small = jnp.pad(small, ((0, 0), (0, pad)))
    small = lax.psum_scatter(small, BOTH, scatter_dimension=0, tiled=True)
    small = lax.all_gather(small, BOTH, axis=0, tiled=True).astype(f32)
    at = w_latent.shape[1]
    grad_latent = small[:, :at]
    grad_router = small[:, at : at + total_experts]
    at = at + total_experts
    grad_gain_attn = small[:, at]
    grad_gain_ffn = small[:, at + 1]
    grad_gain_latent = small[:KVR, at + 2]
    grad_query = lax.psum_scatter(
        grad_query.astype(bf16), "expert", scatter_dimension=0, tiled=True
    ).astype(f32)
    grad_kv = lax.psum_scatter(
        grad_kv.astype(bf16), "expert", scatter_dimension=0, tiled=True
    ).astype(f32)
    grad_out = lax.psum_scatter(
        grad_out.astype(bf16), "expert", scatter_dimension=1, tiled=True
    ).astype(f32)
    return (
        output,
        grad_tokens,
        grad_gain_attn,
        grad_query,
        grad_latent,
        grad_gain_latent,
        grad_kv,
        grad_out,
        grad_gain_ffn,
        grad_router,
        grad_sgate,
        grad_sup,
        grad_sdown,
        grad_gate,
        grad_up,
        grad_down,
    )


def solution(mesh):
    in_specs = (
        P("expert", None),
        P("expert"),
        P("expert", None),
        P(),
        P("expert", "tensor"),
        P(),
        P(),
        P("expert", "tensor"),
        P("tensor", "expert"),
        P(),
        P(),
        P("expert", "tensor"),
        P("expert", "tensor"),
        P("tensor", "expert"),
        P("expert", None, "tensor"),
        P("expert", None, "tensor"),
        P("expert", "tensor", None),
        P("expert", None),
    )
    out_specs = (
        P("expert", None),
        P("expert", None),
        P(),
        P("expert", "tensor"),
        P(),
        P(),
        P("expert", "tensor"),
        P("tensor", "expert"),
        P(),
        P(),
        P("expert", "tensor"),
        P("expert", "tensor"),
        P("tensor", "expert"),
        P("expert", None, "tensor"),
        P("expert", None, "tensor"),
        P("expert", "tensor", None),
    )
    return jax.shard_map(shards, mesh=mesh, in_specs=in_specs, out_specs=out_specs, check_vma=False)
```

```python
import functools

import jax
import jax.numpy as jnp
from jax import lax
from jax.experimental import pallas as pl
from jax.experimental.pallas import tpu as pltpu
from jax.sharding import PartitionSpec as P

F32, BF16 = jnp.float32, jnp.bfloat16

NOPE = 128
ROPE = 64
VD = 128
KVR = 512


EPS = 1e-06
ROPE_BASE = 10000.0


def inv_rms(v):
    return lax.rsqrt(jnp.mean(v * v, axis=-1, keepdims=True) + EPS)


def rope_tables(count, width):
    half = width // 2
    freq = ROPE_BASE ** (-(jnp.arange(half, dtype=jnp.float32) * 2.0 / width))
    angle = jnp.arange(count, dtype=jnp.float32)[:, None] * freq[None, :]
    return (jnp.cos(angle), jnp.sin(angle))


def rotate(v, cosine, sine):
    half = v.shape[-1] // 2
    first = v[..., :half]
    second = v[..., half:]
    return jnp.concatenate(
        [first * cosine - second * sine, second * cosine + first * sine], axis=-1
    )


def rotate_back(grad, cosine, sine):
    half = grad.shape[-1] // 2
    first = grad[..., :half]
    second = grad[..., half:]
    return jnp.concatenate(
        [first * cosine + second * sine, second * cosine - first * sine], axis=-1
    )


def norm_back(grad, normed, scale_row, gain):
    weighted = grad * gain
    return scale_row * (weighted - normed * jnp.mean(weighted * normed, axis=-1, keepdims=True))


def silu_parts(gate):
    sig = jax.nn.sigmoid(gate)
    return (gate * sig, sig * (1.0 + gate * (1.0 - sig)))


def mat(left, right):
    return jnp.dot(left, right, preferred_element_type=jnp.float32)


def mat_tn(left, right):
    return lax.dot_general(
        left, right, (((0,), (0,)), ((), ())), preferred_element_type=jnp.float32
    )


def mat_nt(left, right):
    return lax.dot_general(
        left, right, (((1,), (1,)), ((), ())), preferred_element_type=jnp.float32
    )


MESH = pl.DeviceIdType.MESH
ANY = pl.BlockSpec(memory_space=pl.ANY)
IN_VMEM = pl.BlockSpec(memory_space=pltpu.VMEM)


def places():
    e, t = lax.axis_index("expert"), lax.axis_index("tensor")
    return e // 2, e % 2, t // 2, t % 2


class Net:
    def __init__(self, far, send, recv, local):
        self.far, self.send, self.recv, self.local = far, send, recv, local
        self.e1, self.e0, self.t1, self.t0 = places()
        self.count, self.started, self.locals = 0, [], 0
        self.core = self.at(d=1)
        self.x = self.at(c=1)
        self.y = self.at(b=1)

    def at(self, r=0, b=0, c=0, d=0):
        e = (self.e1 + r + self.far) % self.far * 2 + (self.e0 + b) % 2
        return (e, (self.t1 + c) % 2 * 2 + (self.t0 + d) % 2)

    def slot(self, r=0, b=0, c=0, d=0):
        e, t = self.at(r, b, c, d)
        return e * 4 + t

    def group(self, r=0, b=0):
        return self.at(r, b)[0]

    def greet(self, peers):
        barrier = pltpu.get_barrier_semaphore()
        for peer in peers:
            pl.semaphore_signal(barrier, inc=1, device_id=peer, device_id_type=MESH)
        pl.semaphore_wait(barrier, len(peers))

    def near(self):
        return [self.at(r) for r in range(1, self.far)] + [self.y, self.x, self.core]

    def line(self):
        every = [self.at(r, b) for r in range(self.far) for b in range(2)]
        return every[1:]

    def push(self, src, dst, to):
        k = self.count
        self.count += 1
        copy = pltpu.make_async_remote_copy(
            src_ref=src,
            dst_ref=dst,
            send_sem=self.send.at[k],
            recv_sem=self.recv.at[k],
            device_id=to,
            device_id_type=MESH,
        )
        copy.start()
        self.started.append(copy)
        return k

    def arrived(self, ref, k):
        pltpu.make_async_copy(ref, ref, self.recv.at[k]).wait()

    def load(self, src, dst):
        copy = pltpu.make_async_copy(src, dst, self.local.at[self.locals])
        self.locals += 1
        copy.start()
        return copy

    def finish(self):
        for copy in self.started:
            copy.wait_send()


def add_rows(dst, src, step=16):
    @pl.loop(0, dst.shape[0] // step)
    def _(i):
        rows = pl.ds(pl.multiple_of(i * step, step), step)
        dst[rows, :] = dst[rows, :] + src[rows, :]


class GatherAll:
    def __init__(self, net, own, out_at, order):
        self.net, self.own, self.out_at, self.order = net, own, out_at, order
        self.z, self.first, self.second, self.cores = {}, {}, {}, {}

    def place(self, r, u, v, d=0):
        b, c = (u, v) if self.order == "yx" else (v, u)
        return self.out_at(self.net.slot(-r, b, c, d))

    def pass_on(self, r, u, v, to):
        here = self.own if (r, u, v) == (0, 0, 0) else self.place(r, u, v)
        return self.net.push(here, self.place(r, u, v), to)

    def start(self):
        for r in range(1, self.net.far):
            self.z[r] = self.pass_on(0, 0, 0, self.net.at(r))
        self.links = (self.net.y, self.net.x)[:: 1 if self.order == "yx" else -1]

    def stage_a(self, r):
        if r:
            self.net.arrived(self.place(r, 0, 0), self.z[r])
        self.first[r] = self.pass_on(r, 0, 0, self.links[0])
        self.second[r, 0] = self.pass_on(r, 0, 0, self.links[1])
        self.cores[r, 0, 0] = self.pass_on(r, 0, 0, self.net.core)

    def stage_b(self, r):
        self.net.arrived(self.place(r, 1, 0), self.first[r])
        self.second[r, 1] = self.pass_on(r, 1, 0, self.links[1])
        self.cores[r, 1, 0] = self.pass_on(r, 1, 0, self.net.core)

    def stage_c(self, r):
        for u in range(2):
            self.net.arrived(self.place(r, u, 1), self.second[r, u])
            self.cores[r, u, 1] = self.pass_on(r, u, 1, self.net.core)

    def steps(self):
        return [self.stage_a, self.stage_b, self.stage_c]

    def end(self):
        for (r, u, v), k in self.cores.items():
            self.net.arrived(self.place(r, u, v, 1), k)


class ReduceAll:
    def __init__(self, net, part_at, acc, from_core, from_first, from_second, from_z, order):
        self.net, self.part_at, self.acc, self.order = net, part_at, acc, order
        self.bufs = (from_core, from_first, from_second, from_z)
        self.core, self.first, self.second, self.z, self.loads = {}, {}, {}, {}, {}
        self.turn = list(range(net.far - 1, -1, -1))
        self.spots = ((1, 1), (0, 1), (1, 0), (0, 0))
        self.links = (net.x, net.y) if order == "xy" else (net.y, net.x)

    def dest(self, r, u, v, d):
        b, c = (v, u) if self.order == "xy" else (u, v)
        return self.part_at(self.net.slot(r, b, c, d))

    def load(self):
        for r in self.turn:
            for u, v in self.spots:
                k = r * 4 + u * 2 + v
                self.loads[k] = self.net.load(self.dest(r, u, v, 0), self.acc.at[k])

    def start(self):
        for r in self.turn:
            for u, v in self.spots:
                k = r * 4 + u * 2 + v
                self.core[k] = self.net.push(
                    self.dest(r, u, v, 1), self.bufs[0].at[k], self.net.core
                )

    def merge(self, k, buf, i, token):
        self.net.arrived(buf.at[i], token)
        add_rows(self.acc.at[k], buf.at[i])

    def stage_a(self, i):
        r = self.turn[i]
        for u, v in self.spots:
            k = r * 4 + u * 2 + v
            self.loads[k].wait()
            self.merge(k, self.bufs[0], k, self.core[k])
            if u:
                at = r * 2 + v
                self.first[at] = self.net.push(
                    self.acc.at[k], self.bufs[1].at[at], self.links[0]
                )

    def stage_b(self, i):
        r = self.turn[i]
        for v in (1, 0):
            at = r * 2 + v
            self.merge(r * 4 + v, self.bufs[1], at, self.first[at])
            if v:
                self.second[r] = self.net.push(
                    self.acc.at[r * 4 + v], self.bufs[2].at[r], self.links[1]
                )

    def stage_c(self, i):
        r = self.turn[i]
        self.merge(r * 4, self.bufs[2], r, self.second[r])
        if r:
            self.z[r] = self.net.push(
                self.acc.at[r * 4], self.bufs[3].at[r - 1], self.net.at(r)
            )

    def steps(self):
        return [self.stage_a, self.stage_b, self.stage_c]

    def end(self):
        for r in range(1, self.net.far):
            self.net.arrived(self.bufs[3].at[r - 1], self.z[r])

    def total(self, rows):
        total = self.acc[0, rows, :].astype(F32)
        for r in range(1, self.net.far):
            total = total + self.bufs[3][r - 1, rows, :].astype(F32)
        return total

    @staticmethod
    def scratch(far, rows, width):
        return [
            pltpu.VMEM((4 * far, rows, width), BF16),
            pltpu.VMEM((4 * far, rows, width), BF16),
            pltpu.VMEM((2 * far, rows, width), BF16),
            pltpu.VMEM((far, rows, width), BF16),
            pltpu.VMEM((far - 1, rows, width), BF16),
        ]


def pipelined(far, parts):
    for i in range(far + 2):
        for s in range(3):
            for part in parts:
                if 0 <= i - s < far:
                    part.steps()[s](i - s)


def semaphores(remote, local):
    return [
        pltpu.SemaphoreType.DMA((remote,)),
        pltpu.SemaphoreType.DMA((remote,)),
        pltpu.SemaphoreType.DMA((local,)),
    ]


def cost(us):
    return pl.CostEstimate(flops=0, bytes_accessed=us * 3_000_000, transcendentals=0)


def params(ident, mib=60):
    return pltpu.CompilerParams(
        collective_id=ident, has_side_effects=True, vmem_limit_bytes=mib * 2**20
    )


def begin_kernel(far, *refs):
    n = 3
    ws, blocks, marks = refs[:n], refs[n], refs[n + 1]
    outs, blocks_out, marks_out = refs[n + 2 : 2 * n + 2], refs[2 * n + 2], refs[2 * n + 3]
    net = Net(far, *refs[2 * n + 4 :])
    me = net.group()
    mine = [net.load(w, o.at[me]) for w, o in zip(ws, outs)]
    mine.append(net.load(blocks.at[me], blocks_out.at[me]))
    mine.append(net.load(marks, marks_out.at[me]))
    net.greet(net.line())
    tokens = {}
    others = [(r, b) for r in range(far) for b in range(2)][1:]
    for a, (w, o) in enumerate(zip(ws, outs)):
        for r in range(1, far):
            tokens[a, r] = net.push(w, o.at[me], net.at(r))
        tokens[a, 0, 1] = net.push(w, o.at[me], net.y)
    small = []
    for r, b in others:
        small.append((r, b, marks_out, net.push(marks, marks_out.at[me], net.at(r, b))))
    for a, (w, o) in enumerate(zip(ws, outs)):
        for r in range(1, far):
            place = o.at[net.group(-r)]
            net.arrived(place, tokens[a, r])
            tokens[a, r, 1] = net.push(place, place, net.y)
    for r, b in others:
        to = net.at(r, b)
        small.append((r, b, blocks_out, net.push(blocks.at[to[0]], blocks_out.at[me], to)))
    for a, o in enumerate(outs):
        for r in range(far):
            net.arrived(o.at[net.group(-r, 1)], tokens[a, r, 1])
    for r, b, ref, k in small:
        net.arrived(ref.at[net.group(-r, b)], k)
    net.finish()
    for copy in mine:
        copy.wait()


def begin(ws, blocks, marks, groups, ident):
    far = groups // 2
    outs = [jax.ShapeDtypeStruct((groups, *w.shape), w.dtype) for w in ws]
    outs.append(jax.ShapeDtypeStruct(blocks.shape, blocks.dtype))
    outs.append(jax.ShapeDtypeStruct((groups, *marks.shape), marks.dtype))
    return pl.pallas_call(
        functools.partial(begin_kernel, far),
        out_shape=outs,
        in_specs=[ANY] * 5,
        out_specs=[ANY] * 5,
        scratch_shapes=semaphores(10 * far, 5),
        compiler_params=params(ident),
        cost_estimate=cost(100),
    )(*ws, blocks, marks)


class ReduceGroups:
    def __init__(self, net, part, out, acc, from_y, from_z):
        self.net, self.part, self.out = net, part, out
        self.acc, self.from_y, self.from_z = acc, from_y, from_z
        self.turn = list(range(net.far - 1, -1, -1))

    def load(self):
        self.loads = {
            r: self.net.load(self.part.at[self.net.group(r)], self.acc.at[r]) for r in self.turn
        }

    def start(self):
        self.y = {
            r: self.net.push(self.part.at[self.net.group(r, 1)], self.from_y.at[r], self.net.y)
            for r in self.turn
        }
        self.z = {}

    def step(self, i):
        r = self.turn[i]
        self.loads[r].wait()
        self.net.arrived(self.from_y.at[r], self.y[r])
        add_rows(self.acc.at[r], self.from_y.at[r])
        if r:
            self.z[r] = self.net.push(self.acc.at[r], self.from_z.at[r - 1], self.net.at(r))

    def end(self):
        for r in range(1, self.net.far):
            self.net.arrived(self.from_z.at[r - 1], self.z[r])

        @pl.loop(0, self.out.shape[0] // 16)
        def _(i):
            rows = pl.ds(pl.multiple_of(i * 16, 16), 16)
            total = self.acc[0, rows, :].astype(F32)
            for r in range(1, self.net.far):
                total = total + self.from_z[r - 1, rows, :].astype(F32)
            self.out[rows, :] = total

    @staticmethod
    def scratch(far, rows, width):
        return [
            pltpu.VMEM((far, rows, width), BF16),
            pltpu.VMEM((far, rows, width), BF16),
            pltpu.VMEM((far - 1, rows, width), BF16),
        ]


class GatherTensor:
    def __init__(self, net, own, out):
        self.net, self.own, self.out = net, own, out

    def place(self, c, d):
        return self.out.at[self.net.at(0, 0, c, d)[1]]

    def start(self):
        net = self.net
        self.mine = net.load(self.own, self.place(0, 0))
        self.x = net.push(self.own, self.place(0, 0), net.x)
        self.c0 = net.push(self.own, self.place(0, 0), net.core)

    def step(self):
        self.net.arrived(self.place(1, 0), self.x)
        self.c1 = self.net.push(self.place(1, 0), self.place(1, 0), self.net.core)

    def end(self):
        self.net.arrived(self.place(0, 1), self.c0)
        self.net.arrived(self.place(1, 1), self.c1)
        self.mine.wait()


class ReduceTensor:
    def __init__(self, net, part, acc, from_core, from_x):
        self.net, self.part = net, part
        self.acc, self.from_core, self.from_x = acc, from_core, from_x

    def at(self, c, d):
        return self.part.at[self.net.at(0, 0, c, d)[1]]

    def load(self):
        self.loads = [self.net.load(self.at(c, 0), self.acc.at[c]) for c in (1, 0)]

    def start(self):
        self.core = [
            self.net.push(self.at(c, 1), self.from_core.at[c], self.net.core) for c in (1, 0)
        ]

    def step(self):
        for i, c in enumerate((1, 0)):
            self.loads[i].wait()
            self.net.arrived(self.from_core.at[c], self.core[i])
            add_rows(self.acc.at[c], self.from_core.at[c])
            if c:
                self.x = self.net.push(self.acc.at[c], self.from_x, self.net.x)

    def end(self):
        self.net.arrived(self.from_x, self.x)

    def total(self, rows):
        return self.acc[0, rows, :].astype(F32) + self.from_x[rows, :].astype(F32)

    @staticmethod
    def scratch(rows, width):
        return [
            pltpu.VMEM((2, rows, width), BF16),
            pltpu.VMEM((2, rows, width), BF16),
            pltpu.VMEM((rows, width), BF16),
        ]


def sum_tensor_kernel(far, part, out, *scratch):
    net = Net(far, *scratch[-3:])
    rows_back = ReduceTensor(net, part, *scratch[:3])
    rows_back.load()
    net.greet([net.x, net.core])
    rows_back.start()
    rows_back.step()
    rows_back.end()

    @pl.loop(0, out.shape[0] // 16)
    def _(i):
        rows = pl.ds(pl.multiple_of(i * 16, 16), 16)
        out[rows, :] = rows_back.total(rows)

    net.finish()


def sum_tensor(part, groups, ident):
    _, m, width = part.shape
    return pl.pallas_call(
        functools.partial(sum_tensor_kernel, groups // 2),
        out_shape=jax.ShapeDtypeStruct((m, width), F32),
        in_specs=[ANY],
        out_specs=IN_VMEM,
        scratch_shapes=ReduceTensor.scratch(m, width) + semaphores(3, 2),
        compiler_params=params(ident, 16),
        cost_estimate=cost(16),
    )(part)


def gather_tensor_kernel(far, own, out, *scratch):
    net = Net(far, *scratch)
    give = GatherTensor(net, own, out)
    net.greet([net.x, net.core])
    give.start()
    give.step()
    give.end()
    net.finish()


def gather_tensor(own, groups, tensors, ident):
    m, width = own.shape
    return pl.pallas_call(
        functools.partial(gather_tensor_kernel, groups // 2),
        out_shape=jax.ShapeDtypeStruct((tensors, m, width), own.dtype),
        in_specs=[ANY],
        out_specs=ANY,
        scratch_shapes=semaphores(3, 1),
        compiler_params=params(ident, 16),
        cost_estimate=cost(16),
    )(own)


def finish_kernel(far, *refs):
    (gq, gkv, gout, small, blocks, dxn, dresid, normed, scale, gain) = refs[:10]
    (oq, okv, oout, osmall, oblocks, otokens) = refs[10:16]
    scratch = list(refs[16:])
    net = Net(far, *scratch[-3:])

    def take(n):
        got = scratch[:n]
        del scratch[:n]
        return got

    weights = [ReduceGroups(net, p, o, *take(3)) for p, o in ((gq, oq), (gkv, okv), (gout, oout))]
    cols = 2 * far * 4 // 8
    tall, wide = small.shape[0] // 8, small.shape[1] // cols

    def block(ref):
        def at(s):
            down = pl.ds(pl.multiple_of(s // cols * tall, 16), tall)
            return ref.at[down, pl.ds(pl.multiple_of(s % cols * wide, 128), wide)]

        return at

    sums = ReduceAll(net, block(small), *take(5), "xy")
    rows_back = ReduceTensor(net, dxn, *take(3))
    sum_own, tokens_own = take(2)
    every = GatherAll(net, sum_own, block(osmall), "yx")
    give_tokens = GatherTensor(net, tokens_own, otokens)
    for part in (rows_back, sums, *weights):
        part.load()
    me = net.group()
    mine = [net.load(blocks.at[me], oblocks.at[me])]
    net.greet(net.line() + [net.x, net.core])
    for part in (rows_back, sums, *weights):
        part.start()
    rows_back.step()
    for i in range(far):
        sums.stage_a(i)
    for i in range(far):
        sums.stage_b(i)
    for i in range(far):
        weights[0].step(i)
    rows_back.end()

    @pl.loop(0, tokens_own.shape[0] // 16)
    def _(i):
        rows = pl.ds(pl.multiple_of(i * 16, 16), 16)
        n = normed[rows, :]
        weighted = rows_back.total(rows) * gain[...]
        mean = jnp.mean(weighted * n, axis=-1, keepdims=True)
        back = scale[rows, :] * (weighted - n * mean)
        tokens_own[rows, :] = (dresid[rows, :] + back).astype(BF16)

    give_tokens.start()
    for i in range(far):
        sums.stage_c(i)
    small_tokens = []
    for r in range(far):
        for b in range(2):
            if r or b:
                to = net.at(r, b)
                k = net.push(blocks.at[to[0]], oblocks.at[me], to)
                small_tokens.append((net.group(-r, b), k))
    sums.end()

    @pl.loop(0, sum_own.shape[0] // 16)
    def _(i):
        rows = pl.ds(pl.multiple_of(i * 16, 16), 16)
        sum_own[rows, :] = sums.total(rows).astype(BF16)

    mine.append(net.load(sum_own, block(osmall)(net.slot())))
    every.start()
    for part in weights[1:]:
        for i in range(far):
            part.step(i)
    give_tokens.step()
    pipelined(far, [every])
    for part in (*weights, give_tokens, every):
        part.end()
    for g, k in small_tokens:
        net.arrived(oblocks.at[g], k)
    net.finish()
    for copy in mine:
        copy.wait()


def finish(weights, small, blocks, dxn, dresid, normed, scale, gain, groups, tensors, ident):
    far = groups // 2
    m, width = dresid.shape
    outs = [jax.ShapeDtypeStruct(w.shape[1:], F32) for w in weights]
    outs.append(jax.ShapeDtypeStruct(small.shape, BF16))
    outs.append(jax.ShapeDtypeStruct(blocks.shape, BF16))
    outs.append(jax.ShapeDtypeStruct((tensors, m, width), BF16))
    scratch = []
    for w in weights:
        scratch += ReduceGroups.scratch(far, *w.shape[1:])
    cell = (small.shape[0] // 8, small.shape[1] // (groups * tensors // 8))
    scratch += ReduceAll.scratch(far, *cell)
    scratch += ReduceTensor.scratch(m, width)
    scratch += [pltpu.VMEM(cell, BF16), pltpu.VMEM((m, width), BF16)]
    return pl.pallas_call(
        functools.partial(finish_kernel, far),
        out_shape=outs,
        in_specs=[ANY] * 6 + [IN_VMEM] * 4,
        out_specs=[IN_VMEM] * 3 + [ANY] * 3,
        scratch_shapes=scratch + semaphores(40 * far, 10 * far + 10),
        compiler_params=params(ident),
        cost_estimate=cost(150),
    )(*weights, small, blocks, dxn, dresid, normed, scale, gain)


TILE = 32


def dot_nt(left, right):
    return lax.dot_general(left, right, (((1,), (1,)), ((), ())), preferred_element_type=F32)


def dot_nn(left, right):
    return lax.dot_general(left, right, (((1,), (0,)), ((), ())), preferred_element_type=F32)


def experts_kernel(sizes, *refs):
    far, experts, hidden, shared, total = sizes
    groups = 2 * far
    (x_own, dy_all, picks, wg_hbm, wu_hbm, wd_hbm, ws_hbm, wr_hbm) = refs[:8]
    (outs_hbm, dg_out, gg_hbm, gu_hbm, gd_hbm, gs_hbm, x_all, ffn_all) = refs[8:16]
    (core_in, x0_in, y1_in, y0_in, x1_in, z_in) = refs[16:22]
    (w_in, w_down, h, dh, hs, dgu, hsn, dgun, acc_in, acc_down, x, dy) = refs[22:34]
    (part, ffn_part, acc, own, stage1, stage2, stage3, stage4, dg, dg_in, dg_sum) = refs[34:45]
    (
        ag_s, ag_r, core_s, core_r, x0_s, x0_r, y1_s, y1_r, y0_s, y0_r, x1_s, x1_r, z_s, z_r,
        dg_s, dg_r, wsem, lsem, csem,
    ) = refs[45:]
    routed = experts * hidden
    units = routed + shared
    m, width = x_own.shape
    block, half = 4 * m, m // 2
    chunk = min(256, block)
    per = chunk // m
    low, high = pl.ds(0, half), pl.ds(half, half)
    net = Net(far, None, None, None)
    both, sums = range(2), range(1)

    def remote(src, dst, send, recv, to):
        return pltpu.make_async_remote_copy(
            src_ref=src, dst_ref=dst, send_sem=send, recv_sem=recv, device_id=to, device_id_type=MESH
        )

    def wait_for(ref, sem):
        pltpu.make_async_copy(ref, ref, sem).wait()

    links = ((net.y, net.x), (net.x, net.y))

    def place(p, r, u, v, d=0):
        b, c = (u, v) if p == 0 else (v, u)
        return x_all.at[net.slot(-r, b, c, d), (low, high)[p]]

    def pass_on(p, kind, r, u, v, to):
        ref = place(p, r, u, v)
        remote(ref, ref, ag_s.at[p, kind, r], ag_r.at[p, kind, r], to).start()

    def rows_a(r):
        for p in both:
            pl.when(r > 0)(lambda: wait_for(place(p, r, 0, 0), ag_r.at[p, 0, r]))
            pass_on(p, 1, r, 0, 0, links[p][0])
            pass_on(p, 2, r, 0, 0, links[p][1])
            pass_on(p, 4, r, 0, 0, net.core)

    def rows_b(r):
        for p in both:
            wait_for(place(p, r, 1, 0), ag_r.at[p, 1, r])
            pass_on(p, 3, r, 1, 0, links[p][1])
            pass_on(p, 6, r, 1, 0, net.core)

    def rows_c(r):
        for p in both:
            for u in both:
                wait_for(place(p, r, u, 1), ag_r.at[p, 2 + u, r])
                pass_on(p, 5 + 2 * u, r, u, 1, net.core)

    def rows_d(r):
        for p in both:
            for u in both:
                for v in both:
                    wait_for(place(p, r, u, v, 1), ag_r.at[p, 4 + 2 * u + v, r])

    def load_block(s):
        g = net.group(-(s // 2), 1 - s % 2)
        copies = [
            pltpu.make_async_copy(x_all.at[g * 4 + t], x.at[pl.ds(t * m, m)], lsem.at[t])
            for t in range(4)
        ]
        rows = pl.ds(pl.multiple_of(g * block, block), block)
        return copies + [pltpu.make_async_copy(dy_all.at[rows], dy, lsem.at[4])]

    def mine(c, d):
        t = net.at(0, 0, c, d)[1]
        return pl.ds(pl.multiple_of(t * m, m), m)

    def ffn_copy(s):
        g = net.group(-(s // 2), 1 - s % 2)
        rows = pl.ds(pl.multiple_of(g * block, block), block)
        return pltpu.make_async_copy(ffn_part, ffn_all.at[rows], lsem.at[5])

    def core_push(s, a, c):
        return remote(
            part.at[a, mine(c, 1)], core_in.at[a, s, c], core_s.at[a, s, c], core_r.at[a, s, c], net.core
        )

    def x0_push(s, a):
        return remote(acc.at[a, s % 3, 1, low], x0_in.at[a, s], x0_s.at[a, s], x0_r.at[a, s], net.x)

    def y1_push(s, a, c):
        r = s // 2
        return remote(
            acc.at[a, s % 3, c, high], y1_in.at[a, r, c], y1_s.at[a, r, c], y1_r.at[a, r, c], net.y
        )

    def y0_push(s, a):
        r = s // 2
        return remote(acc.at[a, s % 3, 0, low], y0_in.at[a, r], y0_s.at[a, r], y0_r.at[a, r], net.y)

    def x1_push(s, a):
        r = s // 2
        return remote(acc.at[a, s % 3, 1, high], x1_in.at[a, r], x1_s.at[a, r], x1_r.at[a, r], net.x)

    def z_push(s, a):
        r = s // 2
        return remote(acc.at[a, s % 3, 0], z_in.at[a, r], z_s.at[a, r], z_r.at[a, r], net.at(-r))

    def copy_in(ref, buf, sem, k):
        return pltpu.make_async_copy(ref, buf, sem.at[k])

    def h1_loads(s):
        return [copy_in(core_in.at[a, s], stage1.at[a], csem, a) for a in sums]

    def h2_loads(s):
        return [copy_in(x0_in.at[a, s], stage2.at[a], csem, 2 + a) for a in sums]

    def h2_more(s):
        return [copy_in(y1_in.at[a, s // 2], stage3.at[a], csem, 4 + a) for a in sums]

    def h3_loads(s):
        return [copy_in(y0_in.at[a, s // 2], stage4.at[a, 0], csem, 6 + a) for a in sums] + [
            copy_in(x1_in.at[a, s // 2], stage4.at[a, 1], csem, 8 + a) for a in sums
        ]

    def begin_all(copies):
        for c in copies:
            c.start()

    def wait_all(copies):
        for c in copies:
            c.wait()

    def sends_done(s):
        for a in sums:
            x0_push(s, a).wait_send()

        @pl.when(s % 2 == 0)
        def _():
            for a in sums:
                for c in both:
                    y1_push(s, a, c).wait_send()
                y0_push(s, a).wait_send()

        @pl.when(s % 2 == 1)
        def _():
            for a in sums:
                x1_push(s, a).wait_send()
            pl.when(s > 1)(lambda: [z_push(s, a).wait_send() for a in sums] and None)

    def h1_pre(s):
        for a in sums:
            for c in both:
                wait_for(core_in.at[a, s, c], core_r.at[a, s, c])
        begin_all(h1_loads(s))

    def h1_post(s):
        wait_all(h1_loads(s))
        pl.when(s > 2)(lambda: sends_done(s - 3))
        for a in sums:
            for c in (1, 0):
                base = mine(c, 0).start

                @pl.loop(0, m // 16)
                def _(i):
                    rows = pl.ds(pl.multiple_of(i * 16, 16), 16)
                    there = pl.ds(pl.multiple_of(base + i * 16, 16), 16)
                    acc[a, s % 3, c, rows, :] = part[a, there, :] + stage1[a, c, rows, :]

            x0_push(s, a).start()

        @pl.when(s % 2 == 0)
        def _():
            for a in sums:
                for c in both:
                    y1_push(s, a, c).start()

    def add(a, s, c, base, buf):
        @pl.loop(0, half // 16)
        def _(i):
            rows = pl.ds(pl.multiple_of(base + i * 16, 16), 16)
            there = pl.ds(pl.multiple_of(i * 16, 16), 16)
            acc[a, s % 3, c, rows, :] = acc[a, s % 3, c, rows, :] + buf[there, :]

    def h2_pre(s):
        for a in sums:
            wait_for(x0_in.at[a, s], x0_r.at[a, s])
        begin_all(h2_loads(s))

        @pl.when(s % 2 == 1)
        def _():
            for a in sums:
                for c in both:
                    wait_for(y1_in.at[a, s // 2, c], y1_r.at[a, s // 2, c])
            begin_all(h2_more(s))

    def h2_post(s):
        wait_all(h2_loads(s))
        for a in sums:
            add(a, s, 0, 0, stage2.at[a])

        @pl.when(s % 2 == 0)
        def _():
            for a in sums:
                y0_push(s, a).start()

        @pl.when(s % 2 == 1)
        def _():
            wait_all(h2_more(s))
            for a in sums:
                for c in (1, 0):
                    add(a, s, c, half, stage3.at[a, c])
                x1_push(s, a).start()

    def h3_pre(s):
        for a in sums:
            wait_for(y0_in.at[a, s // 2], y0_r.at[a, s // 2])
            wait_for(x1_in.at[a, s // 2], x1_r.at[a, s // 2])
        begin_all(h3_loads(s))

    def h3_post(s):
        wait_all(h3_loads(s))
        for a in sums:
            for k in both:
                add(a, s, 0, k * half, stage4.at[a, k])

        @pl.when(s > 1)
        def _():
            for a in sums:
                z_push(s, a).start()

        @pl.when(s == 1)
        def _():
            for a in sums:
                own[a] = acc[a, 1, 0]

    def weights():
        pairs = []
        for e in range(experts):
            at = pl.ds(e * hidden, hidden)
            pairs.append((wg_hbm.at[e], w_in.at[at]))
            pairs.append((wu_hbm.at[e], w_in.at[pl.ds(units + e * hidden, hidden)]))
            pairs.append((wd_hbm.at[e], w_down.at[at]))
        pairs.append((ws_hbm.at[0], w_in.at[pl.ds(routed, shared)]))
        pairs.append((ws_hbm.at[1], w_in.at[pl.ds(units + routed, shared)]))
        pairs.append((ws_hbm.at[2], w_down.at[pl.ds(routed, shared)]))
        pairs.append((wr_hbm, w_in.at[pl.ds(2 * units, total)]))
        return [pltpu.make_async_copy(a, b, wsem.at[i]) for i, (a, b) in enumerate(pairs)]

    first = pltpu.make_async_copy(x_own, x_all.at[net.slot()], lsem.at[0])
    first.start()
    net.greet(net.line() + [net.at(c=c, d=d) for c, d in ((0, 1), (1, 0), (1, 1))])
    first.wait()
    for r in range(1, far):
        for p in both:
            ref = place(p, 0, 0, 0)
            remote(ref, ref, ag_s.at[p, 0, r], ag_r.at[p, 0, r], net.at(r)).start()
    rows_a(0)
    begin_all(weights())
    acc_in[...] = jnp.zeros_like(acc_in)
    acc_down[...] = jnp.zeros_like(acc_down)
    dg[...] = jnp.zeros_like(dg)
    hs[units:, :] = jnp.zeros((hs.shape[0] - units, block), BF16)
    dgu[2 * units :, :] = jnp.zeros((dgu.shape[0] - 2 * units, block), BF16)
    rows_b(0)
    rows_c(0)
    rows_d(0)
    begin_all(load_block(0))
    wait_all(weights())

    @pl.loop(0, groups)
    def _(s):
        r = s // 2
        g = net.group(-r, 1 - s % 2)
        more = r + 1 < far
        pl.when((s % 2 == 0) & more)(lambda: rows_a(r + 1))
        pl.when((s % 2 == 1) & more)(lambda: rows_c(r + 1))
        pl.when(s > 0)(lambda: h1_pre(s - 1))
        pl.when(s > 1)(lambda: h2_pre(s - 2))
        wait_all(load_block(s))

        @pl.loop(0, block // chunk)
        def _(n):
            at = pl.ds(pl.multiple_of(n * chunk, chunk), chunk)
            h[...] = dot_nt(w_in[...], x[at, :])
            dh[...] = dot_nt(w_down[...], dy[at, :])
            logits = h[2 * units :, :]
            expo = jnp.exp(logits - jnp.max(logits, axis=0, keepdims=True))
            marked = picks[:, pl.ds(pl.multiple_of(g * block + n * chunk, chunk), chunk)]
            gates = expo / jnp.sum(expo, axis=0, keepdims=True) * marked
            for e in range(experts + 1):
                base, count = (e * hidden, hidden) if e < experts else (routed, shared)
                gate = gates[e : e + 1, :] if e < experts else jnp.ones((1, chunk), F32)

                def body(i, total_):
                    a = pl.multiple_of(base + i * TILE, TILE)
                    here = pl.ds(a, TILE)
                    there = pl.ds(pl.multiple_of(units + a, TILE), TILE)
                    hg, hu, d = h[here, :], h[there, :], dh[here, :]
                    sig = 1.0 / (1.0 + jnp.exp(-hg))
                    act = hg * sig
                    dact = sig + act * (1.0 - sig)
                    hid = act * hu
                    hs[here, at] = (hid * gate).astype(BF16)
                    ds = d * gate
                    dgu[here, at] = (ds * hu * dact).astype(BF16)
                    dgu[there, at] = (ds * act).astype(BF16)
                    return total_ + jnp.sum(hid * d, axis=0, keepdims=True)

                row = lax.fori_loop(0, count // TILE, body, jnp.zeros((1, chunk), F32))
                if e < experts:
                    for j in range(per):
                        dg[n * per + j, g, e : e + 1, :] = row[:, j * m : (j + 1) * m]

        pl.when(s > 0)(lambda: h1_post(s - 1))
        pl.when(s > 1)(lambda: h2_post(s - 2))
        pl.when((s > 2) & (s % 2 == 0))(lambda: h3_pre(s - 3))
        pl.when((s % 2 == 0) & more)(lambda: rows_b(r + 1))

        @pl.loop(0, width // 512)
        def _(c):
            at = pl.ds(pl.multiple_of(c * 512, 512), 512)
            acc_in[:, at] += dot_nn(dgu[: 2 * units, :], x[:, at])
            acc_down[:, at] += dot_nn(hs[:units, :], dy[:, at])

        pl.when((s > 2) & (s % 2 == 0))(lambda: h3_post(s - 3))
        pl.when((s % 2 == 1) & more)(lambda: rows_d(r + 1))
        pl.when(s + 1 < groups)(lambda: begin_all(load_block(s + 1)))
        hsn[...] = hs[...].T
        dgun[...] = dgu[...].T

        @pl.when(s > 0)
        def _():
            for c in both:
                core_push(s - 1, 0, c).wait_send()
            ffn_copy(s - 1).wait()

        @pl.loop(0, width // 512)
        def _(c):
            at = pl.ds(pl.multiple_of(c * 512, 512), 512)
            part[0, :, at] = dot_nn(dgun[:, : 2 * units], w_in[: 2 * units, at]).astype(BF16)

        for c in (1, 0):
            core_push(s, 0, c).start()

        @pl.loop(0, width // 512)
        def _(c):
            at = pl.ds(pl.multiple_of(c * 512, 512), 512)
            ffn_part[:, at] = dot_nn(hsn[:, :units], w_down[:, at]).astype(BF16)

        ffn_copy(s).start()

    def stores():
        pairs = []
        for e in range(experts):
            at = pl.ds(e * hidden, hidden)
            pairs.append((acc_in.at[at], gg_hbm.at[e]))
            pairs.append((acc_in.at[pl.ds(units + e * hidden, hidden)], gu_hbm.at[e]))
            pairs.append((acc_down.at[at], gd_hbm.at[e]))
        pairs.append((acc_in.at[pl.ds(routed, shared)], gs_hbm.at[0]))
        pairs.append((acc_in.at[pl.ds(units + routed, shared)], gs_hbm.at[1]))
        pairs.append((acc_down.at[pl.ds(routed, shared)], gs_hbm.at[2]))
        return [pltpu.make_async_copy(a, b, wsem.at[i]) for i, (a, b) in enumerate(pairs)]

    peers = [(c, d) for c in both for d in both][1:]

    def dg_push(k):
        c, d = peers[k]
        e, t = net.at(0, 0, c, d)
        return remote(dg.at[t], dg_in.at[k], dg_s.at[k], dg_r.at[k], (e, t))

    for k in range(3):
        dg_push(k).start()
    last = groups - 1
    h1_pre(last)
    h2_pre(last - 1)
    h1_post(last)
    begin_all(stores())
    h2_post(last - 1)
    h3_pre(last - 2)
    h3_post(last - 2)
    for k in range(3):
        wait_for(dg_in.at[k], dg_r.at[k])
    dg_sum[...] = dg[net.at()[1]] + dg_in[0] + dg_in[1] + dg_in[2]
    me = net.group()
    dg_out[me] = dg_sum[me]
    others = [(r, b) for r in range(far) for b in both][1:]

    def dg_give(k):
        to = net.at(*others[k])
        return remote(dg_sum.at[to[0]], dg_out.at[me], dg_s.at[3 + k], dg_r.at[3 + k], to)

    for k in range(len(others)):
        dg_give(k).start()
    h2_pre(last)
    h2_post(last)
    h3_pre(last)
    h3_post(last)
    for r in range(1, far):
        for a in sums:
            wait_for(z_in.at[a, r], z_r.at[a, r])
            got = pltpu.make_async_copy(z_in.at[a, r], stage1.at[a, 0], csem.at[a])
            got.start()
            got.wait()

            @pl.loop(0, m // 16)
            def _(i):
                rows = pl.ds(pl.multiple_of(i * 16, 16), 16)
                own[a, rows, :] = own[a, rows, :] + stage1[a, 0, rows, :]

    give = pltpu.make_async_copy(own, outs_hbm, csem.at[0])
    give.start()
    for k in range(len(others)):
        r, b = others[k]
        wait_for(dg_out.at[net.group(-r, b)], dg_r.at[3 + k])
    for s in range(last - 2, last + 1):
        sends_done(s)
    for c in both:
        core_push(last, 0, c).wait_send()
    ffn_copy(last).wait()
    for p in both:
        for r in range(far):
            for kind in range(8):
                if r or kind:
                    wait_for(place(p, 0, 0, 0), ag_s.at[p, kind, r])
    for k in range(3):
        dg_push(k).wait_send()
    for k in range(len(others)):
        dg_give(k).wait_send()
    wait_all(stores())
    give.wait()


def experts_all(x, dy, picks, wg, wu, wd, ws, wr, groups, tensors, ident):
    m, width = x.shape
    far = groups // 2
    experts, hidden, _ = wg.shape
    shared, total = ws.shape[1], wr.shape[0]
    units = experts * hidden + shared
    block, half = 4 * m, m // 2
    chunk = min(256, block)
    up = lambda v: -(-v // 128) * 128
    like = jax.ShapeDtypeStruct
    outs = [
        like((1, m, width), BF16),
        like((groups, 8, m), F32),
        like(wg.shape, F32),
        like(wu.shape, F32),
        like(wd.shape, F32),
        like(ws.shape, F32),
        like((groups * tensors, m, width), BF16),
        like((groups * block, width), BF16),
        like((1, groups, 2, m, width), BF16),
        like((1, groups, half, width), BF16),
        like((1, far, 2, half, width), BF16),
        like((1, far, half, width), BF16),
        like((1, far, half, width), BF16),
        like((1, far, m, width), BF16),
    ]
    dma = pltpu.SemaphoreType.DMA
    scratch = [
        pltpu.VMEM((2 * units + total, width), BF16),
        pltpu.VMEM((units, width), BF16),
        pltpu.VMEM((2 * units + total, chunk), F32),
        pltpu.VMEM((units, chunk), F32),
        pltpu.VMEM((up(units), block), BF16),
        pltpu.VMEM((up(2 * units), block), BF16),
        pltpu.VMEM((block, up(units)), BF16),
        pltpu.VMEM((block, up(2 * units)), BF16),
        pltpu.VMEM((2 * units, width), F32),
        pltpu.VMEM((units, width), F32),
        pltpu.VMEM((block, width), BF16),
        pltpu.VMEM((block, width), BF16),
        pltpu.VMEM((1, block, width), BF16),
        pltpu.VMEM((block, width), BF16),
        pltpu.VMEM((1, 3, 2, m, width), BF16),
        pltpu.VMEM((1, m, width), BF16),
        pltpu.VMEM((1, 2, m, width), BF16),
        pltpu.VMEM((1, half, width), BF16),
        pltpu.VMEM((1, 2, half, width), BF16),
        pltpu.VMEM((1, 2, half, width), BF16),
        pltpu.VMEM((tensors, groups, 8, m), F32),
        pltpu.VMEM((3, groups, 8, m), F32),
        pltpu.VMEM((groups, 8, m), F32),
    ]
    for shape in (
        (2, 8, far), (1, groups, 2), (1, groups), (1, far, 2), (1, far), (1, far), (1, far), (groups + 2,),
    ):
        scratch += [dma(shape), dma(shape)]
    scratch += [dma((3 * experts + 4,)), dma((6,)), dma((10,))]
    got = pl.pallas_call(
        functools.partial(experts_kernel, (far, experts, hidden, shared, total)),
        out_shape=outs,
        in_specs=[ANY, ANY, IN_VMEM] + [ANY] * 5,
        out_specs=[ANY, IN_VMEM] + [ANY] * 12,
        scratch_shapes=scratch,
        compiler_params=params(ident, 63),
        cost_estimate=cost(280),
    )(x, dy, picks, wg, wu, wd, ws, wr)
    return [*got[:6], got[7]]


BOTH = ("expert", "tensor")


def shards(
    tokens,
    lengths,
    routes,
    gain_attn,
    w_query,
    w_latent,
    gain_latent,
    w_kv,
    w_out,
    gain_ffn,
    w_router,
    w_shared_gate,
    w_shared_up,
    w_shared_down,
    w_gate,
    w_up,
    w_down,
    cotangent,
):
    groups = lax.axis_size("expert")
    tensors = lax.axis_size("tensor")
    eindex = lax.axis_index("expert")
    tindex = lax.axis_index("tensor")
    rows, width = tokens.shape
    quarter = rows // tensors
    experts_local, _, hidden_units = w_gate.shape
    total_experts = experts_local * groups
    every = groups * rows
    bf16, f32 = jnp.bfloat16, jnp.float32

    def own(v):
        return lax.dynamic_slice_in_dim(v, tindex * quarter, quarter, 0)

    live_int = (jnp.arange(rows) < lengths[0]).astype(jnp.int32)
    live = live_int.astype(f32)[:, None]
    live_own = own(live)
    cot_own = own(cotangent).astype(f32)
    dffn_own = (cot_own * live_own).astype(bf16)

    part = w_shared_down.shape[0] // groups
    spare = -part % TILE

    def shared_units(v):
        v = jnp.pad(v.reshape(groups, part, v.shape[1]), ((0, 0), (0, spare), (0, 0)))
        return v

    shared_w = jnp.stack(
        [shared_units(v) for v in (w_shared_gate.T, w_shared_up.T, w_shared_down)], axis=1
    )
    choose = jnp.any(routes[..., None] == jnp.arange(total_experts), axis=1).astype(F32)
    picks = choose * live
    query_w, kv_up, out_proj, shared_w, marks = begin(
        (w_query, w_kv, w_out),
        shared_w.reshape(groups, -1, shared_w.shape[-1]),
        picks.T.astype(BF16),
        groups,
        0,
    )
    query_w = query_w.reshape(width, -1)
    kv_up = kv_up.reshape(KVR, -1)
    out_proj = out_proj.transpose(1, 0, 2).reshape(-1, width)
    shared_w = shared_w.transpose(1, 0, 2).reshape(3, part + spare, width)
    gate_t, up_t = w_gate.transpose(0, 2, 1), w_up.transpose(0, 2, 1)
    router_t = jnp.roll(w_router.T, -eindex * experts_local, axis=0)
    parts = max(1, every // 4096)
    some = quarter // parts

    def split(v):
        return v.reshape(parts, some, v.shape[1])

    marks = marks.reshape(groups, total_experts, tensors, parts, some).transpose(3, 1, 0, 2, 4)
    picks_all = marks.reshape(parts, total_experts, -1).astype(F32)
    picks_all = jnp.roll(picks_all, -eindex * experts_local, axis=1)
    dffn = [lax.all_gather(v, BOTH, axis=0, tiled=True) for v in split(dffn_own)]

    heads = out_proj.shape[0] // VD
    xf = tokens.astype(f32)
    scale_one = inv_rms(xf)
    normed_one = xf * scale_one
    xn1 = (normed_one * gain_attn).astype(bf16)
    cosine, sine = rope_tables(rows, ROPE)
    qfull = mat(xn1, query_w).reshape(rows, heads, NOPE + ROPE)
    qcat = jnp.concatenate(
        [qfull[..., :NOPE], rotate(qfull[..., NOPE:], cosine[:, None, :], sine[:, None, :])],
        axis=-1,
    ).astype(bf16)
    latent = mat(xn1, w_latent)
    comp = latent[:, :KVR]
    scale_lat = inv_rms(comp)
    normed_lat = comp * scale_lat
    compressed = (normed_lat * gain_latent).astype(bf16)
    key_rope = rotate(latent[:, KVR:], cosine, sine).astype(bf16)
    key_value = mat(compressed, kv_up).astype(bf16).reshape(rows, heads, NOPE + VD)
    keys = jnp.concatenate(
        [key_value[..., :NOPE], jnp.broadcast_to(key_rope[:, None, :], (rows, heads, ROPE))],
        axis=-1,
    )
    values = key_value[..., NOPE:]
    causal = jnp.arange(rows)[:, None] >= jnp.arange(rows)[None, :]
    score_scale = (NOPE + ROPE) ** (-0.5)
    raw = jnp.einsum("qhd,khd->hqk", qcat, keys, preferred_element_type=f32) * score_scale
    score_now = jnp.where(causal[None], raw, -jnp.inf)
    peak = jnp.max(score_now, axis=-1, keepdims=True)
    expo = jnp.exp(score_now - peak)
    pfull = expo / jnp.sum(expo, axis=-1, keepdims=True)
    probs = pfull.astype(bf16)
    attended = (
        jnp.einsum("hqk,khd->qhd", probs, values, preferred_element_type=f32)
        .astype(bf16)
        .reshape(rows, heads * VD)
    )
    partial = mat(attended, out_proj).astype(bf16).reshape(tensors, quarter, width)
    partial, dffn = lax.optimization_barrier((partial, dffn))
    attn = sum_tensor(partial, groups, parts + 2)
    resid = own(xf) + live_own * attn
    scale_two = inv_rms(resid)
    normed_two = resid * scale_two
    xn2_own = (normed_two * gain_ffn).astype(bf16)
    router = jax.nn.softmax(mat(xn2_own, w_router), axis=-1)
    outs = []
    for k in range(parts):
        dx, dgates, *grads, ffn = experts_all(
            split(xn2_own)[k],
            dffn[k],
            picks_all[k],
            gate_t,
            up_t,
            w_down,
            shared_w,
            router_t,
            groups,
            tensors,
            k + 1,
        )
        dx = dx[0].astype(F32)
        ffn = lax.psum_scatter(ffn, BOTH, scatter_dimension=0, tiled=True).astype(F32)
        dgates = dgates[:, :experts_local].reshape(total_experts, some).T
        outs.append((ffn, dx, dgates, *grads))
    ffn, dx, dgates = (jnp.concatenate(v, axis=0) for v in list(zip(*outs))[:3])
    grads = [functools.reduce(jnp.add, v) for v in list(zip(*outs))[3:]]
    drouter = own(picks) * dgates
    grad_gate, grad_up = (v.transpose(0, 2, 1) for v in grads[:2])
    grad_down = grads[2]
    shared_g = grads[3].reshape(3, part + spare, groups, width // groups).astype(BF16)
    shared_g = shared_g.transpose(2, 0, 1, 3).reshape(groups, -1, width // groups)
    dlogit = router * (drouter - jnp.sum(router * drouter, axis=-1, keepdims=True))
    grad_router = mat_tn(dlogit.astype(bf16), xn2_own)
    dnorm_two = dx + mat_nt(dlogit.astype(bf16), w_router)
    grad_gain_ffn = jnp.sum(dnorm_two * normed_two, axis=0)
    dresid = cot_own + norm_back(dnorm_two, normed_two, scale_two, gain_ffn)
    dattn = gather_tensor((dresid * live_own).astype(bf16), groups, tensors, parts + 3).reshape(rows, width)
    grad_out = mat_tn(attended, dattn)
    dattended = mat_nt(dattn, out_proj).astype(bf16).reshape(rows, heads, VD)
    dvalues = jnp.einsum("hqk,qhd->khd", probs, dattended, preferred_element_type=f32)
    dprobs = jnp.einsum("qhd,khd->hqk", dattended, values, preferred_element_type=f32)
    dscore = (
        pfull * (dprobs - jnp.sum(pfull * dprobs, axis=-1, keepdims=True)) * score_scale
    ).astype(bf16)
    dquery = jnp.einsum("hqk,khd->qhd", dscore, keys, preferred_element_type=f32)
    dkeys = jnp.einsum("hqk,qhd->khd", dscore, qcat, preferred_element_type=f32)
    dkv = (
        jnp.concatenate([dkeys[..., :NOPE], dvalues], axis=-1)
        .astype(bf16)
        .reshape(rows, heads * (NOPE + VD))
    )
    grad_kv = mat_tn(compressed, dkv)
    dcomp = mat_nt(dkv, kv_up)
    grad_gain_latent = jnp.sum(dcomp * normed_lat, axis=0)
    dlatent = jnp.concatenate(
        [
            norm_back(dcomp, normed_lat, scale_lat, gain_latent),
            rotate_back(jnp.sum(dkeys[..., NOPE:], axis=1), cosine, sine),
        ],
        axis=-1,
    ).astype(bf16)
    dqfull = jnp.concatenate(
        [dquery[..., :NOPE], rotate_back(dquery[..., NOPE:], cosine[:, None, :], sine[:, None, :])],
        axis=-1,
    )
    dqfull = dqfull.astype(bf16).reshape(rows, heads * (NOPE + ROPE))
    grad_query = mat_tn(xn1, dqfull)
    grad_latent = mat_tn(dlatent, xn1)
    dnorm_one = mat_nt(dqfull, query_w) + mat_nt(dlatent, w_latent)
    grad_gain_attn = jnp.sum(dnorm_one * normed_one, axis=0)
    small = jnp.concatenate(
        [
            grad_latent,
            grad_router,
            grad_gain_attn[None],
            grad_gain_ffn[None],
            jnp.pad(grad_gain_latent, (0, width - KVR))[None],
        ],
        axis=0,
    ).astype(bf16)
    small = jnp.pad(small, ((0, -small.shape[0] % 128), (0, 0)))
    grad_out = grad_out.astype(bf16).reshape(-1, groups, width // groups).transpose(1, 0, 2)
    grad_query, grad_kv, grad_out, small, shared_g, grad_tokens = finish(
        (
            grad_query.astype(bf16).reshape(groups, -1, grad_query.shape[1]),
            grad_kv.astype(bf16).reshape(groups, -1, grad_kv.shape[1]),
            grad_out,
        ),
        small,
        shared_g,
        dnorm_one.astype(bf16).reshape(tensors, quarter, width),
        dresid,
        own(normed_one),
        own(scale_one),
        gain_attn[None],
        groups,
        tensors,
        parts + 1,
    )
    grad_tokens = grad_tokens.reshape(rows, width)
    grad_tokens, ffn, resid_late = lax.optimization_barrier((grad_tokens, ffn, resid))
    output_own = (resid_late + live_own * ffn).astype(bf16)
    output = lax.all_gather(output_own, "tensor", axis=0, tiled=True)
    at = w_latent.shape[1]
    small = small.astype(f32)
    grad_latent = small[:at].T
    grad_router = small[at : at + total_experts].T
    at = at + total_experts
    grad_gain_attn = small[at]
    grad_gain_ffn = small[at + 1]
    grad_gain_latent = small[at + 2, :KVR]
    shared_g = shared_g.reshape(groups, 3, part + spare, -1)[:, :, :part].transpose(1, 0, 2, 3)
    shared_g = shared_g.reshape(3, groups * part, -1).astype(f32)
    grad_sgate, grad_sup, grad_sdown = shared_g[0].T, shared_g[1].T, shared_g[2]
    return (
        output,
        grad_tokens,
        grad_gain_attn,
        grad_query,
        grad_latent,
        grad_gain_latent,
        grad_kv,
        grad_out,
        grad_gain_ffn,
        grad_router,
        grad_sgate,
        grad_sup,
        grad_sdown,
        grad_gate,
        grad_up,
        grad_down,
    )


def solution(mesh):
    in_specs = (
        P("expert", None),
        P("expert"),
        P("expert", None),
        P(),
        P("expert", "tensor"),
        P(),
        P(),
        P("expert", "tensor"),
        P("tensor", "expert"),
        P(),
        P(),
        P("expert", "tensor"),
        P("expert", "tensor"),
        P("tensor", "expert"),
        P("expert", None, "tensor"),
        P("expert", None, "tensor"),
        P("expert", "tensor", None),
        P("expert", None),
    )
    out_specs = (
        P("expert", None),
        P("expert", None),
        P(),
        P("expert", "tensor"),
        P(),
        P(),
        P("expert", "tensor"),
        P("tensor", "expert"),
        P(),
        P(),
        P("expert", "tensor"),
        P("expert", "tensor"),
        P("tensor", "expert"),
        P("expert", None, "tensor"),
        P("expert", None, "tensor"),
        P("expert", "tensor", None),
    )
    return jax.shard_map(shards, mesh=mesh, in_specs=in_specs, out_specs=out_specs, check_vma=False)
```

```python
import functools

import jax
import jax.numpy as jnp
from jax import lax
from jax.experimental import pallas as pl
from jax.experimental.pallas import tpu as pltpu
from jax.sharding import PartitionSpec as P

F32, BF16 = jnp.float32, jnp.bfloat16

NOPE = 128
ROPE = 64
VD = 128
KVR = 512


EPS = 1e-06
ROPE_BASE = 10000.0


def inv_rms(v):
    return lax.rsqrt(jnp.mean(v * v, axis=-1, keepdims=True) + EPS)


def rope_tables(count, width):
    half = width // 2
    freq = ROPE_BASE ** (-(jnp.arange(half, dtype=jnp.float32) * 2.0 / width))
    angle = jnp.arange(count, dtype=jnp.float32)[:, None] * freq[None, :]
    return (jnp.cos(angle), jnp.sin(angle))


def rotate(v, cosine, sine):
    half = v.shape[-1] // 2
    first = v[..., :half]
    second = v[..., half:]
    return jnp.concatenate(
        [first * cosine - second * sine, second * cosine + first * sine], axis=-1
    )


def rotate_back(grad, cosine, sine):
    half = grad.shape[-1] // 2
    first = grad[..., :half]
    second = grad[..., half:]
    return jnp.concatenate(
        [first * cosine + second * sine, second * cosine - first * sine], axis=-1
    )


def norm_back(grad, normed, scale_row, gain):
    weighted = grad * gain
    return scale_row * (weighted - normed * jnp.mean(weighted * normed, axis=-1, keepdims=True))


def silu_parts(gate):
    sig = jax.nn.sigmoid(gate)
    return (gate * sig, sig * (1.0 + gate * (1.0 - sig)))


def mat(left, right):
    return jnp.dot(left, right, preferred_element_type=jnp.float32)


def mat_tn(left, right):
    return lax.dot_general(
        left, right, (((0,), (0,)), ((), ())), preferred_element_type=jnp.float32
    )


def mat_nt(left, right):
    return lax.dot_general(
        left, right, (((1,), (1,)), ((), ())), preferred_element_type=jnp.float32
    )


MESH = pl.DeviceIdType.MESH
ANY = pl.BlockSpec(memory_space=pl.ANY)
IN_VMEM = pl.BlockSpec(memory_space=pltpu.VMEM)


def places():
    e, t = lax.axis_index("expert"), lax.axis_index("tensor")
    return e // 2, e % 2, t // 2, t % 2


class Net:
    def __init__(self, far, send, recv, local):
        self.far, self.send, self.recv, self.local = far, send, recv, local
        self.e1, self.e0, self.t1, self.t0 = places()
        self.count, self.started, self.locals = 0, [], 0
        self.core = self.at(d=1)
        self.x = self.at(c=1)
        self.y = self.at(b=1)

    def at(self, r=0, b=0, c=0, d=0):
        e = (self.e1 + r + self.far) % self.far * 2 + (self.e0 + b) % 2
        return (e, (self.t1 + c) % 2 * 2 + (self.t0 + d) % 2)

    def slot(self, r=0, b=0, c=0, d=0):
        e, t = self.at(r, b, c, d)
        return e * 4 + t

    def group(self, r=0, b=0):
        return self.at(r, b)[0]

    def greet(self, peers):
        barrier = pltpu.get_barrier_semaphore()
        for peer in peers:
            pl.semaphore_signal(barrier, inc=1, device_id=peer, device_id_type=MESH)
        pl.semaphore_wait(barrier, len(peers))

    def near(self):
        return [self.at(r) for r in range(1, self.far)] + [self.y, self.x, self.core]

    def line(self):
        every = [self.at(r, b) for r in range(self.far) for b in range(2)]
        return every[1:]

    def push(self, src, dst, to):
        k = self.count
        self.count += 1
        copy = pltpu.make_async_remote_copy(
            src_ref=src,
            dst_ref=dst,
            send_sem=self.send.at[k],
            recv_sem=self.recv.at[k],
            device_id=to,
            device_id_type=MESH,
        )
        copy.start()
        self.started.append(copy)
        return k

    def arrived(self, ref, k):
        pltpu.make_async_copy(ref, ref, self.recv.at[k]).wait()

    def load(self, src, dst):
        copy = pltpu.make_async_copy(src, dst, self.local.at[self.locals])
        self.locals += 1
        copy.start()
        return copy

    def finish(self):
        for copy in self.started:
            copy.wait_send()


def add_rows(dst, src, step=16):
    @pl.loop(0, dst.shape[0] // step)
    def _(i):
        rows = pl.ds(pl.multiple_of(i * step, step), step)
        dst[rows, :] = dst[rows, :] + src[rows, :]


class GatherAll:
    def __init__(self, net, own, out_at, order):
        self.net, self.own, self.out_at, self.order = net, own, out_at, order
        self.z, self.first, self.second, self.cores = {}, {}, {}, {}

    def place(self, r, u, v, d=0):
        b, c = (u, v) if self.order == "yx" else (v, u)
        return self.out_at(self.net.slot(-r, b, c, d))

    def pass_on(self, r, u, v, to):
        here = self.own if (r, u, v) == (0, 0, 0) else self.place(r, u, v)
        return self.net.push(here, self.place(r, u, v), to)

    def start(self):
        for r in range(1, self.net.far):
            self.z[r] = self.pass_on(0, 0, 0, self.net.at(r))
        self.links = (self.net.y, self.net.x)[:: 1 if self.order == "yx" else -1]

    def stage_a(self, r):
        if r:
            self.net.arrived(self.place(r, 0, 0), self.z[r])
        self.first[r] = self.pass_on(r, 0, 0, self.links[0])
        self.second[r, 0] = self.pass_on(r, 0, 0, self.links[1])
        self.cores[r, 0, 0] = self.pass_on(r, 0, 0, self.net.core)

    def stage_b(self, r):
        self.net.arrived(self.place(r, 1, 0), self.first[r])
        self.second[r, 1] = self.pass_on(r, 1, 0, self.links[1])
        self.cores[r, 1, 0] = self.pass_on(r, 1, 0, self.net.core)

    def stage_c(self, r):
        for u in range(2):
            self.net.arrived(self.place(r, u, 1), self.second[r, u])
            self.cores[r, u, 1] = self.pass_on(r, u, 1, self.net.core)

    def steps(self):
        return [self.stage_a, self.stage_b, self.stage_c]

    def end(self):
        for (r, u, v), k in self.cores.items():
            self.net.arrived(self.place(r, u, v, 1), k)


class ReduceAll:
    def __init__(self, net, part_at, acc, from_core, from_first, from_second, from_z, order):
        self.net, self.part_at, self.acc, self.order = net, part_at, acc, order
        self.bufs = (from_core, from_first, from_second, from_z)
        self.core, self.first, self.second, self.z, self.loads = {}, {}, {}, {}, {}
        self.turn = list(range(net.far - 1, -1, -1))
        self.spots = ((1, 1), (0, 1), (1, 0), (0, 0))
        self.links = (net.x, net.y) if order == "xy" else (net.y, net.x)

    def dest(self, r, u, v, d):
        b, c = (v, u) if self.order == "xy" else (u, v)
        return self.part_at(self.net.slot(r, b, c, d))

    def load(self):
        for r in self.turn:
            for u, v in self.spots:
                k = r * 4 + u * 2 + v
                self.loads[k] = self.net.load(self.dest(r, u, v, 0), self.acc.at[k])

    def start(self):
        for r in self.turn:
            for u, v in self.spots:
                k = r * 4 + u * 2 + v
                self.core[k] = self.net.push(
                    self.dest(r, u, v, 1), self.bufs[0].at[k], self.net.core
                )

    def merge(self, k, buf, i, token):
        self.net.arrived(buf.at[i], token)
        add_rows(self.acc.at[k], buf.at[i])

    def stage_a(self, i):
        r = self.turn[i]
        for u, v in self.spots:
            k = r * 4 + u * 2 + v
            self.loads[k].wait()
            self.merge(k, self.bufs[0], k, self.core[k])
            if u:
                at = r * 2 + v
                self.first[at] = self.net.push(
                    self.acc.at[k], self.bufs[1].at[at], self.links[0]
                )

    def stage_b(self, i):
        r = self.turn[i]
        for v in (1, 0):
            at = r * 2 + v
            self.merge(r * 4 + v, self.bufs[1], at, self.first[at])
            if v:
                self.second[r] = self.net.push(
                    self.acc.at[r * 4 + v], self.bufs[2].at[r], self.links[1]
                )

    def stage_c(self, i):
        r = self.turn[i]
        self.merge(r * 4, self.bufs[2], r, self.second[r])
        if r:
            self.z[r] = self.net.push(
                self.acc.at[r * 4], self.bufs[3].at[r - 1], self.net.at(r)
            )

    def steps(self):
        return [self.stage_a, self.stage_b, self.stage_c]

    def end(self):
        for r in range(1, self.net.far):
            self.net.arrived(self.bufs[3].at[r - 1], self.z[r])

    def total(self, rows):
        total = self.acc[0, rows, :].astype(F32)
        for r in range(1, self.net.far):
            total = total + self.bufs[3][r - 1, rows, :].astype(F32)
        return total

    @staticmethod
    def scratch(far, rows, width):
        return [
            pltpu.VMEM((4 * far, rows, width), BF16),
            pltpu.VMEM((4 * far, rows, width), BF16),
            pltpu.VMEM((2 * far, rows, width), BF16),
            pltpu.VMEM((far, rows, width), BF16),
            pltpu.VMEM((far - 1, rows, width), BF16),
        ]


class Summed:
    def __init__(self, ref):
        self.ref = ref

    def load(self):
        pass

    start = end = load

    def stage_a(self, i):
        pass

    stage_b = stage_c = stage_a

    def total(self, rows):
        return self.ref[rows, :]


def pipelined(far, parts):
    for i in range(far + 2):
        for s in range(3):
            for part in parts:
                if 0 <= i - s < far:
                    part.steps()[s](i - s)


def semaphores(remote, local):
    return [
        pltpu.SemaphoreType.DMA((remote,)),
        pltpu.SemaphoreType.DMA((remote,)),
        pltpu.SemaphoreType.DMA((local,)),
    ]


def cost(us):
    return pl.CostEstimate(flops=0, bytes_accessed=us * 3_000_000, transcendentals=0)


def params(ident, mib=60):
    return pltpu.CompilerParams(
        collective_id=ident, has_side_effects=True, vmem_limit_bytes=mib * 2**20
    )


def begin_kernel(far, *refs):
    n = 3
    ws, blocks, marks, dy = refs[:n], refs[n], refs[n + 1], refs[n + 2]
    outs, blocks_out, marks_out, near = refs[n + 3 : 2 * n + 3], *refs[2 * n + 3 : 2 * n + 6]
    net = Net(far, *refs[2 * n + 6 :])
    me = net.group()
    mine = [net.load(w, o.at[me]) for w, o in zip(ws, outs)]
    mine.append(net.load(blocks.at[me], blocks_out.at[me]))
    mine.append(net.load(marks, marks_out.at[me]))
    net.greet(net.line() + [net.x, net.core])
    here = [near.at[net.at(0, 0, c, d)[1]] for c in range(2) for d in range(2)]
    dy_y = net.push(dy, here[0], net.y)
    tokens = {}
    others = [(r, b) for r in range(far) for b in range(2)][1:]
    for a, (w, o) in enumerate(zip(ws, outs)):
        for r in range(1, far):
            tokens[a, r] = net.push(w, o.at[me], net.at(r))
        tokens[a, 0, 1] = net.push(w, o.at[me], net.y)
    small = []
    for r, b in others:
        small.append((r, b, marks_out, net.push(marks, marks_out.at[me], net.at(r, b))))
    net.arrived(here[0], dy_y)
    dy_x = net.push(here[0], here[0], net.x)
    dy_core = net.push(here[0], here[0], net.core)
    for a, (w, o) in enumerate(zip(ws, outs)):
        for r in range(1, far):
            place = o.at[net.group(-r)]
            net.arrived(place, tokens[a, r])
            tokens[a, r, 1] = net.push(place, place, net.y)
    for r, b in others:
        to = net.at(r, b)
        small.append((r, b, blocks_out, net.push(blocks.at[to[0]], blocks_out.at[me], to)))
    net.arrived(here[2], dy_x)
    dy_both = net.push(here[2], here[2], net.core)
    for a, o in enumerate(outs):
        for r in range(far):
            net.arrived(o.at[net.group(-r, 1)], tokens[a, r, 1])
    net.arrived(here[1], dy_core)
    net.arrived(here[3], dy_both)
    for r, b, ref, k in small:
        net.arrived(ref.at[net.group(-r, b)], k)
    net.finish()
    for copy in mine:
        copy.wait()


def begin(ws, blocks, marks, dy, groups, tensors, ident):
    far = groups // 2
    outs = [jax.ShapeDtypeStruct((groups, *w.shape), w.dtype) for w in ws]
    outs.append(jax.ShapeDtypeStruct(blocks.shape, blocks.dtype))
    outs.append(jax.ShapeDtypeStruct((groups, *marks.shape), marks.dtype))
    outs.append(jax.ShapeDtypeStruct((tensors, *dy.shape), dy.dtype))
    return pl.pallas_call(
        functools.partial(begin_kernel, far),
        out_shape=outs,
        in_specs=[ANY] * 6,
        out_specs=[ANY] * 6,
        scratch_shapes=semaphores(10 * far, 5),
        compiler_params=params(ident),
        cost_estimate=cost(100),
    )(*ws, blocks, marks, dy)


class ReduceGroups:
    def __init__(self, net, part, out, acc, from_y, from_z):
        self.net, self.part, self.out = net, part, out
        self.acc, self.from_y, self.from_z = acc, from_y, from_z
        self.turn = list(range(net.far - 1, -1, -1))
        self.y, self.z = {}, {}

    def load(self):
        self.loads = {
            r: self.net.load(self.part.at[self.net.group(r)], self.acc.at[r]) for r in self.turn
        }

    def start(self, r):
        part = self.part.at[self.net.group(r, 1)]
        self.y[r] = self.net.push(part, self.from_y.at[r], self.net.y)

    def step(self, r):
        self.loads[r].wait()
        self.net.arrived(self.from_y.at[r], self.y[r])
        add_rows(self.acc.at[r], self.from_y.at[r])
        if r:
            self.z[r] = self.net.push(self.acc.at[r], self.from_z.at[r - 1], self.net.at(r))

    def end(self):
        for r in range(1, self.net.far):
            self.net.arrived(self.from_z.at[r - 1], self.z[r])

        @pl.loop(0, self.out.shape[0] // 16)
        def _(i):
            rows = pl.ds(pl.multiple_of(i * 16, 16), 16)
            total = self.acc[0, rows, :].astype(F32)
            for r in range(1, self.net.far):
                total = total + self.from_z[r - 1, rows, :].astype(F32)
            self.out[rows, :] = total

    @staticmethod
    def scratch(far, rows, width):
        return [
            pltpu.VMEM((far, rows, width), BF16),
            pltpu.VMEM((far, rows, width), BF16),
            pltpu.VMEM((far - 1, rows, width), BF16),
        ]


class GatherTensor:
    def __init__(self, net, own, out):
        self.net, self.own, self.out = net, own, out

    def place(self, c, d):
        return self.out.at[self.net.at(0, 0, c, d)[1]]

    def start(self):
        net = self.net
        self.mine = net.load(self.own, self.place(0, 0))
        self.x = net.push(self.own, self.place(0, 0), net.x)
        self.c0 = net.push(self.own, self.place(0, 0), net.core)

    def step(self):
        self.net.arrived(self.place(1, 0), self.x)
        self.c1 = self.net.push(self.place(1, 0), self.place(1, 0), self.net.core)

    def end(self):
        self.net.arrived(self.place(0, 1), self.c0)
        self.net.arrived(self.place(1, 1), self.c1)
        self.mine.wait()


class ReduceTensor:
    def __init__(self, net, part, acc, from_core, from_x):
        self.net, self.part = net, part
        self.acc, self.from_core, self.from_x = acc, from_core, from_x

    def at(self, c, d):
        return self.part.at[self.net.at(0, 0, c, d)[1]]

    def load(self):
        self.loads = [self.net.load(self.at(c, 0), self.acc.at[c]) for c in (1, 0)]

    def start(self):
        self.core = [
            self.net.push(self.at(c, 1), self.from_core.at[c], self.net.core) for c in (1, 0)
        ]

    def step(self):
        for i, c in enumerate((1, 0)):
            self.loads[i].wait()
            self.net.arrived(self.from_core.at[c], self.core[i])
            add_rows(self.acc.at[c], self.from_core.at[c])
            if c:
                self.x = self.net.push(self.acc.at[c], self.from_x, self.net.x)

    def end(self):
        self.net.arrived(self.from_x, self.x)

    def total(self, rows):
        return self.acc[0, rows, :].astype(F32) + self.from_x[rows, :].astype(F32)

    @staticmethod
    def scratch(rows, width):
        return [
            pltpu.VMEM((2, rows, width), BF16),
            pltpu.VMEM((2, rows, width), BF16),
            pltpu.VMEM((rows, width), BF16),
        ]


def sum_tensor_kernel(far, part, out, *scratch):
    net = Net(far, *scratch[-3:])
    rows_back = ReduceTensor(net, part, *scratch[:3])
    rows_back.load()
    net.greet([net.x, net.core])
    rows_back.start()
    rows_back.step()
    rows_back.end()

    @pl.loop(0, out.shape[0] // 16)
    def _(i):
        rows = pl.ds(pl.multiple_of(i * 16, 16), 16)
        out[rows, :] = rows_back.total(rows)

    net.finish()


def sum_tensor(part, groups, ident):
    _, m, width = part.shape
    return pl.pallas_call(
        functools.partial(sum_tensor_kernel, groups // 2),
        out_shape=jax.ShapeDtypeStruct((m, width), F32),
        in_specs=[ANY],
        out_specs=IN_VMEM,
        scratch_shapes=ReduceTensor.scratch(m, width) + semaphores(3, 2),
        compiler_params=params(ident, 16),
        cost_estimate=cost(16),
    )(part)


def gather_tensor_kernel(far, own, blocks, out, blocks_out, *scratch):
    net = Net(far, *scratch)
    give = GatherTensor(net, own, out)
    me = net.group()
    net.greet(net.line() + [net.x, net.core])
    give.start()
    mine = net.load(blocks.at[me], blocks_out.at[me])
    small = []
    for r in range(far):
        for b in range(2):
            if r or b:
                to = net.at(r, b)
                small.append((net.group(-r, b), net.push(blocks.at[to[0]], blocks_out.at[me], to)))
    give.step()
    give.end()
    for g, k in small:
        net.arrived(blocks_out.at[g], k)
    net.finish()
    mine.wait()


def gather_tensor(own, blocks, groups, tensors, ident):
    m, width = own.shape
    return pl.pallas_call(
        functools.partial(gather_tensor_kernel, groups // 2),
        out_shape=[
            jax.ShapeDtypeStruct((tensors, m, width), own.dtype),
            jax.ShapeDtypeStruct(blocks.shape, blocks.dtype),
        ],
        in_specs=[ANY] * 2,
        out_specs=[ANY] * 2,
        scratch_shapes=semaphores(2 + groups, 2),
        compiler_params=params(ident, 16),
        cost_estimate=cost(25),
    )(own, blocks)


def reduce_rows_kernel(far, part, out, *scratch):
    net = Net(far, *scratch[-3:])
    sums = ReduceAll(net, lambda s: part.at[s], *scratch[:5], "xy")
    sums.load()
    net.greet(net.near())
    sums.start()
    pipelined(far, [sums])
    sums.end()

    @pl.loop(0, out.shape[0] // 16)
    def _(i):
        rows = pl.ds(pl.multiple_of(i * 16, 16), 16)
        out[rows, :] = sums.total(rows)

    net.finish()


def reduce_rows(part, groups, ident):
    far = groups // 2
    return pl.pallas_call(
        functools.partial(reduce_rows_kernel, far),
        out_shape=jax.ShapeDtypeStruct(part.shape[1:], F32),
        in_specs=[ANY],
        out_specs=IN_VMEM,
        scratch_shapes=ReduceAll.scratch(far, *part.shape[1:]) + semaphores(12 * far, 4 * far),
        compiler_params=params(ident),
        cost_estimate=cost(90),
    )(part)


def cells(groups, tensors):
    across = 8 if groups * tensors <= 32 else 16
    return groups * tensors // across, across


def finish_kernel(far, *refs):
    (gq, gkv, gout, latent, misc, dxn, ffn, dresid, normed, scale, gain, resid, live) = refs[:13]
    (oq, okv, oout, osmall, otokens, ooutput) = refs[13:19]
    scratch = list(refs[19:])
    net = Net(far, *scratch[-3:])

    def take(n):
        got = scratch[:n]
        del scratch[:n]
        return got

    weights = [ReduceGroups(net, p, o, *take(3)) for p, o in ((gq, oq), (gkv, okv), (gout, oout))]
    down, across = cells(2 * far, 4)
    tall, wide = osmall.shape[0] // down, osmall.shape[1] // across
    tall_latent, tall_misc = latent.shape[0] // down, misc.shape[0] // down

    def cell(ref):
        def at(s):
            here = pl.ds(pl.multiple_of(s // across * tall, 16), tall)
            return ref.at[here, pl.ds(pl.multiple_of(s % across * wide, 128), wide)]

        return at

    summed = len(ffn.shape) == 2
    small, sum_own, tokens_own, output_own = scratch[-7:-3]
    sums = ReduceAll(net, cell(small), *take(5), "xy")
    rows_back = ReduceTensor(net, dxn, *take(3))
    ffns = Summed(ffn) if summed else ReduceAll(net, lambda s: ffn.at[s], *take(5), "xy")
    give_output = GatherTensor(net, output_own, ooutput)
    every = GatherAll(net, sum_own, cell(osmall), "yx")
    give_tokens = GatherTensor(net, tokens_own, otokens)
    moved = []
    for k in range(down):
        here = pl.ds(k * tall, tall_latent)
        moved.append(net.load(latent.at[pl.ds(k * tall_latent, tall_latent)], small.at[here]))
        here = pl.ds(k * tall + tall_latent, tall_misc)
        moved.append(net.load(misc.at[pl.ds(k * tall_misc, tall_misc)], small.at[here]))
    for part in (rows_back, *weights, ffns):
        part.load()
    mine = []
    net.greet(net.near())

    def send_weights(r):
        for part in weights:
            part.start(r)

    def step_weights(r):
        for part in weights:
            part.step(r)

    def each(count, body):
        @pl.loop(0, count // 16)
        def _(i):
            body(pl.ds(pl.multiple_of(i * 16, 16), 16))

    def tokens_rows(rows):
        n = normed[rows, :]
        weighted = rows_back.total(rows) * gain[...]
        mean = jnp.mean(weighted * n, axis=-1, keepdims=True)
        back = scale[rows, :] * (weighted - n * mean)
        tokens_own[rows, :] = (dresid[rows, :] + back).astype(BF16)

    def output_rows(rows):
        output_own[rows, :] = (resid[rows, :] + live[rows, :] * ffns.total(rows)).astype(BF16)

    def sum_rows(rows):
        sum_own[rows, :] = sums.total(rows).astype(BF16)

    turn = list(range(far - 1, -1, -1))
    rows_back.start()
    for copy in moved:
        copy.wait()
    sums.load()
    sums.start()
    ffns.start()
    send_weights(turn[0])
    rows_back.step()
    for i in range(far):
        sums.stage_a(i)
    ffns.stage_a(0)
    send_weights(turn[1])
    for i in range(far):
        sums.stage_b(i)
    rows_back.end()
    each(tokens_own.shape[0], tokens_rows)
    give_tokens.start()
    ffns.stage_a(1)
    for i in range(far):
        sums.stage_c(i)
    for k in range(far - 2):
        step_weights(turn[k])
        send_weights(turn[k + 2])
        ffns.stage_b(k)
        ffns.stage_a(k + 2)
    sums.end()
    each(sum_own.shape[0], sum_rows)
    mine.append(net.load(sum_own, cell(osmall)(net.slot())))
    every.start()
    every.stage_a(0)
    step_weights(turn[far - 2])
    for k in range(far - 2):
        ffns.stage_c(k)
    give_tokens.step()
    every.stage_b(0)
    every.stage_c(0)
    ffns.stage_b(far - 2)
    for r in range(1, far):
        every.stage_a(r)
    step_weights(turn[far - 1])
    for r in range(1, far):
        every.stage_b(r)
    ffns.stage_c(far - 2)
    ffns.stage_b(far - 1)
    for r in range(1, far):
        every.stage_c(r)
    ffns.stage_c(far - 1)
    ffns.end()
    each(output_own.shape[0], output_rows)
    give_output.start()
    for part in weights:
        part.end()
    give_output.step()
    for part in (give_tokens, every, give_output):
        part.end()
    net.finish()
    for copy in mine:
        copy.wait()


def finish(weights, latent, misc, dxn, ffn, rows, groups, tensors, ident):
    far = groups // 2
    m, width = rows[0].shape
    down, across = cells(groups, tensors)
    size = (latent.shape[0] + misc.shape[0], width)
    cell = (size[0] // down, width // across)
    outs = [jax.ShapeDtypeStruct(w.shape[1:], F32) for w in weights]
    outs.append(jax.ShapeDtypeStruct(size, BF16))
    outs += [jax.ShapeDtypeStruct((tensors, m, width), BF16)] * 2
    scratch = []
    for w in weights:
        scratch += ReduceGroups.scratch(far, *w.shape[1:])
    scratch += ReduceAll.scratch(far, *cell)
    scratch += ReduceTensor.scratch(m, width)
    if len(ffn.shape) == 3:
        scratch += ReduceAll.scratch(far, *ffn.shape[1:])
    scratch += [pltpu.VMEM(size, BF16), pltpu.VMEM(cell, BF16)]
    scratch += [pltpu.VMEM((m, width), BF16)] * 2
    return pl.pallas_call(
        functools.partial(finish_kernel, far),
        out_shape=outs,
        in_specs=[ANY] * 6 + [ANY if len(ffn.shape) == 3 else IN_VMEM] + [IN_VMEM] * 6,
        out_specs=[IN_VMEM] * 3 + [ANY] * 3,
        scratch_shapes=scratch + semaphores(50 * far, 14 * far + 30),
        compiler_params=params(ident),
        cost_estimate=cost(110),
    )(*weights, latent, misc, dxn, ffn, *rows)


TILE = 32


def dot_nt(left, right):
    return lax.dot_general(left, right, (((1,), (1,)), ((), ())), preferred_element_type=F32)


def dot_nn(left, right):
    return lax.dot_general(left, right, (((1,), (0,)), ((), ())), preferred_element_type=F32)


def swap_halves(v):
    half = v.shape[1] // 2
    return jnp.concatenate([v[:, half:], v[:, :half]], axis=1)


def attend_kernel(
    heads,
    tokens, gain, w_query, w_latent, gain_lat, w_kv, w_out, cosine, sine,
    partial, xn1, qcat, kv, key_rope, probs, attended, normed_lat, scale_lat, compressed, scale_one,
    q_raw, latent,
):
    rows, width = tokens.shape
    blocks = w_out.shape[0]
    step = width // blocks

    @pl.loop(0, rows // 64)
    def _(i):
        at = pl.ds(pl.multiple_of(i * 64, 64), 64)
        v = tokens[at, :].astype(F32)
        scale = lax.rsqrt(jnp.mean(v * v, axis=-1, keepdims=True) + EPS)
        scale_one[at, :] = scale
        xn1[at, :] = (v * scale * gain[...]).astype(BF16)

    latent[...] = dot_nt(xn1[...], w_latent[...])
    q_raw[...] = dot_nn(xn1[...], w_query[...])

    @pl.loop(0, rows // 128)
    def _(i):
        at = pl.ds(pl.multiple_of(i * 128, 128), 128)
        v = latent[at, :KVR]
        scale = lax.rsqrt(jnp.mean(v * v, axis=-1, keepdims=True) + EPS)
        scale_lat[at, :] = scale
        normed = v * scale
        normed_lat[at, :] = normed
        compressed[at, :] = (normed * gain_lat[...]).astype(BF16)
        rope = latent[at, KVR:]
        c, s = cosine[at, :], sine[at, :]
        key_rope[at, :] = (rope * c + swap_halves(rope) * s).astype(BF16)
        for h in range(heads):
            base = h * (NOPE + ROPE)
            qcat[h, at, :NOPE] = q_raw[at, base : base + NOPE].astype(BF16)
            rope = q_raw[at, base + NOPE : base + NOPE + ROPE]
            qcat[h, at, NOPE:] = (rope * c + swap_halves(rope) * s).astype(BF16)

    kv[...] = dot_nn(compressed[...], w_kv[...]).astype(BF16)
    score_scale = (NOPE + ROPE) ** (-0.5)
    for h in range(heads):
        base = h * (NOPE + VD)

        @pl.loop(0, rows // 128)
        def _(i):
            at = pl.ds(pl.multiple_of(i * 128, 128), 128)
            score = dot_nt(qcat[h, at, :NOPE], kv[:, base : base + NOPE])
            score = (score + dot_nt(qcat[h, at, NOPE:], key_rope[...])) * score_scale
            mine = lax.broadcasted_iota(jnp.int32, score.shape, 0) + i * 128
            seen = lax.broadcasted_iota(jnp.int32, score.shape, 1) <= mine
            score = jnp.where(seen, score, -1e30)
            expo = jnp.exp(score - jnp.max(score, axis=-1, keepdims=True))
            prob = (expo / jnp.sum(expo, axis=-1, keepdims=True)).astype(BF16)
            probs[h, at, :] = prob
            out = dot_nn(prob, kv[:, base + NOPE : base + NOPE + VD])
            attended[at, h * VD : (h + 1) * VD] = out.astype(BF16)

    for e in range(blocks):
        partial[:, e * step : (e + 1) * step] = dot_nn(attended[...], w_out[e]).astype(BF16)


def attend(tokens, gain, w_query, w_latent, gain_lat, w_kv, w_out, cosine, sine):
    rows, width = tokens.shape
    heads = w_out.shape[1] // VD
    like = jax.ShapeDtypeStruct
    outs = [
        like((rows, width), BF16),
        like((rows, width), BF16),
        like((heads, rows, NOPE + ROPE), BF16),
        like((rows, w_kv.shape[1]), BF16),
        like((rows, ROPE), BF16),
        like((heads, rows, rows), BF16),
        like((rows, heads * VD), BF16),
        like((rows, KVR), F32),
        like((rows, 1), F32),
        like((rows, KVR), BF16),
        like((rows, 1), F32),
    ]
    return pl.pallas_call(
        functools.partial(attend_kernel, heads),
        out_shape=outs,
        in_specs=[IN_VMEM] * 9,
        out_specs=[IN_VMEM] * 11,
        scratch_shapes=[
            pltpu.VMEM((rows, w_query.shape[1]), F32),
            pltpu.VMEM((rows, w_latent.shape[0]), F32),
        ],
        compiler_params=pltpu.CompilerParams(vmem_limit_bytes=60 * 2**20),
        cost_estimate=cost(20),
    )(tokens, gain, w_query, w_latent, gain_lat, w_kv, w_out, cosine, sine)


def attend_back_kernel(
    heads,
    dattn, tokens, xn1, qcat, kv, key_rope, probs, attended, normed_lat, scale_lat, compressed, scale_one,
    w_query, w_latent, gain_lat, w_kv, w_out, cosine, sine,
    g_query, g_kv, g_out, g_latent, g_gain, g_gain_lat, dxn,
    dattended, dscore, dq, dkv, dkr, dlatent, turned, dcomp,
):
    rows, width = tokens.shape
    blocks = w_out.shape[0]
    step = width // blocks
    total = jnp.zeros((rows, heads * VD), F32)
    for e in range(blocks):
        total = total + dot_nt(dattn[:, e * step : (e + 1) * step], w_out[e])
    dattended[...] = total.astype(BF16)
    turned_att = attended[...].T
    for e in range(blocks):
        g_out[e] = dot_nn(turned_att, dattn[:, e * step : (e + 1) * step]).astype(BF16)
    score_scale = (NOPE + ROPE) ** (-0.5)
    for h in range(heads):
        base, qbase = h * (NOPE + VD), h * (NOPE + ROPE)

        @pl.loop(0, rows // 128)
        def _(i):
            at = pl.ds(pl.multiple_of(i * 128, 128), 128)
            dprob = dot_nt(dattended[at, h * VD : (h + 1) * VD], kv[:, base + NOPE : base + NOPE + VD])
            prob = probs[h, at, :].astype(F32)
            along = prob * dprob
            ds = (along - prob * jnp.sum(along, axis=-1, keepdims=True)) * score_scale
            dscore[at, :] = ds.astype(BF16)

        @pl.loop(0, rows // 128)
        def _(i):
            at = pl.ds(pl.multiple_of(i * 128, 128), 128)
            ds = dscore[at, :]
            dq[at, qbase : qbase + NOPE] = dot_nn(ds, kv[:, base : base + NOPE]).astype(BF16)
            rope = dot_nn(ds, key_rope[...])
            rope = rope * cosine[at, :] - swap_halves(rope) * sine[at, :]
            dq[at, qbase + NOPE : qbase + NOPE + ROPE] = rope.astype(BF16)

        turned_p = probs[h].T
        dv = dot_nn(turned_p, dattended[:, h * VD : (h + 1) * VD])
        dkv[:, base + NOPE : base + NOPE + VD] = dv.astype(BF16)
        turned_s = dscore[...].T
        dkv[:, base : base + NOPE] = dot_nn(turned_s, qcat[h, :, :NOPE]).astype(BF16)
        rope = dot_nn(turned_s, qcat[h, :, NOPE:])
        dkr[...] = rope if h == 0 else dkr[...] + rope

    turned_c = compressed[...].T
    g_kv[...] = dot_nn(turned_c, dkv[...]).astype(BF16)
    dcomp[...] = dot_nt(dkv[...], w_kv[...])
    dlatent[...] = jnp.zeros_like(dlatent)
    g_gain_lat[...] = jnp.zeros_like(g_gain_lat)

    @pl.loop(0, rows // 128)
    def _(i):
        at = pl.ds(pl.multiple_of(i * 128, 128), 128)
        d, n = dcomp[at, :], normed_lat[at, :]
        g_gain_lat[...] += jnp.sum(d * n, axis=0, keepdims=True)
        weighted = d * gain_lat[...]
        mean = jnp.mean(weighted * n, axis=-1, keepdims=True)
        dlatent[at, :KVR] = (scale_lat[at, :] * (weighted - n * mean)).astype(BF16)
        rope = dkr[at, :]
        rope = rope * cosine[at, :] - swap_halves(rope) * sine[at, :]
        dlatent[at, KVR : KVR + ROPE] = rope.astype(BF16)

    turned[...] = dlatent[...].T
    units = w_latent.shape[0]

    @pl.loop(0, width // 512)
    def _(c):
        at = pl.ds(pl.multiple_of(c * 512, 512), 512)
        g_query[at, :] = dot_nn(xn1[:, at].T, dq[...]).astype(BF16)
        g_latent[:, at] = dot_nn(turned[:units, :], xn1[:, at]).astype(BF16)
        d = dot_nt(dq[...], w_query[at, :]) + dot_nn(dlatent[:, :units], w_latent[:, at])
        dxn[:, at] = d.astype(BF16)
        normed = tokens[:, at].astype(F32) * scale_one[...]
        g_gain[:, at] = jnp.sum(d * normed, axis=0, keepdims=True)


def attend_back(dattn, tokens, kept, w_query, w_latent, gain_lat, w_kv, w_out, cosine, sine):
    rows, width = tokens.shape
    heads = w_out.shape[1] // VD
    like = jax.ShapeDtypeStruct
    units = w_latent.shape[0]
    padded = -(-units // 128) * 128
    outs = [
        like(w_query.shape, BF16),
        like(w_kv.shape, BF16),
        like(w_out.shape, BF16),
        like(w_latent.shape, BF16),
        like((1, width), F32),
        like((1, KVR), F32),
        like((rows, width), BF16),
    ]
    return pl.pallas_call(
        functools.partial(attend_back_kernel, heads),
        out_shape=outs,
        in_specs=[IN_VMEM] * 19,
        out_specs=[IN_VMEM] * 7,
        scratch_shapes=[
            pltpu.VMEM((rows, heads * VD), BF16),
            pltpu.VMEM((rows, rows), BF16),
            pltpu.VMEM((rows, w_query.shape[1]), BF16),
            pltpu.VMEM((rows, w_kv.shape[1]), BF16),
            pltpu.VMEM((rows, ROPE), F32),
            pltpu.VMEM((rows, padded), BF16),
            pltpu.VMEM((padded, rows), BF16),
            pltpu.VMEM((rows, KVR), F32),
        ],
        compiler_params=pltpu.CompilerParams(vmem_limit_bytes=62 * 2**20),
        cost_estimate=cost(40),
    )(dattn, tokens, *kept, w_query, w_latent, gain_lat, w_kv, w_out, cosine, sine)


def experts_kernel(sizes, *refs):
    far, experts, hidden, shared, total = sizes
    groups = 2 * far
    (x_own, dy_own, dy_near, picks, wg_hbm, wu_hbm, wd_hbm, ws_hbm, wr_hbm) = refs[:9]
    (outs_hbm, dg_out, gg_hbm, gu_hbm, gd_hbm, gs_hbm, x_all, dy_all, ffn_all) = refs[9:18]
    (core_in, x0_in, y1_in, y0_in, x1_in, z_in) = refs[18:24]
    (w_in, w_down, h, dh, hs, dgu, hsn, dgun, acc_in, acc_down, x, dy) = refs[24:36]
    (part, ffn_part, acc, own, stage1, stage2, stage3, stage4, dg, dg_in, dg_sum) = refs[36:47]
    (
        ag_s, ag_r, core_s, core_r, x0_s, x0_r, y1_s, y1_r, y0_s, y0_r, x1_s, x1_r, z_s, z_r,
        dg_s, dg_r, wsem, lsem, csem,
    ) = refs[47:]
    routed = experts * hidden
    units = routed + shared
    m, width = x_own.shape
    block, half = 4 * m, m // 2
    chunk = min(256, block)
    per = chunk // m
    low, high = pl.ds(0, half), pl.ds(half, half)
    net = Net(far, None, None, None)
    both, sums = range(2), range(1)

    def remote(src, dst, send, recv, to):
        return pltpu.make_async_remote_copy(
            src_ref=src, dst_ref=dst, send_sem=send, recv_sem=recv, device_id=to, device_id_type=MESH
        )

    def wait_for(ref, sem):
        pltpu.make_async_copy(ref, ref, sem).wait()

    links = ((net.y, net.x), (net.x, net.y))

    def place(q, r, u, v, d=0):
        p = q % 2
        b, c = (u, v) if p == 0 else (v, u)
        return (x_all, dy_all)[q // 2].at[net.slot(-r, b, c, d), (low, high)[p]]

    def pass_on(q, kind, r, u, v, to):
        ref = place(q, r, u, v)
        remote(ref, ref, ag_s.at[q, kind, r], ag_r.at[q, kind, r], to).start()

    def flows(r):
        return range(2 if isinstance(r, int) and r == 0 else 4)

    def rows_z(r):
        for q in range(4):
            ref = place(q, 0, 0, 0)
            src = ref if q < 2 else dy_own.at[net.at()[1], (low, high)[q % 2]]
            remote(src, ref, ag_s.at[q, 0, r], ag_r.at[q, 0, r], net.at(r)).start()

    def rows_a(r):
        for q in flows(r):
            if len(flows(r)) == 4:
                wait_for(place(q, r, 0, 0), ag_r.at[q, 0, r])
            pass_on(q, 1, r, 0, 0, links[q % 2][0])
            pass_on(q, 2, r, 0, 0, links[q % 2][1])
            pass_on(q, 4, r, 0, 0, net.core)

    def rows_b(r):
        for q in flows(r):
            wait_for(place(q, r, 1, 0), ag_r.at[q, 1, r])
            pass_on(q, 3, r, 1, 0, links[q % 2][1])
            pass_on(q, 6, r, 1, 0, net.core)

    def rows_c(r):
        for q in flows(r):
            for u in both:
                wait_for(place(q, r, u, 1), ag_r.at[q, 2 + u, r])
                pass_on(q, 5 + 2 * u, r, u, 1, net.core)

    def rows_d(r):
        for q in flows(r):
            for u in both:
                for v in both:
                    wait_for(place(q, r, u, v, 1), ag_r.at[q, 4 + 2 * u + v, r])

    def block_copies(s, dy_from):
        g = net.group(-(s // 2), 1 - s % 2)
        copies = []
        for t in range(4):
            here = pl.ds(t * m, m)
            copies.append(pltpu.make_async_copy(x_all.at[g * 4 + t], x.at[here], lsem.at[t]))
            source = dy_all.at[g * 4 + t] if dy_from is None else dy_from.at[t]
            copies.append(pltpu.make_async_copy(source, dy.at[here], lsem.at[4 + t]))
        return copies

    def load_block(s):
        pl.when(s == 1)(lambda: begin_all(block_copies(s, dy_own)))
        pl.when(s > 1)(lambda: begin_all(block_copies(s, None)))

    def mine(c, d):
        t = net.at(0, 0, c, d)[1]
        return pl.ds(pl.multiple_of(t * m, m), m)

    def ffn_copy(s):
        g = net.group(-(s // 2), 1 - s % 2)
        rows = pl.ds(pl.multiple_of(g * block, block), block)
        return pltpu.make_async_copy(ffn_part, ffn_all.at[rows], lsem.at[8])

    def core_push(s, a, c):
        return remote(
            part.at[a, mine(c, 1)], core_in.at[a, s, c], core_s.at[a, s, c], core_r.at[a, s, c], net.core
        )

    def x0_push(s, a):
        return remote(acc.at[a, s % 5, 1, low], x0_in.at[a, s], x0_s.at[a, s], x0_r.at[a, s], net.x)

    def y1_push(s, a, c):
        r = s // 2
        return remote(
            acc.at[a, s % 5, c, high], y1_in.at[a, r, c], y1_s.at[a, r, c], y1_r.at[a, r, c], net.y
        )

    def y0_push(s, a):
        r = s // 2
        return remote(acc.at[a, s % 5, 0, low], y0_in.at[a, r], y0_s.at[a, r], y0_r.at[a, r], net.y)

    def x1_push(s, a):
        r = s // 2
        return remote(acc.at[a, s % 5, 1, high], x1_in.at[a, r], x1_s.at[a, r], x1_r.at[a, r], net.x)

    def z_push(s, a):
        r = s // 2
        return remote(acc.at[a, s % 5, 0], z_in.at[a, r], z_s.at[a, r], z_r.at[a, r], net.at(-r))

    def copy_in(ref, buf, sem, k):
        return pltpu.make_async_copy(ref, buf, sem.at[k])

    def h1_loads(s):
        return [copy_in(core_in.at[a, s], stage1.at[a], csem, a) for a in sums]

    def h2_loads(s):
        return [copy_in(x0_in.at[a, s], stage2.at[a], csem, 2 + a) for a in sums]

    def h2_more(s):
        return [copy_in(y1_in.at[a, s // 2], stage3.at[a], csem, 4 + a) for a in sums]

    def h3_loads(s):
        return [copy_in(y0_in.at[a, s // 2], stage4.at[a, 0], csem, 6 + a) for a in sums] + [
            copy_in(x1_in.at[a, s // 2], stage4.at[a, 1], csem, 8 + a) for a in sums
        ]

    def begin_all(copies):
        for c in copies:
            c.start()

    def wait_all(copies):
        for c in copies:
            c.wait()

    def sends_done(s):
        for a in sums:
            x0_push(s, a).wait_send()

        @pl.when(s % 2 == 0)
        def _():
            for a in sums:
                for c in both:
                    y1_push(s, a, c).wait_send()
                y0_push(s, a).wait_send()

        @pl.when(s % 2 == 1)
        def _():
            for a in sums:
                x1_push(s, a).wait_send()
            pl.when(s > 1)(lambda: [z_push(s, a).wait_send() for a in sums] and None)

    def h1_pre(s):
        for a in sums:
            for c in both:
                wait_for(core_in.at[a, s, c], core_r.at[a, s, c])
        begin_all(h1_loads(s))

    def h1_post(s):
        wait_all(h1_loads(s))
        pl.when(s > 4)(lambda: sends_done(s - 5))
        for a in sums:
            for c in (1, 0):
                base = mine(c, 0).start

                @pl.loop(0, m // 16)
                def _(i):
                    rows = pl.ds(pl.multiple_of(i * 16, 16), 16)
                    there = pl.ds(pl.multiple_of(base + i * 16, 16), 16)
                    acc[a, s % 5, c, rows, :] = part[a, there, :] + stage1[a, c, rows, :]

            x0_push(s, a).start()

        @pl.when(s % 2 == 0)
        def _():
            for a in sums:
                for c in both:
                    y1_push(s, a, c).start()

    def add(a, s, c, base, buf):
        @pl.loop(0, half // 16)
        def _(i):
            rows = pl.ds(pl.multiple_of(base + i * 16, 16), 16)
            there = pl.ds(pl.multiple_of(i * 16, 16), 16)
            acc[a, s % 5, c, rows, :] = acc[a, s % 5, c, rows, :] + buf[there, :]

    def h2_pre(s):
        for a in sums:
            wait_for(x0_in.at[a, s], x0_r.at[a, s])
        begin_all(h2_loads(s))

        @pl.when(s % 2 == 1)
        def _():
            for a in sums:
                for c in both:
                    wait_for(y1_in.at[a, s // 2, c], y1_r.at[a, s // 2, c])
            begin_all(h2_more(s))

    def h2_post(s):
        wait_all(h2_loads(s))
        for a in sums:
            add(a, s, 0, 0, stage2.at[a])

        @pl.when(s % 2 == 0)
        def _():
            for a in sums:
                y0_push(s, a).start()

        @pl.when(s % 2 == 1)
        def _():
            wait_all(h2_more(s))
            for a in sums:
                for c in (1, 0):
                    add(a, s, c, half, stage3.at[a, c])
                x1_push(s, a).start()

    def h3_pre(s):
        for a in sums:
            wait_for(y0_in.at[a, s // 2], y0_r.at[a, s // 2])
            wait_for(x1_in.at[a, s // 2], x1_r.at[a, s // 2])
        begin_all(h3_loads(s))

    def h3_post(s):
        wait_all(h3_loads(s))
        for a in sums:
            for k in both:
                add(a, s, 0, k * half, stage4.at[a, k])

        @pl.when(s > 1)
        def _():
            for a in sums:
                z_push(s, a).start()

        @pl.when(s == 1)
        def _():
            for a in sums:
                own[a] = acc[a, 1, 0]

    def weights():
        pairs = []
        for e in range(experts):
            at = pl.ds(e * hidden, hidden)
            pairs.append((wg_hbm.at[e], w_in.at[at]))
            pairs.append((wu_hbm.at[e], w_in.at[pl.ds(units + e * hidden, hidden)]))
            pairs.append((wd_hbm.at[e], w_down.at[at]))
        pairs.append((ws_hbm.at[0], w_in.at[pl.ds(routed, shared)]))
        pairs.append((ws_hbm.at[1], w_in.at[pl.ds(units + routed, shared)]))
        pairs.append((ws_hbm.at[2], w_down.at[pl.ds(routed, shared)]))
        pairs.append((wr_hbm, w_in.at[pl.ds(2 * units, total)]))
        return [pltpu.make_async_copy(a, b, wsem.at[i]) for i, (a, b) in enumerate(pairs)]

    first = pltpu.make_async_copy(x_own, x_all.at[net.slot()], lsem.at[0])
    first.start()
    net.greet(net.line() + [net.at(c=c, d=d) for c, d in ((0, 1), (1, 0), (1, 1))])
    first.wait()
    rows_a(0)
    rows_z(1)
    begin_all(weights())
    acc_in[...] = jnp.zeros_like(acc_in)
    acc_down[...] = jnp.zeros_like(acc_down)
    dg[...] = jnp.zeros_like(dg)
    hs[units:, :] = jnp.zeros((hs.shape[0] - units, block), BF16)
    dgu[2 * units :, :] = jnp.zeros((dgu.shape[0] - 2 * units, block), BF16)
    rows_b(0)
    rows_c(0)
    rows_d(0)
    begin_all(block_copies(0, dy_near))
    wait_all(weights())

    @pl.loop(0, groups)
    def _(s):
        r = s // 2
        g = net.group(-r, 1 - s % 2)
        more = r + 1 < far
        pl.when((s % 2 == 0) & more)(lambda: rows_a(r + 1))
        pl.when((s % 2 == 0) & (r + 2 < far))(lambda: rows_z(r + 2))
        pl.when(s > 0)(lambda: h1_pre(s - 1))
        pl.when(s > 2)(lambda: h2_pre(s - 3))
        wait_all(block_copies(s, None))

        @pl.loop(0, block // chunk)
        def _(n):
            at = pl.ds(pl.multiple_of(n * chunk, chunk), chunk)
            h[...] = dot_nt(w_in[...], x[at, :])
            dh[...] = dot_nt(w_down[...], dy[at, :])
            logits = h[2 * units :, :]
            expo = jnp.exp(logits - jnp.max(logits, axis=0, keepdims=True))
            marked = picks[:, pl.ds(pl.multiple_of(g * block + n * chunk, chunk), chunk)]
            gates = expo / jnp.sum(expo, axis=0, keepdims=True) * marked
            for e in range(experts + 1):
                base, count = (e * hidden, hidden) if e < experts else (routed, shared)
                gate = gates[e : e + 1, :] if e < experts else jnp.ones((1, chunk), F32)

                def body(i, total_):
                    a = pl.multiple_of(base + i * TILE, TILE)
                    here = pl.ds(a, TILE)
                    there = pl.ds(pl.multiple_of(units + a, TILE), TILE)
                    hg, hu, d = h[here, :], h[there, :], dh[here, :]
                    sig = 1.0 / (1.0 + jnp.exp(-hg))
                    act = hg * sig
                    dact = sig + act * (1.0 - sig)
                    hid = act * hu
                    hs[here, at] = (hid * gate).astype(BF16)
                    ds = d * gate
                    dgu[here, at] = (ds * hu * dact).astype(BF16)
                    dgu[there, at] = (ds * act).astype(BF16)
                    return total_ + jnp.sum(hid * d, axis=0, keepdims=True)

                row = lax.fori_loop(0, count // TILE, body, jnp.zeros((1, chunk), F32))
                if e < experts:
                    for j in range(per):
                        dg[n * per + j, g, e : e + 1, :] = row[:, j * m : (j + 1) * m]

        pl.when(s > 0)(lambda: h1_post(s - 1))
        pl.when(s > 2)(lambda: h2_post(s - 3))
        pl.when((s > 4) & (s % 2 == 0))(lambda: h3_pre(s - 5))
        pl.when((s % 2 == 1) & more)(lambda: rows_c(r + 1))

        @pl.loop(0, width // 512)
        def _(c):
            at = pl.ds(pl.multiple_of(c * 512, 512), 512)
            acc_in[:, at] += dot_nn(dgu[: 2 * units, :], x[:, at])
            acc_down[:, at] += dot_nn(hs[:units, :], dy[:, at])

        pl.when((s > 4) & (s % 2 == 0))(lambda: h3_post(s - 5))
        pl.when((s % 2 == 1) & more)(lambda: rows_d(r + 1))
        pl.when(s + 1 < groups)(lambda: load_block(s + 1))
        hsn[...] = hs[...].T
        dgun[...] = dgu[...].T

        @pl.when(s > 0)
        def _():
            for c in both:
                core_push(s - 1, 0, c).wait_send()
            ffn_copy(s - 1).wait()

        @pl.loop(0, width // 512)
        def _(c):
            at = pl.ds(pl.multiple_of(c * 512, 512), 512)
            part[0, :, at] = dot_nn(dgun[:, : 2 * units], w_in[: 2 * units, at]).astype(BF16)

        for c in (1, 0):
            core_push(s, 0, c).start()

        @pl.loop(0, width // 512)
        def _(c):
            at = pl.ds(pl.multiple_of(c * 512, 512), 512)
            ffn_part[:, at] = dot_nn(hsn[:, :units], w_down[:, at]).astype(BF16)

        ffn_copy(s).start()
        pl.when((s % 2 == 0) & more)(lambda: rows_b(r + 1))

    def stores():
        pairs = []
        for e in range(experts):
            at = pl.ds(e * hidden, hidden)
            pairs.append((acc_in.at[at], gg_hbm.at[e]))
            pairs.append((acc_in.at[pl.ds(units + e * hidden, hidden)], gu_hbm.at[e]))
            pairs.append((acc_down.at[at], gd_hbm.at[e]))
        pairs.append((acc_in.at[pl.ds(routed, shared)], gs_hbm.at[0]))
        pairs.append((acc_in.at[pl.ds(units + routed, shared)], gs_hbm.at[1]))
        pairs.append((acc_down.at[pl.ds(routed, shared)], gs_hbm.at[2]))
        return [pltpu.make_async_copy(a, b, wsem.at[i]) for i, (a, b) in enumerate(pairs)]

    peers = [(c, d) for c in both for d in both][1:]

    def dg_push(k):
        c, d = peers[k]
        e, t = net.at(0, 0, c, d)
        return remote(dg.at[t], dg_in.at[k], dg_s.at[k], dg_r.at[k], (e, t))

    for k in range(3):
        dg_push(k).start()
    last = groups - 1
    h1_pre(last)
    h2_pre(last - 2)
    h1_post(last)
    begin_all(stores())
    h2_post(last - 2)
    h2_pre(last - 1)
    h2_post(last - 1)
    h3_pre(last - 4)
    h3_post(last - 4)
    h3_pre(last - 2)
    h3_post(last - 2)
    for k in range(3):
        wait_for(dg_in.at[k], dg_r.at[k])
    dg_sum[...] = dg[net.at()[1]] + dg_in[0] + dg_in[1] + dg_in[2]
    me = net.group()
    dg_out[me] = dg_sum[me]
    others = [(r, b) for r in range(far) for b in both][1:]

    def dg_give(k):
        to = net.at(*others[k])
        return remote(dg_sum.at[to[0]], dg_out.at[me], dg_s.at[3 + k], dg_r.at[3 + k], to)

    for k in range(len(others)):
        dg_give(k).start()
    h2_pre(last)
    h2_post(last)
    h3_pre(last)
    h3_post(last)
    for r in range(1, far):
        for a in sums:
            wait_for(z_in.at[a, r], z_r.at[a, r])
            got = pltpu.make_async_copy(z_in.at[a, r], stage1.at[a, 0], csem.at[a])
            got.start()
            got.wait()

            @pl.loop(0, m // 16)
            def _(i):
                rows = pl.ds(pl.multiple_of(i * 16, 16), 16)
                own[a, rows, :] = own[a, rows, :] + stage1[a, 0, rows, :]

    give = pltpu.make_async_copy(own, outs_hbm, csem.at[0])
    give.start()
    for k in range(len(others)):
        r, b = others[k]
        wait_for(dg_out.at[net.group(-r, b)], dg_r.at[3 + k])
    for s in range(last - 4, last + 1):
        sends_done(s)
    for c in both:
        core_push(last, 0, c).wait_send()
    ffn_copy(last).wait()
    for q in range(4):
        for r in range(far):
            for kind in range(8):
                if r or (kind and q < 2):
                    wait_for(place(q, 0, 0, 0), ag_s.at[q, kind, r])
    for k in range(3):
        dg_push(k).wait_send()
    for k in range(len(others)):
        dg_give(k).wait_send()
    wait_all(stores())
    give.wait()


def experts_all(x, dy_own, dy_near, picks, wg, wu, wd, ws, wr, groups, tensors, ident):
    m, width = x.shape
    far = groups // 2
    experts, hidden, _ = wg.shape
    shared, total = ws.shape[1], wr.shape[0]
    units = experts * hidden + shared
    block, half = 4 * m, m // 2
    chunk = min(256, block)
    up = lambda v: -(-v // 128) * 128
    like = jax.ShapeDtypeStruct
    outs = [
        like((1, m, width), BF16),
        like((groups, 8, m), F32),
        like(wg.shape, F32),
        like(wu.shape, F32),
        like(wd.shape, F32),
        like(ws.shape, F32),
        like((groups * tensors, m, width), BF16),
        like((groups * tensors, m, width), BF16),
        like((groups * block, width), BF16),
        like((1, groups, 2, m, width), BF16),
        like((1, groups, half, width), BF16),
        like((1, far, 2, half, width), BF16),
        like((1, far, half, width), BF16),
        like((1, far, half, width), BF16),
        like((1, far, m, width), BF16),
    ]
    dma = pltpu.SemaphoreType.DMA
    scratch = [
        pltpu.VMEM((2 * units + total, width), BF16),
        pltpu.VMEM((units, width), BF16),
        pltpu.VMEM((2 * units + total, chunk), F32),
        pltpu.VMEM((units, chunk), F32),
        pltpu.VMEM((up(units), block), BF16),
        pltpu.VMEM((up(2 * units), block), BF16),
        pltpu.VMEM((block, up(units)), BF16),
        pltpu.VMEM((block, up(2 * units)), BF16),
        pltpu.VMEM((2 * units, width), F32),
        pltpu.VMEM((units, width), F32),
        pltpu.VMEM((block, width), BF16),
        pltpu.VMEM((block, width), BF16),
        pltpu.VMEM((1, block, width), BF16),
        pltpu.VMEM((block, width), BF16),
        pltpu.VMEM((1, 5, 2, m, width), BF16),
        pltpu.VMEM((1, m, width), BF16),
        pltpu.VMEM((1, 2, m, width), BF16),
        pltpu.VMEM((1, half, width), BF16),
        pltpu.VMEM((1, 2, half, width), BF16),
        pltpu.VMEM((1, 2, half, width), BF16),
        pltpu.VMEM((tensors, groups, 8, m), F32),
        pltpu.VMEM((3, groups, 8, m), F32),
        pltpu.VMEM((groups, 8, m), F32),
    ]
    for shape in (
        (4, 8, far), (1, groups, 2), (1, groups), (1, far, 2), (1, far), (1, far), (1, far), (groups + 2,),
    ):
        scratch += [dma(shape), dma(shape)]
    scratch += [dma((3 * experts + 4,)), dma((9,)), dma((10,))]
    got = pl.pallas_call(
        functools.partial(experts_kernel, (far, experts, hidden, shared, total)),
        out_shape=outs,
        in_specs=[ANY] * 3 + [IN_VMEM] + [ANY] * 5,
        out_specs=[ANY, IN_VMEM] + [ANY] * 13,
        scratch_shapes=scratch,
        compiler_params=params(ident, 63),
        cost_estimate=cost(280),
    )(x, dy_own, dy_near, picks, wg, wu, wd, ws, wr)
    return [*got[:6], got[8]]


BOTH = ("expert", "tensor")


def shards(
    tokens,
    lengths,
    routes,
    gain_attn,
    w_query,
    w_latent,
    gain_latent,
    w_kv,
    w_out,
    gain_ffn,
    w_router,
    w_shared_gate,
    w_shared_up,
    w_shared_down,
    w_gate,
    w_up,
    w_down,
    cotangent,
):
    groups = lax.axis_size("expert")
    tensors = lax.axis_size("tensor")
    eindex = lax.axis_index("expert")
    tindex = lax.axis_index("tensor")
    rows, width = tokens.shape
    quarter = rows // tensors
    experts_local, _, hidden_units = w_gate.shape
    total_experts = experts_local * groups
    every = groups * rows
    bf16, f32 = jnp.bfloat16, jnp.float32

    def own(v):
        return lax.dynamic_slice_in_dim(v, tindex * quarter, quarter, 0)

    live_int = (jnp.arange(rows) < lengths[0]).astype(jnp.int32)
    live = live_int.astype(f32)[:, None]
    live_own = own(live)
    cot_own = own(cotangent).astype(f32)
    dffn_group = (cotangent * live.astype(bf16)).reshape(tensors, quarter, width)
    dffn_own = own(cotangent) * live_own.astype(bf16)

    part = w_shared_down.shape[0] // groups
    spare = -part % TILE

    def shared_units(v):
        v = jnp.pad(v.reshape(groups, part, v.shape[1]), ((0, 0), (0, spare), (0, 0)))
        return v

    shared_w = jnp.stack(
        [shared_units(v) for v in (w_shared_gate.T, w_shared_up.T, w_shared_down)], axis=1
    )
    choose = jnp.any(routes[..., None] == jnp.arange(total_experts), axis=1).astype(F32)
    picks = choose * live
    query_w, kv_up, out_proj, shared_w, marks, dffn_near = begin(
        (w_query, w_kv, w_out),
        shared_w.reshape(groups, -1, shared_w.shape[-1]),
        picks.T.astype(BF16),
        dffn_own,
        groups,
        tensors,
        0,
    )
    query_w = query_w.reshape(width, -1)
    kv_up = kv_up.reshape(KVR, -1)
    shared_w = shared_w.transpose(1, 0, 2).reshape(3, part + spare, width)
    gate_t, up_t = w_gate.transpose(0, 2, 1), w_up.transpose(0, 2, 1)
    router_t = jnp.roll(w_router.T, -eindex * experts_local, axis=0)
    parts = max(1, every // 4096)
    some = quarter // parts

    def split(v):
        return v.reshape(parts, some, v.shape[1])

    marks = marks.reshape(groups, total_experts, tensors, parts, some).transpose(3, 1, 0, 2, 4)
    picks_all = marks.reshape(parts, total_experts, -1).astype(F32)
    picks_all = jnp.roll(picks_all, -eindex * experts_local, axis=1)
    xf = tokens.astype(f32)
    cosine, sine = rope_tables(rows, ROPE)
    cosine = jnp.concatenate([cosine, cosine], axis=1)
    sine = jnp.concatenate([-sine, sine], axis=1)
    attend_w = (query_w, w_latent.T, gain_latent[None], kv_up, out_proj, cosine, sine)
    partial, *kept = attend(tokens, gain_attn[None], *attend_w)
    scale_one = own(kept[-1])
    normed_one = own(xf) * scale_one
    partial = partial.reshape(tensors, quarter, width)
    attn = sum_tensor(partial, groups, parts + 2)
    resid = own(xf) + live_own * attn
    scale_two = inv_rms(resid)
    normed_two = resid * scale_two
    xn2_own = (normed_two * gain_ffn).astype(bf16)
    router = jax.nn.softmax(mat(xn2_own, w_router), axis=-1)
    outs = []
    for k in range(parts):
        dx, dgates, *grads, ffn = experts_all(
            split(xn2_own)[k],
            dffn_group[:, k * some : (k + 1) * some],
            dffn_near[:, k * some : (k + 1) * some],
            picks_all[k],
            gate_t,
            up_t,
            w_down,
            shared_w,
            router_t,
            groups,
            tensors,
            k + 1,
        )
        dx = dx[0].astype(F32)
        ffn = ffn.reshape(-1, some, width)
        if parts > 1:
            ffn = reduce_rows(ffn, groups, parts + 4 + k)
        dgates = dgates[:, :experts_local].reshape(total_experts, some).T
        outs.append((ffn, dx, dgates, *grads))
    dx, dgates = (jnp.concatenate(v, axis=0) for v in list(zip(*outs))[1:3])
    ffn = outs[0][0] if parts == 1 else jnp.concatenate([v[0] for v in outs], axis=0)
    grads = [functools.reduce(jnp.add, v) for v in list(zip(*outs))[3:]]
    drouter = own(picks) * dgates
    grad_gate, grad_up = (v.transpose(0, 2, 1) for v in grads[:2])
    grad_down = grads[2]
    dlogit = router * (drouter - jnp.sum(router * drouter, axis=-1, keepdims=True))
    grad_router = mat_tn(dlogit.astype(bf16), xn2_own)
    dnorm_two = dx + mat_nt(dlogit.astype(bf16), w_router)
    grad_gain_ffn = jnp.sum(dnorm_two * normed_two, axis=0)
    dresid = cot_own + norm_back(dnorm_two, normed_two, scale_two, gain_ffn)
    shared_g = grads[3].reshape(3, part + spare, groups, width // groups).astype(BF16)
    shared_g = shared_g.transpose(2, 0, 1, 3).reshape(groups, -1, width // groups)
    dattn, shared_g = gather_tensor((dresid * live_own).astype(bf16), shared_g, groups, tensors, parts + 3)
    dattn = dattn.reshape(rows, width)
    grad_query, grad_kv, grad_out, grad_latent, grad_gain_attn, grad_gain_latent, dnorm_one = (
        attend_back(dattn, tokens, kept, *attend_w)
    )
    down = cells(groups, tensors)[0]

    def whole_cells(v):
        return jnp.pad(v, ((0, -v.shape[0] % (16 * down)), (0, 0)))

    latent_g = whole_cells(grad_latent)
    misc = jnp.concatenate(
        [
            grad_router,
            grad_gain_attn,
            grad_gain_ffn[None],
            jnp.pad(grad_gain_latent, ((0, 0), (0, width - KVR))),
        ],
        axis=0,
    )
    misc = whole_cells(misc.astype(bf16))
    grad_query, grad_kv, grad_out, small, grad_tokens, output = finish(
        (
            grad_query.reshape(groups, -1, grad_query.shape[1]),
            grad_kv.reshape(groups, -1, grad_kv.shape[1]),
            grad_out,
        ),
        latent_g,
        misc,
        dnorm_one.reshape(tensors, quarter, width),
        ffn,
        (dresid, normed_one, scale_one, gain_attn[None], resid, live_own),
        groups,
        tensors,
        parts + 1,
    )
    grad_tokens = grad_tokens.reshape(rows, width)
    output = output.reshape(rows, width)
    small = small.reshape(down, -1, width)
    tall = latent_g.shape[0] // down
    grad_latent = small[:, :tall].reshape(-1, width)[: w_latent.shape[1]].astype(f32).T
    misc = small[:, tall:].reshape(-1, width).astype(f32)
    grad_router = misc[:total_experts].T
    grad_gain_attn = misc[total_experts]
    grad_gain_ffn = misc[total_experts + 1]
    grad_gain_latent = misc[total_experts + 2, :KVR]
    shared_g = shared_g.reshape(groups, 3, part + spare, -1)[:, :, :part].transpose(1, 0, 2, 3)
    shared_g = shared_g.reshape(3, groups * part, -1).astype(f32)
    grad_sgate, grad_sup, grad_sdown = shared_g[0].T, shared_g[1].T, shared_g[2]
    return (
        output,
        grad_tokens,
        grad_gain_attn,
        grad_query,
        grad_latent,
        grad_gain_latent,
        grad_kv,
        grad_out,
        grad_gain_ffn,
        grad_router,
        grad_sgate,
        grad_sup,
        grad_sdown,
        grad_gate,
        grad_up,
        grad_down,
    )


def solution(mesh):
    in_specs = (
        P("expert", None),
        P("expert"),
        P("expert", None),
        P(),
        P("expert", "tensor"),
        P(),
        P(),
        P("expert", "tensor"),
        P("tensor", "expert"),
        P(),
        P(),
        P("expert", "tensor"),
        P("expert", "tensor"),
        P("tensor", "expert"),
        P("expert", None, "tensor"),
        P("expert", None, "tensor"),
        P("expert", "tensor", None),
        P("expert", None),
    )
    out_specs = (
        P("expert", None),
        P("expert", None),
        P(),
        P("expert", "tensor"),
        P(),
        P(),
        P("expert", "tensor"),
        P("tensor", "expert"),
        P(),
        P(),
        P("expert", "tensor"),
        P("expert", "tensor"),
        P("tensor", "expert"),
        P("expert", None, "tensor"),
        P("expert", None, "tensor"),
        P("expert", "tensor", None),
    )
    return jax.shard_map(shards, mesh=mesh, in_specs=in_specs, out_specs=out_specs, check_vma=False)
```

```python
import functools

import jax
import jax.numpy as jnp
from jax import lax
from jax.experimental import pallas as pl
from jax.experimental.pallas import tpu as pltpu
from jax.sharding import PartitionSpec as P

F32, BF16 = jnp.float32, jnp.bfloat16

NOPE = 128
ROPE = 64
VD = 128
KVR = 512


EPS = 1e-06
ROPE_BASE = 10000.0


def inv_rms(v):
    return lax.rsqrt(jnp.mean(v * v, axis=-1, keepdims=True) + EPS)


def rope_tables(count, width):
    half = width // 2
    freq = ROPE_BASE ** (-(jnp.arange(half, dtype=jnp.float32) * 2.0 / width))
    angle = jnp.arange(count, dtype=jnp.float32)[:, None] * freq[None, :]
    return (jnp.cos(angle), jnp.sin(angle))


def rotate(v, cosine, sine):
    half = v.shape[-1] // 2
    first = v[..., :half]
    second = v[..., half:]
    return jnp.concatenate(
        [first * cosine - second * sine, second * cosine + first * sine], axis=-1
    )


def rotate_back(grad, cosine, sine):
    half = grad.shape[-1] // 2
    first = grad[..., :half]
    second = grad[..., half:]
    return jnp.concatenate(
        [first * cosine + second * sine, second * cosine - first * sine], axis=-1
    )


def norm_back(grad, normed, scale_row, gain):
    weighted = grad * gain
    return scale_row * (weighted - normed * jnp.mean(weighted * normed, axis=-1, keepdims=True))


def silu_parts(gate):
    sig = jax.nn.sigmoid(gate)
    return (gate * sig, sig * (1.0 + gate * (1.0 - sig)))


def mat(left, right):
    return jnp.dot(left, right, preferred_element_type=jnp.float32)


def mat_tn(left, right):
    return lax.dot_general(
        left, right, (((0,), (0,)), ((), ())), preferred_element_type=jnp.float32
    )


def mat_nt(left, right):
    return lax.dot_general(
        left, right, (((1,), (1,)), ((), ())), preferred_element_type=jnp.float32
    )


MESH = pl.DeviceIdType.MESH
ANY = pl.BlockSpec(memory_space=pl.ANY)
IN_VMEM = pl.BlockSpec(memory_space=pltpu.VMEM)


def places():
    e, t = lax.axis_index("expert"), lax.axis_index("tensor")
    return e // 2, e % 2, t // 2, t % 2


def far_first(far):
    return sorted(range(far), key=lambda r: -min(r, far - r))


class Net:
    def __init__(self, far, send, recv, local):
        self.far, self.send, self.recv, self.local = far, send, recv, local
        self.e1, self.e0, self.t1, self.t0 = places()
        self.count, self.started, self.locals = 0, [], 0
        self.core = self.at(d=1)
        self.x = self.at(c=1)
        self.y = self.at(b=1)

    def at(self, r=0, b=0, c=0, d=0):
        e = (self.e1 + r + self.far) % self.far * 2 + (self.e0 + b) % 2
        return (e, (self.t1 + c) % 2 * 2 + (self.t0 + d) % 2)

    def slot(self, r=0, b=0, c=0, d=0):
        e, t = self.at(r, b, c, d)
        return e * 4 + t

    def group(self, r=0, b=0):
        return self.at(r, b)[0]

    def greet(self, peers):
        barrier = pltpu.get_barrier_semaphore()
        for peer in peers:
            pl.semaphore_signal(barrier, inc=1, device_id=peer, device_id_type=MESH)
        pl.semaphore_wait(barrier, len(peers))

    def near(self):
        return [self.at(r) for r in range(1, self.far)] + [self.y, self.x, self.core]

    def line(self):
        every = [self.at(r, b) for r in range(self.far) for b in range(2)]
        return every[1:]

    def push(self, src, dst, to):
        k = self.count
        self.count += 1
        copy = pltpu.make_async_remote_copy(
            src_ref=src,
            dst_ref=dst,
            send_sem=self.send.at[k],
            recv_sem=self.recv.at[k],
            device_id=to,
            device_id_type=MESH,
        )
        copy.start()
        self.started.append(copy)
        return k

    def arrived(self, ref, k):
        pltpu.make_async_copy(ref, ref, self.recv.at[k]).wait()

    def load(self, src, dst):
        copy = pltpu.make_async_copy(src, dst, self.local.at[self.locals])
        self.locals += 1
        copy.start()
        return copy

    def finish(self):
        for copy in self.started:
            copy.wait_send()


def add_rows(dst, src, step=16):
    @pl.loop(0, dst.shape[0] // step)
    def _(i):
        rows = pl.ds(pl.multiple_of(i * step, step), step)
        dst[rows, :] = dst[rows, :] + src[rows, :]


class GatherAll:
    def __init__(self, net, own, out_at, order):
        self.net, self.own, self.out_at, self.order = net, own, out_at, order
        self.z, self.first, self.second, self.cores = {}, {}, {}, {}

    def place(self, r, u, v, d=0):
        b, c = (u, v) if self.order == "yx" else (v, u)
        return self.out_at(self.net.slot(-r, b, c, d))

    def pass_on(self, r, u, v, to):
        here = self.own if (r, u, v) == (0, 0, 0) else self.place(r, u, v)
        return self.net.push(here, self.place(r, u, v), to)

    def start(self):
        for r in range(1, self.net.far):
            self.z[r] = self.pass_on(0, 0, 0, self.net.at(r))
        self.links = (self.net.y, self.net.x)[:: 1 if self.order == "yx" else -1]

    def stage_a(self, r):
        if r:
            self.net.arrived(self.place(r, 0, 0), self.z[r])
        self.first[r] = self.pass_on(r, 0, 0, self.links[0])
        self.second[r, 0] = self.pass_on(r, 0, 0, self.links[1])
        self.cores[r, 0, 0] = self.pass_on(r, 0, 0, self.net.core)

    def stage_b(self, r):
        self.net.arrived(self.place(r, 1, 0), self.first[r])
        self.second[r, 1] = self.pass_on(r, 1, 0, self.links[1])
        self.cores[r, 1, 0] = self.pass_on(r, 1, 0, self.net.core)

    def stage_c(self, r):
        for u in range(2):
            self.net.arrived(self.place(r, u, 1), self.second[r, u])
            self.cores[r, u, 1] = self.pass_on(r, u, 1, self.net.core)

    def steps(self):
        return [self.stage_a, self.stage_b, self.stage_c]

    def end(self):
        for (r, u, v), k in self.cores.items():
            self.net.arrived(self.place(r, u, v, 1), k)


class ReduceAll:
    def __init__(self, net, part_at, acc, from_core, from_first, from_second, from_z, order):
        self.net, self.part_at, self.acc, self.order = net, part_at, acc, order
        self.bufs = (from_core, from_first, from_second, from_z)
        self.core, self.first, self.second, self.z, self.loads = {}, {}, {}, {}, {}
        self.turn = far_first(net.far)
        self.spots = ((1, 1), (0, 1), (1, 0), (0, 0))
        self.links = (net.x, net.y) if order == "xy" else (net.y, net.x)

    def dest(self, r, u, v, d):
        b, c = (v, u) if self.order == "xy" else (u, v)
        return self.part_at(self.net.slot(r, b, c, d))

    def load(self):
        for r in self.turn:
            for u, v in self.spots:
                k = r * 4 + u * 2 + v
                self.loads[k] = self.net.load(self.dest(r, u, v, 0), self.acc.at[k])

    def start(self):
        for r in self.turn:
            for u, v in self.spots:
                k = r * 4 + u * 2 + v
                self.core[k] = self.net.push(
                    self.dest(r, u, v, 1), self.bufs[0].at[k], self.net.core
                )

    def merge(self, k, buf, i, token):
        self.net.arrived(buf.at[i], token)
        add_rows(self.acc.at[k], buf.at[i])

    def stage_a(self, i):
        r = self.turn[i]
        for u, v in self.spots:
            k = r * 4 + u * 2 + v
            self.loads[k].wait()
            self.merge(k, self.bufs[0], k, self.core[k])
            if u:
                at = r * 2 + v
                self.first[at] = self.net.push(
                    self.acc.at[k], self.bufs[1].at[at], self.links[0]
                )

    def stage_b(self, i):
        r = self.turn[i]
        for v in (1, 0):
            at = r * 2 + v
            self.merge(r * 4 + v, self.bufs[1], at, self.first[at])
            if v:
                self.second[r] = self.net.push(
                    self.acc.at[r * 4 + v], self.bufs[2].at[r], self.links[1]
                )

    def stage_c(self, i):
        r = self.turn[i]
        self.merge(r * 4, self.bufs[2], r, self.second[r])
        if r:
            self.z[r] = self.net.push(
                self.acc.at[r * 4], self.bufs[3].at[r - 1], self.net.at(r)
            )

    def steps(self):
        return [self.stage_a, self.stage_b, self.stage_c]

    def end(self):
        for r in range(1, self.net.far):
            self.net.arrived(self.bufs[3].at[r - 1], self.z[r])

    def total(self, rows):
        total = self.acc[0, rows, :].astype(F32)
        for r in range(1, self.net.far):
            total = total + self.bufs[3][r - 1, rows, :].astype(F32)
        return total

    @staticmethod
    def scratch(far, rows, width):
        return [
            pltpu.VMEM((4 * far, rows, width), BF16),
            pltpu.VMEM((4 * far, rows, width), BF16),
            pltpu.VMEM((2 * far, rows, width), BF16),
            pltpu.VMEM((far, rows, width), BF16),
            pltpu.VMEM((far - 1, rows, width), BF16),
        ]


class ReduceDirect(ReduceAll):
    def stage_b(self, i):
        r = self.turn[i]
        for v in (1, 0):
            at = r * 2 + v
            self.merge(r * 4 + v, self.bufs[1], at, self.first[at])
            if at:
                self.z[at] = self.net.push(
                    self.acc.at[r * 4 + v], self.bufs[2].at[at], self.net.at(r, v)
                )

    def end(self):
        for at, k in self.z.items():
            self.net.arrived(self.bufs[2].at[at], k)

    def total(self, rows):
        total = self.acc[0, rows, :].astype(F32)
        for at in range(1, 2 * self.net.far):
            total = total + self.bufs[2][at, rows, :].astype(F32)
        return total

    @staticmethod
    def scratch(far, rows, width):
        return [
            pltpu.VMEM((4 * far, rows, width), BF16),
            pltpu.VMEM((4 * far, rows, width), BF16),
            pltpu.VMEM((2 * far, rows, width), BF16),
            pltpu.VMEM((2 * far, rows, width), BF16),
        ]


class GatherDirect:
    def __init__(self, net, own, out_at):
        self.net, self.own, self.out_at = net, own, out_at
        self.spots = [(r, b) for r in range(net.far) for b in range(2)]
        self.direct, self.x, self.cores = {}, {}, {}

    def place(self, r, b, c=0, d=0):
        return self.out_at(self.net.slot(-r, b, c, d))

    def start(self):
        for r, b in self.spots[1:]:
            self.direct[r, b] = self.net.push(self.own, self.place(0, 0), self.net.at(r, b))

    def stage_a(self, i):
        r, b = self.spots[i]
        here = self.place(r, b) if i else self.own
        if i:
            self.net.arrived(here, self.direct[r, b])
        self.x[r, b] = self.net.push(here, self.place(r, b), self.net.x)
        self.cores[r, b, 0] = self.net.push(here, self.place(r, b), self.net.core)

    def stage_b(self, i):
        r, b = self.spots[i]
        here = self.place(r, b, 1)
        self.net.arrived(here, self.x[r, b])
        self.cores[r, b, 1] = self.net.push(here, here, self.net.core)

    def end(self):
        for (r, b, c), k in self.cores.items():
            self.net.arrived(self.place(r, b, c, 1), k)


class Summed:
    def __init__(self, ref):
        self.ref = ref

    def load(self):
        pass

    start = end = load

    def stage_a(self, i):
        pass

    stage_b = stage_c = stage_a

    def total(self, rows):
        return self.ref[rows, :]


def pipelined(far, parts):
    for i in range(far + 2):
        for s in range(3):
            for part in parts:
                if 0 <= i - s < far:
                    part.steps()[s](i - s)


def semaphores(remote, local):
    return [
        pltpu.SemaphoreType.DMA((remote,)),
        pltpu.SemaphoreType.DMA((remote,)),
        pltpu.SemaphoreType.DMA((local,)),
    ]


def cost(us):
    return pl.CostEstimate(flops=0, bytes_accessed=us * 3_000_000, transcendentals=0)


def params(ident, mib=60):
    return pltpu.CompilerParams(
        collective_id=ident, has_side_effects=True, vmem_limit_bytes=mib * 2**20
    )


def begin_kernel(far, *refs):
    n = 3
    ws, blocks, marks, dy = refs[:n], refs[n], refs[n + 1], refs[n + 2]
    outs, blocks_out, marks_out, near = refs[n + 3 : 2 * n + 3], *refs[2 * n + 3 : 2 * n + 6]
    net = Net(far, *refs[2 * n + 6 :])
    me = net.group()
    mine = [net.load(w, o.at[me]) for w, o in zip(ws, outs)]
    mine.append(net.load(blocks.at[me], blocks_out.at[me]))
    mine.append(net.load(marks, marks_out.at[me]))
    net.greet(net.line() + [net.x, net.core])
    here = [near.at[net.at(0, 0, c, d)[1]] for c in range(2) for d in range(2)]
    dy_y = net.push(dy, here[0], net.y)
    tokens = {}
    others = [(r, b) for r in range(far) for b in range(2)][1:]
    for a, (w, o) in enumerate(zip(ws, outs)):
        for r in range(1, far):
            tokens[a, r] = net.push(w, o.at[me], net.at(r))
        tokens[a, 0, 1] = net.push(w, o.at[me], net.y)
    small = []
    for r, b in others:
        small.append((r, b, marks_out, net.push(marks, marks_out.at[me], net.at(r, b))))
    net.arrived(here[0], dy_y)
    dy_x = net.push(here[0], here[0], net.x)
    dy_core = net.push(here[0], here[0], net.core)
    for a, (w, o) in enumerate(zip(ws, outs)):
        for r in range(1, far):
            place = o.at[net.group(-r)]
            net.arrived(place, tokens[a, r])
            tokens[a, r, 1] = net.push(place, place, net.y)
    for r, b in others:
        to = net.at(r, b)
        small.append((r, b, blocks_out, net.push(blocks.at[to[0]], blocks_out.at[me], to)))
    net.arrived(here[2], dy_x)
    dy_both = net.push(here[2], here[2], net.core)
    for a, o in enumerate(outs):
        for r in range(far):
            net.arrived(o.at[net.group(-r, 1)], tokens[a, r, 1])
    net.arrived(here[1], dy_core)
    net.arrived(here[3], dy_both)
    for r, b, ref, k in small:
        net.arrived(ref.at[net.group(-r, b)], k)
    net.finish()
    for copy in mine:
        copy.wait()


def begin(ws, blocks, marks, dy, groups, tensors, ident):
    far = groups // 2
    outs = [jax.ShapeDtypeStruct((groups, *w.shape), w.dtype) for w in ws]
    outs.append(jax.ShapeDtypeStruct(blocks.shape, blocks.dtype))
    outs.append(jax.ShapeDtypeStruct((groups, *marks.shape), marks.dtype))
    outs.append(jax.ShapeDtypeStruct((tensors, *dy.shape), dy.dtype))
    return pl.pallas_call(
        functools.partial(begin_kernel, far),
        out_shape=outs,
        in_specs=[ANY] * 6,
        out_specs=[ANY] * 6,
        scratch_shapes=semaphores(10 * far, 5),
        compiler_params=params(ident),
        cost_estimate=cost(100),
    )(*ws, blocks, marks, dy)


class ReduceGroups:
    def __init__(self, net, part, out, acc, from_y, from_z):
        self.net, self.part, self.out = net, part, out
        self.acc, self.from_y, self.from_z = acc, from_y, from_z
        self.turn = far_first(net.far)
        self.y, self.z = {}, {}

    def load(self):
        self.loads = {
            r: self.net.load(self.part.at[self.net.group(r)], self.acc.at[r]) for r in self.turn
        }

    def start(self, r):
        part = self.part.at[self.net.group(r, 1)]
        self.y[r] = self.net.push(part, self.from_y.at[r], self.net.y)

    def step(self, r):
        self.loads[r].wait()
        self.net.arrived(self.from_y.at[r], self.y[r])
        add_rows(self.acc.at[r], self.from_y.at[r])
        if r:
            self.z[r] = self.net.push(self.acc.at[r], self.from_z.at[r - 1], self.net.at(r))

    def end(self):
        for r in range(1, self.net.far):
            self.net.arrived(self.from_z.at[r - 1], self.z[r])

        @pl.loop(0, self.out.shape[0] // 16)
        def _(i):
            rows = pl.ds(pl.multiple_of(i * 16, 16), 16)
            total = self.acc[0, rows, :].astype(F32)
            for r in range(1, self.net.far):
                total = total + self.from_z[r - 1, rows, :].astype(F32)
            self.out[rows, :] = total

    @staticmethod
    def scratch(far, rows, width):
        return [
            pltpu.VMEM((far, rows, width), BF16),
            pltpu.VMEM((far, rows, width), BF16),
            pltpu.VMEM((far - 1, rows, width), BF16),
        ]


class GatherTensor:
    def __init__(self, net, own, out):
        self.net, self.own, self.out = net, own, out

    def place(self, c, d):
        return self.out.at[self.net.at(0, 0, c, d)[1]]

    def start(self):
        net = self.net
        self.mine = net.load(self.own, self.place(0, 0))
        self.x = net.push(self.own, self.place(0, 0), net.x)
        self.c0 = net.push(self.own, self.place(0, 0), net.core)

    def step(self):
        self.net.arrived(self.place(1, 0), self.x)
        self.c1 = self.net.push(self.place(1, 0), self.place(1, 0), self.net.core)

    def end(self):
        self.net.arrived(self.place(0, 1), self.c0)
        self.net.arrived(self.place(1, 1), self.c1)
        self.mine.wait()


class ReduceTensor:
    def __init__(self, net, part, acc, from_core, from_x):
        self.net, self.part = net, part
        self.acc, self.from_core, self.from_x = acc, from_core, from_x

    def at(self, c, d):
        return self.part.at[self.net.at(0, 0, c, d)[1]]

    def load(self):
        self.loads = [self.net.load(self.at(c, 0), self.acc.at[c]) for c in (1, 0)]

    def start(self):
        self.core = [
            self.net.push(self.at(c, 1), self.from_core.at[c], self.net.core) for c in (1, 0)
        ]

    def step(self):
        for i, c in enumerate((1, 0)):
            self.loads[i].wait()
            self.net.arrived(self.from_core.at[c], self.core[i])
            add_rows(self.acc.at[c], self.from_core.at[c])
            if c:
                self.x = self.net.push(self.acc.at[c], self.from_x, self.net.x)

    def end(self):
        self.net.arrived(self.from_x, self.x)

    def total(self, rows):
        return self.acc[0, rows, :].astype(F32) + self.from_x[rows, :].astype(F32)

    @staticmethod
    def scratch(rows, width):
        return [
            pltpu.VMEM((2, rows, width), BF16),
            pltpu.VMEM((2, rows, width), BF16),
            pltpu.VMEM((rows, width), BF16),
        ]


def sum_tensor_kernel(far, part, out, *scratch):
    net = Net(far, *scratch[-3:])
    rows_back = ReduceTensor(net, part, *scratch[:3])
    rows_back.load()
    net.greet([net.x, net.core])
    rows_back.start()
    rows_back.step()
    rows_back.end()

    @pl.loop(0, out.shape[0] // 16)
    def _(i):
        rows = pl.ds(pl.multiple_of(i * 16, 16), 16)
        out[rows, :] = rows_back.total(rows)

    net.finish()


def sum_tensor(part, groups, ident):
    _, m, width = part.shape
    return pl.pallas_call(
        functools.partial(sum_tensor_kernel, groups // 2),
        out_shape=jax.ShapeDtypeStruct((m, width), F32),
        in_specs=[ANY],
        out_specs=IN_VMEM,
        scratch_shapes=ReduceTensor.scratch(m, width) + semaphores(3, 2),
        compiler_params=params(ident, 16),
        cost_estimate=cost(16),
    )(part)


def gather_tensor_kernel(far, own, blocks, out, blocks_out, *scratch):
    net = Net(far, *scratch)
    give = GatherTensor(net, own, out)
    me = net.group()
    net.greet(net.line() + [net.x, net.core])
    give.start()
    mine = net.load(blocks.at[me], blocks_out.at[me])
    small = []
    for r in range(far):
        for b in range(2):
            if r or b:
                to = net.at(r, b)
                small.append((net.group(-r, b), net.push(blocks.at[to[0]], blocks_out.at[me], to)))
    give.step()
    give.end()
    for g, k in small:
        net.arrived(blocks_out.at[g], k)
    net.finish()
    mine.wait()


def gather_tensor(own, blocks, groups, tensors, ident):
    m, width = own.shape
    return pl.pallas_call(
        functools.partial(gather_tensor_kernel, groups // 2),
        out_shape=[
            jax.ShapeDtypeStruct((tensors, m, width), own.dtype),
            jax.ShapeDtypeStruct(blocks.shape, blocks.dtype),
        ],
        in_specs=[ANY] * 2,
        out_specs=[ANY] * 2,
        scratch_shapes=semaphores(2 + groups, 2),
        compiler_params=params(ident, 16),
        cost_estimate=cost(25),
    )(own, blocks)


def reduce_rows_kernel(far, part, out, *scratch):
    net = Net(far, *scratch[-3:])
    sums = ReduceAll(net, lambda s: part.at[s], *scratch[:5], "xy")
    sums.load()
    net.greet(net.near())
    sums.start()
    pipelined(far, [sums])
    sums.end()

    @pl.loop(0, out.shape[0] // 16)
    def _(i):
        rows = pl.ds(pl.multiple_of(i * 16, 16), 16)
        out[rows, :] = sums.total(rows)

    net.finish()


def reduce_rows(part, groups, ident):
    far = groups // 2
    return pl.pallas_call(
        functools.partial(reduce_rows_kernel, far),
        out_shape=jax.ShapeDtypeStruct(part.shape[1:], F32),
        in_specs=[ANY],
        out_specs=IN_VMEM,
        scratch_shapes=ReduceAll.scratch(far, *part.shape[1:]) + semaphores(12 * far, 4 * far),
        compiler_params=params(ident),
        cost_estimate=cost(90),
    )(part)


def cells(groups, tensors):
    across = 8 if groups * tensors <= 32 else 16
    return groups * tensors // across, across


def finish_kernel(far, *refs):
    (gq, gkv, gout, latent, misc, dxn, ffn, dresid, normed, scale, gain, resid, live) = refs[:13]
    (oq, okv, oout, osmall, otokens, ooutput) = refs[13:19]
    scratch = list(refs[19:])
    net = Net(far, *scratch[-3:])

    def take(n):
        got = scratch[:n]
        del scratch[:n]
        return got

    weights = [ReduceGroups(net, p, o, *take(3)) for p, o in ((gq, oq), (gkv, okv), (gout, oout))]
    down, across = cells(2 * far, 4)
    tall, wide = osmall.shape[0] // down, osmall.shape[1] // across
    tall_latent, tall_misc = latent.shape[0] // down, misc.shape[0] // down

    def cell(ref):
        def at(s):
            here = pl.ds(pl.multiple_of(s // across * tall, 16), tall)
            return ref.at[here, pl.ds(pl.multiple_of(s % across * wide, 128), wide)]

        return at

    summed = len(ffn.shape) == 2
    small, sum_own, tokens_own, output_own = scratch[-7:-3]
    sums = ReduceDirect(net, cell(small), *take(4), None, "xy")
    rows_back = ReduceTensor(net, dxn, *take(3))
    ffns = Summed(ffn) if summed else ReduceAll(net, lambda s: ffn.at[s], *take(5), "xy")
    give_output = GatherTensor(net, output_own, ooutput)
    every = GatherDirect(net, sum_own, cell(osmall))
    give_tokens = GatherTensor(net, tokens_own, otokens)
    moved = []
    for k in range(down):
        here = pl.ds(k * tall, tall_latent)
        moved.append(net.load(latent.at[pl.ds(k * tall_latent, tall_latent)], small.at[here]))
        here = pl.ds(k * tall + tall_latent, tall_misc)
        moved.append(net.load(misc.at[pl.ds(k * tall_misc, tall_misc)], small.at[here]))
    for part in (rows_back, *weights, ffns):
        part.load()
    mine = []
    net.greet(net.line() + [net.x, net.core])

    def send_weights(r):
        for part in weights:
            part.start(r)

    def step_weights(r):
        for part in weights:
            part.step(r)

    def each(count, body):
        @pl.loop(0, count // 16)
        def _(i):
            body(pl.ds(pl.multiple_of(i * 16, 16), 16))

    def tokens_rows(rows):
        n = normed[rows, :]
        weighted = rows_back.total(rows) * gain[...]
        mean = jnp.mean(weighted * n, axis=-1, keepdims=True)
        back = scale[rows, :] * (weighted - n * mean)
        tokens_own[rows, :] = (dresid[rows, :] + back).astype(BF16)

    def output_rows(rows):
        output_own[rows, :] = (resid[rows, :] + live[rows, :] * ffns.total(rows)).astype(BF16)

    def sum_rows(rows):
        sum_own[rows, :] = sums.total(rows).astype(BF16)

    turn = far_first(far)
    rows_back.start()
    for copy in moved:
        copy.wait()
    sums.load()
    sums.start()
    ffns.start()
    send_weights(turn[0])
    rows_back.step()
    for i in range(far):
        sums.stage_a(i)
    ffns.stage_a(0)
    for i in range(far):
        sums.stage_b(i)
    send_weights(turn[1])
    rows_back.end()
    each(tokens_own.shape[0], tokens_rows)
    give_tokens.start()
    ffns.stage_a(1)
    step_weights(turn[0])
    sums.end()
    each(sum_own.shape[0], sum_rows)
    mine.append(net.load(sum_own, cell(osmall)(net.slot())))
    every.start()
    every.stage_a(0)
    for k in range(far - 2):
        if k:
            step_weights(turn[k])
        send_weights(turn[k + 2])
        ffns.stage_b(k)
        ffns.stage_a(k + 2)
    give_tokens.step()
    for k in range(far - 2):
        ffns.stage_c(k)
    step_weights(turn[far - 2])
    for i in range(1, 2 * far):
        every.stage_a(i)
    ffns.stage_b(far - 2)
    step_weights(turn[far - 1])
    ffns.stage_c(far - 2)
    ffns.stage_b(far - 1)
    for i in range(2 * far):
        every.stage_b(i)
    ffns.stage_c(far - 1)
    ffns.end()
    each(output_own.shape[0], output_rows)
    give_output.start()
    for part in weights:
        part.end()
    give_output.step()
    for part in (give_tokens, every, give_output):
        part.end()
    net.finish()
    for copy in mine:
        copy.wait()


def finish(weights, latent, misc, dxn, ffn, rows, groups, tensors, ident):
    far = groups // 2
    m, width = rows[0].shape
    down, across = cells(groups, tensors)
    size = (latent.shape[0] + misc.shape[0], width)
    cell = (size[0] // down, width // across)
    outs = [jax.ShapeDtypeStruct(w.shape[1:], F32) for w in weights]
    outs.append(jax.ShapeDtypeStruct(size, BF16))
    outs += [jax.ShapeDtypeStruct((tensors, m, width), BF16)] * 2
    scratch = []
    for w in weights:
        scratch += ReduceGroups.scratch(far, *w.shape[1:])
    scratch += ReduceDirect.scratch(far, *cell)
    scratch += ReduceTensor.scratch(m, width)
    if len(ffn.shape) == 3:
        scratch += ReduceAll.scratch(far, *ffn.shape[1:])
    scratch += [pltpu.VMEM(size, BF16), pltpu.VMEM(cell, BF16)]
    scratch += [pltpu.VMEM((m, width), BF16)] * 2
    return pl.pallas_call(
        functools.partial(finish_kernel, far),
        out_shape=outs,
        in_specs=[ANY] * 6 + [ANY if len(ffn.shape) == 3 else IN_VMEM] + [IN_VMEM] * 6,
        out_specs=[IN_VMEM] * 3 + [ANY] * 3,
        scratch_shapes=scratch + semaphores(50 * far, 14 * far + 30),
        compiler_params=params(ident),
        cost_estimate=cost(110),
    )(*weights, latent, misc, dxn, ffn, *rows)


TILE = 32


def dot_nt(left, right):
    return lax.dot_general(left, right, (((1,), (1,)), ((), ())), preferred_element_type=F32)


def dot_nn(left, right):
    return lax.dot_general(left, right, (((1,), (0,)), ((), ())), preferred_element_type=F32)


def swap_halves(v):
    half = v.shape[1] // 2
    return jnp.concatenate([v[:, half:], v[:, :half]], axis=1)


def attend_kernel(
    heads,
    tokens, gain, w_query, w_latent, gain_lat, w_kv, w_out, cosine, sine,
    partial, xn1, qcat, kv, key_rope, probs, attended, normed_lat, scale_lat, compressed, scale_one,
    q_raw, latent,
):
    rows, width = tokens.shape
    blocks = w_out.shape[0]
    step = width // blocks

    @pl.loop(0, rows // 64)
    def _(i):
        at = pl.ds(pl.multiple_of(i * 64, 64), 64)
        v = tokens[at, :].astype(F32)
        scale = lax.rsqrt(jnp.mean(v * v, axis=-1, keepdims=True) + EPS)
        scale_one[at, :] = scale
        xn1[at, :] = (v * scale * gain[...]).astype(BF16)

    latent[...] = dot_nt(xn1[...], w_latent[...])
    q_raw[...] = dot_nn(xn1[...], w_query[...])

    @pl.loop(0, rows // 128)
    def _(i):
        at = pl.ds(pl.multiple_of(i * 128, 128), 128)
        v = latent[at, :KVR]
        scale = lax.rsqrt(jnp.mean(v * v, axis=-1, keepdims=True) + EPS)
        scale_lat[at, :] = scale
        normed = v * scale
        normed_lat[at, :] = normed
        compressed[at, :] = (normed * gain_lat[...]).astype(BF16)
        rope = latent[at, KVR:]
        c, s = cosine[at, :], sine[at, :]
        key_rope[at, :] = (rope * c + swap_halves(rope) * s).astype(BF16)
        for h in range(heads):
            base = h * (NOPE + ROPE)
            qcat[h, at, :NOPE] = q_raw[at, base : base + NOPE].astype(BF16)
            rope = q_raw[at, base + NOPE : base + NOPE + ROPE]
            qcat[h, at, NOPE:] = (rope * c + swap_halves(rope) * s).astype(BF16)

    kv[...] = dot_nn(compressed[...], w_kv[...]).astype(BF16)
    score_scale = (NOPE + ROPE) ** (-0.5)
    for h in range(heads):
        base = h * (NOPE + VD)

        @pl.loop(0, rows // 128)
        def _(i):
            at = pl.ds(pl.multiple_of(i * 128, 128), 128)
            score = dot_nt(qcat[h, at, :NOPE], kv[:, base : base + NOPE])
            score = (score + dot_nt(qcat[h, at, NOPE:], key_rope[...])) * score_scale
            mine = lax.broadcasted_iota(jnp.int32, score.shape, 0) + i * 128
            seen = lax.broadcasted_iota(jnp.int32, score.shape, 1) <= mine
            score = jnp.where(seen, score, -1e30)
            expo = jnp.exp(score - jnp.max(score, axis=-1, keepdims=True))
            prob = (expo / jnp.sum(expo, axis=-1, keepdims=True)).astype(BF16)
            probs[h, at, :] = prob
            out = dot_nn(prob, kv[:, base + NOPE : base + NOPE + VD])
            attended[at, h * VD : (h + 1) * VD] = out.astype(BF16)

    for e in range(blocks):
        partial[:, e * step : (e + 1) * step] = dot_nn(attended[...], w_out[e]).astype(BF16)


def attend(tokens, gain, w_query, w_latent, gain_lat, w_kv, w_out, cosine, sine):
    rows, width = tokens.shape
    heads = w_out.shape[1] // VD
    like = jax.ShapeDtypeStruct
    outs = [
        like((rows, width), BF16),
        like((rows, width), BF16),
        like((heads, rows, NOPE + ROPE), BF16),
        like((rows, w_kv.shape[1]), BF16),
        like((rows, ROPE), BF16),
        like((heads, rows, rows), BF16),
        like((rows, heads * VD), BF16),
        like((rows, KVR), F32),
        like((rows, 1), F32),
        like((rows, KVR), BF16),
        like((rows, 1), F32),
    ]
    return pl.pallas_call(
        functools.partial(attend_kernel, heads),
        out_shape=outs,
        in_specs=[IN_VMEM] * 9,
        out_specs=[IN_VMEM] * 11,
        scratch_shapes=[
            pltpu.VMEM((rows, w_query.shape[1]), F32),
            pltpu.VMEM((rows, w_latent.shape[0]), F32),
        ],
        compiler_params=pltpu.CompilerParams(vmem_limit_bytes=60 * 2**20),
        cost_estimate=cost(20),
    )(tokens, gain, w_query, w_latent, gain_lat, w_kv, w_out, cosine, sine)


def attend_back_kernel(
    heads,
    dattn, tokens, xn1, qcat, kv, key_rope, probs, attended, normed_lat, scale_lat, compressed, scale_one,
    w_query, w_latent, gain_lat, w_kv, w_out, cosine, sine,
    g_query, g_kv, g_out, g_latent, g_gain, g_gain_lat, dxn,
    dattended, dscore, dq, dkv, dkr, dlatent, turned, dcomp,
):
    rows, width = tokens.shape
    blocks = w_out.shape[0]
    step = width // blocks
    total = jnp.zeros((rows, heads * VD), F32)
    for e in range(blocks):
        total = total + dot_nt(dattn[:, e * step : (e + 1) * step], w_out[e])
    dattended[...] = total.astype(BF16)
    turned_att = attended[...].T
    for e in range(blocks):
        g_out[e] = dot_nn(turned_att, dattn[:, e * step : (e + 1) * step]).astype(BF16)
    score_scale = (NOPE + ROPE) ** (-0.5)
    for h in range(heads):
        base, qbase = h * (NOPE + VD), h * (NOPE + ROPE)

        @pl.loop(0, rows // 128)
        def _(i):
            at = pl.ds(pl.multiple_of(i * 128, 128), 128)
            dprob = dot_nt(dattended[at, h * VD : (h + 1) * VD], kv[:, base + NOPE : base + NOPE + VD])
            prob = probs[h, at, :].astype(F32)
            along = prob * dprob
            ds = (along - prob * jnp.sum(along, axis=-1, keepdims=True)) * score_scale
            dscore[at, :] = ds.astype(BF16)

        @pl.loop(0, rows // 128)
        def _(i):
            at = pl.ds(pl.multiple_of(i * 128, 128), 128)
            ds = dscore[at, :]
            dq[at, qbase : qbase + NOPE] = dot_nn(ds, kv[:, base : base + NOPE]).astype(BF16)
            rope = dot_nn(ds, key_rope[...])
            rope = rope * cosine[at, :] - swap_halves(rope) * sine[at, :]
            dq[at, qbase + NOPE : qbase + NOPE + ROPE] = rope.astype(BF16)

        turned_p = probs[h].T
        dv = dot_nn(turned_p, dattended[:, h * VD : (h + 1) * VD])
        dkv[:, base + NOPE : base + NOPE + VD] = dv.astype(BF16)
        turned_s = dscore[...].T
        dkv[:, base : base + NOPE] = dot_nn(turned_s, qcat[h, :, :NOPE]).astype(BF16)
        rope = dot_nn(turned_s, qcat[h, :, NOPE:])
        dkr[...] = rope if h == 0 else dkr[...] + rope

    turned_c = compressed[...].T
    g_kv[...] = dot_nn(turned_c, dkv[...]).astype(BF16)
    dcomp[...] = dot_nt(dkv[...], w_kv[...])
    dlatent[...] = jnp.zeros_like(dlatent)
    g_gain_lat[...] = jnp.zeros_like(g_gain_lat)

    @pl.loop(0, rows // 128)
    def _(i):
        at = pl.ds(pl.multiple_of(i * 128, 128), 128)
        d, n = dcomp[at, :], normed_lat[at, :]
        g_gain_lat[...] += jnp.sum(d * n, axis=0, keepdims=True)
        weighted = d * gain_lat[...]
        mean = jnp.mean(weighted * n, axis=-1, keepdims=True)
        dlatent[at, :KVR] = (scale_lat[at, :] * (weighted - n * mean)).astype(BF16)
        rope = dkr[at, :]
        rope = rope * cosine[at, :] - swap_halves(rope) * sine[at, :]
        dlatent[at, KVR : KVR + ROPE] = rope.astype(BF16)

    turned[...] = dlatent[...].T
    units = w_latent.shape[0]

    @pl.loop(0, width // 512)
    def _(c):
        at = pl.ds(pl.multiple_of(c * 512, 512), 512)
        g_query[at, :] = dot_nn(xn1[:, at].T, dq[...]).astype(BF16)
        g_latent[:, at] = dot_nn(turned[:units, :], xn1[:, at]).astype(BF16)
        d = dot_nt(dq[...], w_query[at, :]) + dot_nn(dlatent[:, :units], w_latent[:, at])
        dxn[:, at] = d.astype(BF16)
        normed = tokens[:, at].astype(F32) * scale_one[...]
        g_gain[:, at] = jnp.sum(d * normed, axis=0, keepdims=True)


def attend_back(dattn, tokens, kept, w_query, w_latent, gain_lat, w_kv, w_out, cosine, sine):
    rows, width = tokens.shape
    heads = w_out.shape[1] // VD
    like = jax.ShapeDtypeStruct
    units = w_latent.shape[0]
    padded = -(-units // 128) * 128
    outs = [
        like(w_query.shape, BF16),
        like(w_kv.shape, BF16),
        like(w_out.shape, BF16),
        like(w_latent.shape, BF16),
        like((1, width), F32),
        like((1, KVR), F32),
        like((rows, width), BF16),
    ]
    return pl.pallas_call(
        functools.partial(attend_back_kernel, heads),
        out_shape=outs,
        in_specs=[IN_VMEM] * 19,
        out_specs=[IN_VMEM] * 7,
        scratch_shapes=[
            pltpu.VMEM((rows, heads * VD), BF16),
            pltpu.VMEM((rows, rows), BF16),
            pltpu.VMEM((rows, w_query.shape[1]), BF16),
            pltpu.VMEM((rows, w_kv.shape[1]), BF16),
            pltpu.VMEM((rows, ROPE), F32),
            pltpu.VMEM((rows, padded), BF16),
            pltpu.VMEM((padded, rows), BF16),
            pltpu.VMEM((rows, KVR), F32),
        ],
        compiler_params=pltpu.CompilerParams(vmem_limit_bytes=62 * 2**20),
        cost_estimate=cost(40),
    )(dattn, tokens, *kept, w_query, w_latent, gain_lat, w_kv, w_out, cosine, sine)


def experts_kernel(sizes, *refs):
    far, experts, hidden, shared, total = sizes
    groups = 2 * far
    (x_own, dy_own, dy_near, picks, wg_hbm, wu_hbm, wd_hbm, ws_hbm, wr_hbm) = refs[:9]
    (outs_hbm, dg_out, gg_hbm, gu_hbm, gd_hbm, gs_hbm, x_all, dy_all, ffn_all) = refs[9:18]
    (core_in, x0_in, y1_in, y0_in, x1_in, z_in) = refs[18:24]
    (w_in, w_down, h, dh, hs, dgu, hsn, dgun, acc_in, acc_down, x, dy) = refs[24:36]
    (part, ffn_part, acc, own, stage1, stage2, stage3, stage4, dg, dg_in, dg_sum) = refs[36:47]
    (
        ag_s, ag_r, core_s, core_r, x0_s, x0_r, y1_s, y1_r, y0_s, y0_r, x1_s, x1_r, z_s, z_r,
        dg_s, dg_r, wsem, lsem, csem,
    ) = refs[47:]
    routed = experts * hidden
    units = routed + shared
    m, width = x_own.shape
    block, half = 4 * m, m // 2
    chunk = min(256, block)
    per = chunk // m
    low, high = pl.ds(0, half), pl.ds(half, half)
    net = Net(far, None, None, None)
    both, sums = range(2), range(1)

    def remote(src, dst, send, recv, to):
        return pltpu.make_async_remote_copy(
            src_ref=src, dst_ref=dst, send_sem=send, recv_sem=recv, device_id=to, device_id_type=MESH
        )

    def wait_for(ref, sem):
        pltpu.make_async_copy(ref, ref, sem).wait()

    links = ((net.y, net.x), (net.x, net.y))

    def place(q, r, u, v, d=0):
        p = q % 2
        b, c = (u, v) if p == 0 else (v, u)
        return (x_all, dy_all)[q // 2].at[net.slot(-r, b, c, d), (low, high)[p]]

    def pass_on(q, kind, r, u, v, to):
        ref = place(q, r, u, v)
        remote(ref, ref, ag_s.at[q, kind, r], ag_r.at[q, kind, r], to).start()

    def flows(r):
        return range(2 if isinstance(r, int) and r == 0 else 4)

    def rows_z(r):
        for q in range(4):
            ref = place(q, 0, 0, 0)
            src = ref if q < 2 else dy_own.at[net.at()[1], (low, high)[q % 2]]
            remote(src, ref, ag_s.at[q, 0, r], ag_r.at[q, 0, r], net.at(r)).start()

    def rows_a(r):
        for q in flows(r):
            if len(flows(r)) == 4:
                wait_for(place(q, r, 0, 0), ag_r.at[q, 0, r])
            pass_on(q, 1, r, 0, 0, links[q % 2][0])
            pass_on(q, 2, r, 0, 0, links[q % 2][1])
            pass_on(q, 4, r, 0, 0, net.core)

    def rows_b(r):
        for q in flows(r):
            wait_for(place(q, r, 1, 0), ag_r.at[q, 1, r])
            pass_on(q, 3, r, 1, 0, links[q % 2][1])
            pass_on(q, 6, r, 1, 0, net.core)

    def rows_c(r):
        for q in flows(r):
            for u in both:
                wait_for(place(q, r, u, 1), ag_r.at[q, 2 + u, r])
                pass_on(q, 5 + 2 * u, r, u, 1, net.core)

    def rows_d(r):
        for q in flows(r):
            for u in both:
                for v in both:
                    wait_for(place(q, r, u, v, 1), ag_r.at[q, 4 + 2 * u + v, r])

    def block_copies(s, dy_from):
        g = net.group(-(s // 2), 1 - s % 2)
        copies = []
        for t in range(4):
            here = pl.ds(t * m, m)
            copies.append(pltpu.make_async_copy(x_all.at[g * 4 + t], x.at[here], lsem.at[t]))
            source = dy_all.at[g * 4 + t] if dy_from is None else dy_from.at[t]
            copies.append(pltpu.make_async_copy(source, dy.at[here], lsem.at[4 + t]))
        return copies

    def load_block(s):
        pl.when(s == 1)(lambda: begin_all(block_copies(s, dy_own)))
        pl.when(s > 1)(lambda: begin_all(block_copies(s, None)))

    def mine(c, d):
        t = net.at(0, 0, c, d)[1]
        return pl.ds(pl.multiple_of(t * m, m), m)

    def ffn_copy(s):
        g = net.group(-(s // 2), 1 - s % 2)
        rows = pl.ds(pl.multiple_of(g * block, block), block)
        return pltpu.make_async_copy(ffn_part, ffn_all.at[rows], lsem.at[8])

    def core_push(s, a, c):
        return remote(
            part.at[a, mine(c, 1)], core_in.at[a, s, c], core_s.at[a, s, c], core_r.at[a, s, c], net.core
        )

    def x0_push(s, a):
        return remote(acc.at[a, s % 5, 1, low], x0_in.at[a, s], x0_s.at[a, s], x0_r.at[a, s], net.x)

    def y1_push(s, a, c):
        r = s // 2
        return remote(
            acc.at[a, s % 5, c, high], y1_in.at[a, r, c], y1_s.at[a, r, c], y1_r.at[a, r, c], net.y
        )

    def y0_push(s, a):
        r = s // 2
        return remote(acc.at[a, s % 5, 0, low], y0_in.at[a, r], y0_s.at[a, r], y0_r.at[a, r], net.y)

    def x1_push(s, a):
        r = s // 2
        return remote(acc.at[a, s % 5, 1, high], x1_in.at[a, r], x1_s.at[a, r], x1_r.at[a, r], net.x)

    def z_push(s, a):
        r = s // 2
        return remote(acc.at[a, s % 5, 0], z_in.at[a, r], z_s.at[a, r], z_r.at[a, r], net.at(-r))

    def copy_in(ref, buf, sem, k):
        return pltpu.make_async_copy(ref, buf, sem.at[k])

    def h1_loads(s):
        return [copy_in(core_in.at[a, s], stage1.at[a], csem, a) for a in sums]

    def h2_loads(s):
        return [copy_in(x0_in.at[a, s], stage2.at[a], csem, 2 + a) for a in sums]

    def h2_more(s):
        return [copy_in(y1_in.at[a, s // 2], stage3.at[a], csem, 4 + a) for a in sums]

    def h3_loads(s):
        return [copy_in(y0_in.at[a, s // 2], stage4.at[a, 0], csem, 6 + a) for a in sums] + [
            copy_in(x1_in.at[a, s // 2], stage4.at[a, 1], csem, 8 + a) for a in sums
        ]

    def begin_all(copies):
        for c in copies:
            c.start()

    def wait_all(copies):
        for c in copies:
            c.wait()

    def sends_done(s):
        for a in sums:
            x0_push(s, a).wait_send()

        @pl.when(s % 2 == 0)
        def _():
            for a in sums:
                for c in both:
                    y1_push(s, a, c).wait_send()
                y0_push(s, a).wait_send()

        @pl.when(s % 2 == 1)
        def _():
            for a in sums:
                x1_push(s, a).wait_send()
            pl.when(s > 1)(lambda: [z_push(s, a).wait_send() for a in sums] and None)

    def h1_pre(s):
        for a in sums:
            for c in both:
                wait_for(core_in.at[a, s, c], core_r.at[a, s, c])
        begin_all(h1_loads(s))

    def h1_post(s):
        wait_all(h1_loads(s))
        pl.when(s > 4)(lambda: sends_done(s - 5))
        for a in sums:
            for c in (1, 0):
                base = mine(c, 0).start

                @pl.loop(0, m // 16)
                def _(i):
                    rows = pl.ds(pl.multiple_of(i * 16, 16), 16)
                    there = pl.ds(pl.multiple_of(base + i * 16, 16), 16)
                    acc[a, s % 5, c, rows, :] = part[a, there, :] + stage1[a, c, rows, :]

            x0_push(s, a).start()

        @pl.when(s % 2 == 0)
        def _():
            for a in sums:
                for c in both:
                    y1_push(s, a, c).start()

    def add(a, s, c, base, buf):
        @pl.loop(0, half // 16)
        def _(i):
            rows = pl.ds(pl.multiple_of(base + i * 16, 16), 16)
            there = pl.ds(pl.multiple_of(i * 16, 16), 16)
            acc[a, s % 5, c, rows, :] = acc[a, s % 5, c, rows, :] + buf[there, :]

    def h2_pre(s):
        for a in sums:
            wait_for(x0_in.at[a, s], x0_r.at[a, s])
        begin_all(h2_loads(s))

        @pl.when(s % 2 == 1)
        def _():
            for a in sums:
                for c in both:
                    wait_for(y1_in.at[a, s // 2, c], y1_r.at[a, s // 2, c])
            begin_all(h2_more(s))

    def h2_post(s):
        wait_all(h2_loads(s))
        for a in sums:
            add(a, s, 0, 0, stage2.at[a])

        @pl.when(s % 2 == 0)
        def _():
            for a in sums:
                y0_push(s, a).start()

        @pl.when(s % 2 == 1)
        def _():
            wait_all(h2_more(s))
            for a in sums:
                for c in (1, 0):
                    add(a, s, c, half, stage3.at[a, c])
                x1_push(s, a).start()

    def h3_pre(s):
        for a in sums:
            wait_for(y0_in.at[a, s // 2], y0_r.at[a, s // 2])
            wait_for(x1_in.at[a, s // 2], x1_r.at[a, s // 2])
        begin_all(h3_loads(s))

    def h3_post(s):
        wait_all(h3_loads(s))
        for a in sums:
            for k in both:
                add(a, s, 0, k * half, stage4.at[a, k])

        @pl.when(s > 1)
        def _():
            for a in sums:
                z_push(s, a).start()

        @pl.when(s == 1)
        def _():
            for a in sums:
                own[a] = acc[a, 1, 0]

    def weights():
        pairs = []
        for e in range(experts):
            at = pl.ds(e * hidden, hidden)
            pairs.append((wg_hbm.at[e], w_in.at[at]))
            pairs.append((wu_hbm.at[e], w_in.at[pl.ds(units + e * hidden, hidden)]))
            pairs.append((wd_hbm.at[e], w_down.at[at]))
        pairs.append((ws_hbm.at[0], w_in.at[pl.ds(routed, shared)]))
        pairs.append((ws_hbm.at[1], w_in.at[pl.ds(units + routed, shared)]))
        pairs.append((ws_hbm.at[2], w_down.at[pl.ds(routed, shared)]))
        pairs.append((wr_hbm, w_in.at[pl.ds(2 * units, total)]))
        return [pltpu.make_async_copy(a, b, wsem.at[i]) for i, (a, b) in enumerate(pairs)]

    first = pltpu.make_async_copy(x_own, x_all.at[net.slot()], lsem.at[0])
    first.start()
    net.greet(net.line() + [net.at(c=c, d=d) for c, d in ((0, 1), (1, 0), (1, 1))])
    first.wait()
    rows_a(0)
    rows_z(1)
    begin_all(weights())
    acc_in[...] = jnp.zeros_like(acc_in)
    acc_down[...] = jnp.zeros_like(acc_down)
    dg[...] = jnp.zeros_like(dg)
    hs[units:, :] = jnp.zeros((hs.shape[0] - units, block), BF16)
    dgu[2 * units :, :] = jnp.zeros((dgu.shape[0] - 2 * units, block), BF16)
    rows_b(0)
    rows_c(0)
    rows_d(0)
    begin_all(block_copies(0, dy_near))
    wait_all(weights())

    last = groups - 1

    @pl.loop(0, groups)
    def _(s):
        r = s // 2
        g = net.group(-r, 1 - s % 2)
        more = r + 1 < far
        pl.when((s % 2 == 0) & more)(lambda: rows_a(r + 1))
        pl.when((s % 2 == 0) & (r + 2 < far))(lambda: rows_z(r + 2))
        pl.when(s > 0)(lambda: h1_pre(s - 1))
        pl.when(s > 2)(lambda: h2_pre(s - 3))
        wait_all(block_copies(s, None))

        @pl.loop(0, block // chunk)
        def _(n):
            at = pl.ds(pl.multiple_of(n * chunk, chunk), chunk)
            h[...] = dot_nt(w_in[...], x[at, :])
            dh[...] = dot_nt(w_down[...], dy[at, :])
            logits = h[2 * units :, :]
            expo = jnp.exp(logits - jnp.max(logits, axis=0, keepdims=True))
            marked = picks[:, pl.ds(pl.multiple_of(g * block + n * chunk, chunk), chunk)]
            gates = expo / jnp.sum(expo, axis=0, keepdims=True) * marked
            for e in range(experts + 1):
                base, count = (e * hidden, hidden) if e < experts else (routed, shared)
                gate = gates[e : e + 1, :] if e < experts else jnp.ones((1, chunk), F32)

                def body(i, total_):
                    a = pl.multiple_of(base + i * TILE, TILE)
                    here = pl.ds(a, TILE)
                    there = pl.ds(pl.multiple_of(units + a, TILE), TILE)
                    hg, hu, d = h[here, :], h[there, :], dh[here, :]
                    sig = 1.0 / (1.0 + jnp.exp(-hg))
                    act = hg * sig
                    dact = sig + act * (1.0 - sig)
                    hid = act * hu
                    hs[here, at] = (hid * gate).astype(BF16)
                    ds = d * gate
                    dgu[here, at] = (ds * hu * dact).astype(BF16)
                    dgu[there, at] = (ds * act).astype(BF16)
                    return total_ + jnp.sum(hid * d, axis=0, keepdims=True)

                row = lax.fori_loop(0, count // TILE, body, jnp.zeros((1, chunk), F32))
                if e < experts:
                    for j in range(per):
                        dg[n * per + j, g, e : e + 1, :] = row[:, j * m : (j + 1) * m]

        pl.when(s > 0)(lambda: h1_post(s - 1))
        pl.when(s > 2)(lambda: h2_post(s - 3))
        pl.when((s > 4) & (s % 2 == 0))(lambda: h3_pre(s - 5))
        pl.when(s == last)(lambda: h3_pre(last - 4))
        pl.when((s % 2 == 1) & more)(lambda: rows_c(r + 1))

        @pl.loop(0, width // 512)
        def _(c):
            at = pl.ds(pl.multiple_of(c * 512, 512), 512)
            acc_in[:, at] += dot_nn(dgu[: 2 * units, :], x[:, at])
            acc_down[:, at] += dot_nn(hs[:units, :], dy[:, at])

        pl.when((s > 4) & (s % 2 == 0))(lambda: h3_post(s - 5))

        @pl.when(s == last)
        def _():
            h3_post(last - 4)
            h2_pre(last - 2)

        pl.when((s % 2 == 1) & more)(lambda: rows_d(r + 1))
        pl.when(s + 1 < groups)(lambda: load_block(s + 1))
        hsn[...] = hs[...].T
        dgun[...] = dgu[...].T

        @pl.when(s > 0)
        def _():
            for c in both:
                core_push(s - 1, 0, c).wait_send()
            ffn_copy(s - 1).wait()

        @pl.loop(0, width // 512)
        def _(c):
            at = pl.ds(pl.multiple_of(c * 512, 512), 512)
            part[0, :, at] = dot_nn(dgun[:, : 2 * units], w_in[: 2 * units, at]).astype(BF16)

        for c in (1, 0):
            core_push(s, 0, c).start()

        @pl.loop(0, width // 512)
        def _(c):
            at = pl.ds(pl.multiple_of(c * 512, 512), 512)
            ffn_part[:, at] = dot_nn(hsn[:, :units], w_down[:, at]).astype(BF16)

        ffn_copy(s).start()
        pl.when(s == last)(lambda: h2_post(last - 2))
        pl.when((s % 2 == 0) & more)(lambda: rows_b(r + 1))

    def stores():
        pairs = []
        for e in range(experts):
            at = pl.ds(e * hidden, hidden)
            pairs.append((acc_in.at[at], gg_hbm.at[e]))
            pairs.append((acc_in.at[pl.ds(units + e * hidden, hidden)], gu_hbm.at[e]))
            pairs.append((acc_down.at[at], gd_hbm.at[e]))
        pairs.append((acc_in.at[pl.ds(routed, shared)], gs_hbm.at[0]))
        pairs.append((acc_in.at[pl.ds(units + routed, shared)], gs_hbm.at[1]))
        pairs.append((acc_down.at[pl.ds(routed, shared)], gs_hbm.at[2]))
        return [pltpu.make_async_copy(a, b, wsem.at[i]) for i, (a, b) in enumerate(pairs)]

    peers = [(c, d) for c in both for d in both][1:]

    def dg_push(k):
        c, d = peers[k]
        e, t = net.at(0, 0, c, d)
        return remote(dg.at[t], dg_in.at[k], dg_s.at[k], dg_r.at[k], (e, t))

    for k in range(3):
        dg_push(k).start()
    h2_pre(last - 1)
    h1_pre(last)
    h2_post(last - 1)
    h1_post(last)
    begin_all(stores())
    for a in sums:
        for c in both:
            wait_for(y1_in.at[a, last // 2, c], y1_r.at[a, last // 2, c])
    begin_all(h2_more(last))
    wait_all(h2_more(last))
    for a in sums:
        for c in (1, 0):
            add(a, last, c, half, stage3.at[a, c])
        x1_push(last, a).start()
    h3_pre(last - 2)
    h3_post(last - 2)
    for k in range(3):
        wait_for(dg_in.at[k], dg_r.at[k])
    dg_sum[...] = dg[net.at()[1]] + dg_in[0] + dg_in[1] + dg_in[2]
    me = net.group()
    dg_out[me] = dg_sum[me]
    others = [(r, b) for r in range(far) for b in both][1:]

    def dg_give(k):
        to = net.at(*others[k])
        return remote(dg_sum.at[to[0]], dg_out.at[me], dg_s.at[3 + k], dg_r.at[3 + k], to)

    for k in range(len(others)):
        dg_give(k).start()
    for a in sums:
        wait_for(x0_in.at[a, last], x0_r.at[a, last])
    begin_all(h2_loads(last))
    wait_all(h2_loads(last))
    for a in sums:
        add(a, last, 0, 0, stage2.at[a])
    h3_pre(last)
    h3_post(last)
    for r in range(1, far):
        for a in sums:
            wait_for(z_in.at[a, r], z_r.at[a, r])
            got = pltpu.make_async_copy(z_in.at[a, r], stage1.at[a, 0], csem.at[a])
            got.start()
            got.wait()

            @pl.loop(0, m // 16)
            def _(i):
                rows = pl.ds(pl.multiple_of(i * 16, 16), 16)
                own[a, rows, :] = own[a, rows, :] + stage1[a, 0, rows, :]

    give = pltpu.make_async_copy(own, outs_hbm, csem.at[0])
    give.start()
    for k in range(len(others)):
        r, b = others[k]
        wait_for(dg_out.at[net.group(-r, b)], dg_r.at[3 + k])
    for s in range(last - 4, last + 1):
        sends_done(s)
    for c in both:
        core_push(last, 0, c).wait_send()
    ffn_copy(last).wait()
    for q in range(4):
        for r in range(far):
            for kind in range(8):
                if r or (kind and q < 2):
                    wait_for(place(q, 0, 0, 0), ag_s.at[q, kind, r])
    for k in range(3):
        dg_push(k).wait_send()
    for k in range(len(others)):
        dg_give(k).wait_send()
    wait_all(stores())
    give.wait()


def experts_all(x, dy_own, dy_near, picks, wg, wu, wd, ws, wr, groups, tensors, ident):
    m, width = x.shape
    far = groups // 2
    experts, hidden, _ = wg.shape
    shared, total = ws.shape[1], wr.shape[0]
    units = experts * hidden + shared
    block, half = 4 * m, m // 2
    chunk = min(256, block)
    up = lambda v: -(-v // 128) * 128
    like = jax.ShapeDtypeStruct
    outs = [
        like((1, m, width), BF16),
        like((groups, 8, m), F32),
        like(wg.shape, F32),
        like(wu.shape, F32),
        like(wd.shape, F32),
        like(ws.shape, F32),
        like((groups * tensors, m, width), BF16),
        like((groups * tensors, m, width), BF16),
        like((groups * block, width), BF16),
        like((1, groups, 2, m, width), BF16),
        like((1, groups, half, width), BF16),
        like((1, far, 2, half, width), BF16),
        like((1, far, half, width), BF16),
        like((1, far, half, width), BF16),
        like((1, far, m, width), BF16),
    ]
    dma = pltpu.SemaphoreType.DMA
    scratch = [
        pltpu.VMEM((2 * units + total, width), BF16),
        pltpu.VMEM((units, width), BF16),
        pltpu.VMEM((2 * units + total, chunk), F32),
        pltpu.VMEM((units, chunk), F32),
        pltpu.VMEM((up(units), block), BF16),
        pltpu.VMEM((up(2 * units), block), BF16),
        pltpu.VMEM((block, up(units)), BF16),
        pltpu.VMEM((block, up(2 * units)), BF16),
        pltpu.VMEM((2 * units, width), F32),
        pltpu.VMEM((units, width), F32),
        pltpu.VMEM((block, width), BF16),
        pltpu.VMEM((block, width), BF16),
        pltpu.VMEM((1, block, width), BF16),
        pltpu.VMEM((block, width), BF16),
        pltpu.VMEM((1, 5, 2, m, width), BF16),
        pltpu.VMEM((1, m, width), BF16),
        pltpu.VMEM((1, 2, m, width), BF16),
        pltpu.VMEM((1, half, width), BF16),
        pltpu.VMEM((1, 2, half, width), BF16),
        pltpu.VMEM((1, 2, half, width), BF16),
        pltpu.VMEM((tensors, groups, 8, m), F32),
        pltpu.VMEM((3, groups, 8, m), F32),
        pltpu.VMEM((groups, 8, m), F32),
    ]
    for shape in (
        (4, 8, far), (1, groups, 2), (1, groups), (1, far, 2), (1, far), (1, far), (1, far), (groups + 2,),
    ):
        scratch += [dma(shape), dma(shape)]
    scratch += [dma((3 * experts + 4,)), dma((9,)), dma((10,))]
    got = pl.pallas_call(
        functools.partial(experts_kernel, (far, experts, hidden, shared, total)),
        out_shape=outs,
        in_specs=[ANY] * 3 + [IN_VMEM] + [ANY] * 5,
        out_specs=[ANY, IN_VMEM] + [ANY] * 13,
        scratch_shapes=scratch,
        compiler_params=params(ident, 63),
        cost_estimate=cost(280),
    )(x, dy_own, dy_near, picks, wg, wu, wd, ws, wr)
    return [*got[:6], got[8]]


BOTH = ("expert", "tensor")


def shards(
    tokens,
    lengths,
    routes,
    gain_attn,
    w_query,
    w_latent,
    gain_latent,
    w_kv,
    w_out,
    gain_ffn,
    w_router,
    w_shared_gate,
    w_shared_up,
    w_shared_down,
    w_gate,
    w_up,
    w_down,
    cotangent,
):
    groups = lax.axis_size("expert")
    tensors = lax.axis_size("tensor")
    eindex = lax.axis_index("expert")
    tindex = lax.axis_index("tensor")
    rows, width = tokens.shape
    quarter = rows // tensors
    experts_local, _, hidden_units = w_gate.shape
    total_experts = experts_local * groups
    every = groups * rows
    bf16, f32 = jnp.bfloat16, jnp.float32

    def own(v):
        return lax.dynamic_slice_in_dim(v, tindex * quarter, quarter, 0)

    live_int = (jnp.arange(rows) < lengths[0]).astype(jnp.int32)
    live = live_int.astype(f32)[:, None]
    live_own = own(live)
    cot_own = own(cotangent).astype(f32)
    dffn_group = (cotangent * live.astype(bf16)).reshape(tensors, quarter, width)
    dffn_own = own(cotangent) * live_own.astype(bf16)

    part = w_shared_down.shape[0] // groups
    spare = -part % TILE

    def shared_units(v):
        v = jnp.pad(v.reshape(groups, part, v.shape[1]), ((0, 0), (0, spare), (0, 0)))
        return v

    shared_w = jnp.stack(
        [shared_units(v) for v in (w_shared_gate.T, w_shared_up.T, w_shared_down)], axis=1
    )
    choose = jnp.any(routes[..., None] == jnp.arange(total_experts), axis=1).astype(F32)
    picks = choose * live
    query_w, kv_up, out_proj, shared_w, marks, dffn_near = begin(
        (w_query, w_kv, w_out),
        shared_w.reshape(groups, -1, shared_w.shape[-1]),
        picks.T.astype(BF16),
        dffn_own,
        groups,
        tensors,
        0,
    )
    query_w = query_w.reshape(width, -1)
    kv_up = kv_up.reshape(KVR, -1)
    shared_w = shared_w.transpose(1, 0, 2).reshape(3, part + spare, width)
    gate_t, up_t = w_gate.transpose(0, 2, 1), w_up.transpose(0, 2, 1)
    router_t = jnp.roll(w_router.T, -eindex * experts_local, axis=0)
    parts = max(1, every // 4096)
    some = quarter // parts

    def split(v):
        return v.reshape(parts, some, v.shape[1])

    marks = marks.reshape(groups, total_experts, tensors, parts, some).transpose(3, 1, 0, 2, 4)
    picks_all = marks.reshape(parts, total_experts, -1).astype(F32)
    picks_all = jnp.roll(picks_all, -eindex * experts_local, axis=1)
    xf = tokens.astype(f32)
    cosine, sine = rope_tables(rows, ROPE)
    cosine = jnp.concatenate([cosine, cosine], axis=1)
    sine = jnp.concatenate([-sine, sine], axis=1)
    attend_w = (query_w, w_latent.T, gain_latent[None], kv_up, out_proj, cosine, sine)
    partial, *kept = attend(tokens, gain_attn[None], *attend_w)
    scale_one = own(kept[-1])
    normed_one = own(xf) * scale_one
    partial = partial.reshape(tensors, quarter, width)
    attn = sum_tensor(partial, groups, parts + 2)
    resid = own(xf) + live_own * attn
    scale_two = inv_rms(resid)
    normed_two = resid * scale_two
    xn2_own = (normed_two * gain_ffn).astype(bf16)
    router = jax.nn.softmax(mat(xn2_own, w_router), axis=-1)
    outs = []
    for k in range(parts):
        dx, dgates, *grads, ffn = experts_all(
            split(xn2_own)[k],
            dffn_group[:, k * some : (k + 1) * some],
            dffn_near[:, k * some : (k + 1) * some],
            picks_all[k],
            gate_t,
            up_t,
            w_down,
            shared_w,
            router_t,
            groups,
            tensors,
            k + 1,
        )
        dx = dx[0].astype(F32)
        ffn = ffn.reshape(-1, some, width)
        if parts > 1:
            ffn = reduce_rows(ffn, groups, parts + 4 + k)
        dgates = dgates[:, :experts_local].reshape(total_experts, some).T
        outs.append((ffn, dx, dgates, *grads))
    dx, dgates = (jnp.concatenate(v, axis=0) for v in list(zip(*outs))[1:3])
    ffn = outs[0][0] if parts == 1 else jnp.concatenate([v[0] for v in outs], axis=0)
    grads = [functools.reduce(jnp.add, v) for v in list(zip(*outs))[3:]]
    drouter = own(picks) * dgates
    grad_gate, grad_up = (v.transpose(0, 2, 1) for v in grads[:2])
    grad_down = grads[2]
    dlogit = router * (drouter - jnp.sum(router * drouter, axis=-1, keepdims=True))
    grad_router = mat_tn(dlogit.astype(bf16), xn2_own)
    dnorm_two = dx + mat_nt(dlogit.astype(bf16), w_router)
    grad_gain_ffn = jnp.sum(dnorm_two * normed_two, axis=0)
    dresid = cot_own + norm_back(dnorm_two, normed_two, scale_two, gain_ffn)
    shared_g = grads[3].reshape(3, part + spare, groups, width // groups).astype(BF16)
    shared_g = shared_g.transpose(2, 0, 1, 3).reshape(groups, -1, width // groups)
    dattn, shared_g = gather_tensor((dresid * live_own).astype(bf16), shared_g, groups, tensors, parts + 3)
    dattn = dattn.reshape(rows, width)
    grad_query, grad_kv, grad_out, grad_latent, grad_gain_attn, grad_gain_latent, dnorm_one = (
        attend_back(dattn, tokens, kept, *attend_w)
    )
    down = cells(groups, tensors)[0]

    def whole_cells(v):
        return jnp.pad(v, ((0, -v.shape[0] % (16 * down)), (0, 0)))

    latent_g = whole_cells(grad_latent)
    misc = jnp.concatenate(
        [
            grad_router,
            grad_gain_attn,
            grad_gain_ffn[None],
            jnp.pad(grad_gain_latent, ((0, 0), (0, width - KVR))),
        ],
        axis=0,
    )
    misc = whole_cells(misc.astype(bf16))
    grad_query, grad_kv, grad_out, small, grad_tokens, output = finish(
        (
            grad_query.reshape(groups, -1, grad_query.shape[1]),
            grad_kv.reshape(groups, -1, grad_kv.shape[1]),
            grad_out,
        ),
        latent_g,
        misc,
        dnorm_one.reshape(tensors, quarter, width),
        ffn,
        (dresid, normed_one, scale_one, gain_attn[None], resid, live_own),
        groups,
        tensors,
        parts + 1,
    )
    grad_tokens = grad_tokens.reshape(rows, width)
    output = output.reshape(rows, width)
    small = small.reshape(down, -1, width)
    tall = latent_g.shape[0] // down
    grad_latent = small[:, :tall].reshape(-1, width)[: w_latent.shape[1]].astype(f32).T
    misc = small[:, tall:].reshape(-1, width).astype(f32)
    grad_router = misc[:total_experts].T
    grad_gain_attn = misc[total_experts]
    grad_gain_ffn = misc[total_experts + 1]
    grad_gain_latent = misc[total_experts + 2, :KVR]
    shared_g = shared_g.reshape(groups, 3, part + spare, -1)[:, :, :part].transpose(1, 0, 2, 3)
    shared_g = shared_g.reshape(3, groups * part, -1).astype(f32)
    grad_sgate, grad_sup, grad_sdown = shared_g[0].T, shared_g[1].T, shared_g[2]
    return (
        output,
        grad_tokens,
        grad_gain_attn,
        grad_query,
        grad_latent,
        grad_gain_latent,
        grad_kv,
        grad_out,
        grad_gain_ffn,
        grad_router,
        grad_sgate,
        grad_sup,
        grad_sdown,
        grad_gate,
        grad_up,
        grad_down,
    )


def solution(mesh):
    in_specs = (
        P("expert", None),
        P("expert"),
        P("expert", None),
        P(),
        P("expert", "tensor"),
        P(),
        P(),
        P("expert", "tensor"),
        P("tensor", "expert"),
        P(),
        P(),
        P("expert", "tensor"),
        P("expert", "tensor"),
        P("tensor", "expert"),
        P("expert", None, "tensor"),
        P("expert", None, "tensor"),
        P("expert", "tensor", None),
        P("expert", None),
    )
    out_specs = (
        P("expert", None),
        P("expert", None),
        P(),
        P("expert", "tensor"),
        P(),
        P(),
        P("expert", "tensor"),
        P("tensor", "expert"),
        P(),
        P(),
        P("expert", "tensor"),
        P("expert", "tensor"),
        P("tensor", "expert"),
        P("expert", None, "tensor"),
        P("expert", None, "tensor"),
        P("expert", "tensor", None),
    )
    return jax.shard_map(shards, mesh=mesh, in_specs=in_specs, out_specs=out_specs, check_vma=False)
```

```python
import functools

import jax
import jax.numpy as jnp
from jax import lax
from jax.experimental import pallas as pl
from jax.experimental.pallas import tpu as pltpu
from jax.sharding import PartitionSpec as P

F32, BF16 = jnp.float32, jnp.bfloat16

NOPE = 128
ROPE = 64
VD = 128
KVR = 512


EPS = 1e-06
ROPE_BASE = 10000.0


def inv_rms(v):
    return lax.rsqrt(jnp.mean(v * v, axis=-1, keepdims=True) + EPS)


def rope_tables(count, width):
    half = width // 2
    freq = ROPE_BASE ** (-(jnp.arange(half, dtype=jnp.float32) * 2.0 / width))
    angle = jnp.arange(count, dtype=jnp.float32)[:, None] * freq[None, :]
    return (jnp.cos(angle), jnp.sin(angle))


def rotate(v, cosine, sine):
    half = v.shape[-1] // 2
    first = v[..., :half]
    second = v[..., half:]
    return jnp.concatenate(
        [first * cosine - second * sine, second * cosine + first * sine], axis=-1
    )


def rotate_back(grad, cosine, sine):
    half = grad.shape[-1] // 2
    first = grad[..., :half]
    second = grad[..., half:]
    return jnp.concatenate(
        [first * cosine + second * sine, second * cosine - first * sine], axis=-1
    )


def norm_back(grad, normed, scale_row, gain):
    weighted = grad * gain
    return scale_row * (weighted - normed * jnp.mean(weighted * normed, axis=-1, keepdims=True))


def silu_parts(gate):
    sig = jax.nn.sigmoid(gate)
    return (gate * sig, sig * (1.0 + gate * (1.0 - sig)))


def mat(left, right):
    return jnp.dot(left, right, preferred_element_type=jnp.float32)


def mat_tn(left, right):
    return lax.dot_general(
        left, right, (((0,), (0,)), ((), ())), preferred_element_type=jnp.float32
    )


def mat_nt(left, right):
    return lax.dot_general(
        left, right, (((1,), (1,)), ((), ())), preferred_element_type=jnp.float32
    )


MESH = pl.DeviceIdType.MESH
ANY = pl.BlockSpec(memory_space=pl.ANY)
IN_VMEM = pl.BlockSpec(memory_space=pltpu.VMEM)


def places():
    e, t = lax.axis_index("expert"), lax.axis_index("tensor")
    return e // 2, e % 2, t // 2, t % 2


def far_first(far):
    return sorted(range(far), key=lambda r: -min(r, far - r))


class Net:
    def __init__(self, far, send, recv, local):
        self.far, self.send, self.recv, self.local = far, send, recv, local
        self.e1, self.e0, self.t1, self.t0 = places()
        self.count, self.started, self.locals = 0, [], 0
        self.core = self.at(d=1)
        self.x = self.at(c=1)
        self.y = self.at(b=1)

    def at(self, r=0, b=0, c=0, d=0):
        e = (self.e1 + r + self.far) % self.far * 2 + (self.e0 + b) % 2
        return (e, (self.t1 + c) % 2 * 2 + (self.t0 + d) % 2)

    def slot(self, r=0, b=0, c=0, d=0):
        e, t = self.at(r, b, c, d)
        return e * 4 + t

    def group(self, r=0, b=0):
        return self.at(r, b)[0]

    def greet(self, peers):
        barrier = pltpu.get_barrier_semaphore()
        for peer in peers:
            pl.semaphore_signal(barrier, inc=1, device_id=peer, device_id_type=MESH)
        pl.semaphore_wait(barrier, len(peers))

    def near(self):
        return [self.at(r) for r in range(1, self.far)] + [self.y, self.x, self.core]

    def line(self):
        every = [self.at(r, b) for r in range(self.far) for b in range(2)]
        return every[1:]

    def push(self, src, dst, to):
        k = self.count
        self.count += 1
        copy = pltpu.make_async_remote_copy(
            src_ref=src,
            dst_ref=dst,
            send_sem=self.send.at[k],
            recv_sem=self.recv.at[k],
            device_id=to,
            device_id_type=MESH,
        )
        copy.start()
        self.started.append(copy)
        return k

    def arrived(self, ref, k):
        pltpu.make_async_copy(ref, ref, self.recv.at[k]).wait()

    def load(self, src, dst):
        copy = pltpu.make_async_copy(src, dst, self.local.at[self.locals])
        self.locals += 1
        copy.start()
        return copy

    def finish(self):
        for copy in self.started:
            copy.wait_send()


def add_rows(dst, src, step=16):
    @pl.loop(0, dst.shape[0] // step)
    def _(i):
        rows = pl.ds(pl.multiple_of(i * step, step), step)
        dst[rows, :] = dst[rows, :] + src[rows, :]


class GatherAll:
    def __init__(self, net, own, out_at, order):
        self.net, self.own, self.out_at, self.order = net, own, out_at, order
        self.z, self.first, self.second, self.cores = {}, {}, {}, {}

    def place(self, r, u, v, d=0):
        b, c = (u, v) if self.order == "yx" else (v, u)
        return self.out_at(self.net.slot(-r, b, c, d))

    def pass_on(self, r, u, v, to):
        here = self.own if (r, u, v) == (0, 0, 0) else self.place(r, u, v)
        return self.net.push(here, self.place(r, u, v), to)

    def start(self):
        for r in range(1, self.net.far):
            self.z[r] = self.pass_on(0, 0, 0, self.net.at(r))
        self.links = (self.net.y, self.net.x)[:: 1 if self.order == "yx" else -1]

    def stage_a(self, r):
        if r:
            self.net.arrived(self.place(r, 0, 0), self.z[r])
        self.first[r] = self.pass_on(r, 0, 0, self.links[0])
        self.second[r, 0] = self.pass_on(r, 0, 0, self.links[1])
        self.cores[r, 0, 0] = self.pass_on(r, 0, 0, self.net.core)

    def stage_b(self, r):
        self.net.arrived(self.place(r, 1, 0), self.first[r])
        self.second[r, 1] = self.pass_on(r, 1, 0, self.links[1])
        self.cores[r, 1, 0] = self.pass_on(r, 1, 0, self.net.core)

    def stage_c(self, r):
        for u in range(2):
            self.net.arrived(self.place(r, u, 1), self.second[r, u])
            self.cores[r, u, 1] = self.pass_on(r, u, 1, self.net.core)

    def steps(self):
        return [self.stage_a, self.stage_b, self.stage_c]

    def end(self):
        for (r, u, v), k in self.cores.items():
            self.net.arrived(self.place(r, u, v, 1), k)


class ReduceAll:
    def __init__(self, net, part_at, acc, from_core, from_first, from_second, from_z, order):
        self.net, self.part_at, self.acc, self.order = net, part_at, acc, order
        self.bufs = (from_core, from_first, from_second, from_z)
        self.core, self.first, self.second, self.z, self.loads = {}, {}, {}, {}, {}
        self.turn = far_first(net.far)
        self.spots = ((1, 1), (0, 1), (1, 0), (0, 0))
        self.links = (net.x, net.y) if order == "xy" else (net.y, net.x)

    def dest(self, r, u, v, d):
        b, c = (v, u) if self.order == "xy" else (u, v)
        return self.part_at(self.net.slot(r, b, c, d))

    def load(self):
        for r in self.turn:
            for u, v in self.spots:
                k = r * 4 + u * 2 + v
                self.loads[k] = self.net.load(self.dest(r, u, v, 0), self.acc.at[k])

    def start(self):
        for r in self.turn:
            for u, v in self.spots:
                k = r * 4 + u * 2 + v
                self.core[k] = self.net.push(
                    self.dest(r, u, v, 1), self.bufs[0].at[k], self.net.core
                )

    def merge(self, k, buf, i, token):
        self.net.arrived(buf.at[i], token)
        add_rows(self.acc.at[k], buf.at[i])

    def stage_a(self, i):
        r = self.turn[i]
        for u, v in self.spots:
            k = r * 4 + u * 2 + v
            self.loads[k].wait()
            self.merge(k, self.bufs[0], k, self.core[k])
            if u:
                at = r * 2 + v
                self.first[at] = self.net.push(
                    self.acc.at[k], self.bufs[1].at[at], self.links[0]
                )

    def stage_b(self, i):
        r = self.turn[i]
        for v in (1, 0):
            at = r * 2 + v
            self.merge(r * 4 + v, self.bufs[1], at, self.first[at])
            if v:
                self.second[r] = self.net.push(
                    self.acc.at[r * 4 + v], self.bufs[2].at[r], self.links[1]
                )

    def stage_c(self, i):
        r = self.turn[i]
        self.merge(r * 4, self.bufs[2], r, self.second[r])
        if r:
            self.z[r] = self.net.push(
                self.acc.at[r * 4], self.bufs[3].at[r - 1], self.net.at(r)
            )

    def steps(self):
        return [self.stage_a, self.stage_b, self.stage_c]

    def end(self):
        for r in range(1, self.net.far):
            self.net.arrived(self.bufs[3].at[r - 1], self.z[r])

    def total(self, rows):
        total = self.acc[0, rows, :].astype(F32)
        for r in range(1, self.net.far):
            total = total + self.bufs[3][r - 1, rows, :].astype(F32)
        return total

    @staticmethod
    def scratch(far, rows, width):
        return [
            pltpu.VMEM((4 * far, rows, width), BF16),
            pltpu.VMEM((4 * far, rows, width), BF16),
            pltpu.VMEM((2 * far, rows, width), BF16),
            pltpu.VMEM((far, rows, width), BF16),
            pltpu.VMEM((far - 1, rows, width), BF16),
        ]


class ReduceDirect(ReduceAll):
    def stage_b(self, i):
        r = self.turn[i]
        for v in (1, 0):
            at = r * 2 + v
            self.merge(r * 4 + v, self.bufs[1], at, self.first[at])
            if at:
                self.z[at] = self.net.push(
                    self.acc.at[r * 4 + v], self.bufs[2].at[at], self.net.at(r, v)
                )

    def end(self):
        for at, k in self.z.items():
            self.net.arrived(self.bufs[2].at[at], k)

    def total(self, rows):
        total = self.acc[0, rows, :].astype(F32)
        for at in range(1, 2 * self.net.far):
            total = total + self.bufs[2][at, rows, :].astype(F32)
        return total

    @staticmethod
    def scratch(far, rows, width):
        return [
            pltpu.VMEM((4 * far, rows, width), BF16),
            pltpu.VMEM((4 * far, rows, width), BF16),
            pltpu.VMEM((2 * far, rows, width), BF16),
            pltpu.VMEM((2 * far, rows, width), BF16),
        ]


class GatherDirect:
    def __init__(self, net, own, out_at):
        self.net, self.own, self.out_at = net, own, out_at
        self.spots = [(r, b) for r in range(net.far) for b in range(2)]
        self.direct, self.x, self.cores = {}, {}, {}

    def place(self, r, b, c=0, d=0):
        return self.out_at(self.net.slot(-r, b, c, d))

    def start(self):
        for r, b in self.spots[1:]:
            self.direct[r, b] = self.net.push(self.own, self.place(0, 0), self.net.at(r, b))

    def stage_a(self, i):
        r, b = self.spots[i]
        here = self.place(r, b) if i else self.own
        if i:
            self.net.arrived(here, self.direct[r, b])
        self.x[r, b] = self.net.push(here, self.place(r, b), self.net.x)
        self.cores[r, b, 0] = self.net.push(here, self.place(r, b), self.net.core)

    def stage_b(self, i):
        r, b = self.spots[i]
        here = self.place(r, b, 1)
        self.net.arrived(here, self.x[r, b])
        self.cores[r, b, 1] = self.net.push(here, here, self.net.core)

    def end(self):
        for (r, b, c), k in self.cores.items():
            self.net.arrived(self.place(r, b, c, 1), k)


class Summed:
    def __init__(self, ref):
        self.ref = ref

    def load(self):
        pass

    start = end = load

    def stage_a(self, i):
        pass

    stage_b = stage_c = stage_a

    def total(self, rows):
        return self.ref[rows, :]


def pipelined(far, parts):
    for i in range(far + 2):
        for s in range(3):
            for part in parts:
                if 0 <= i - s < far:
                    part.steps()[s](i - s)


def semaphores(remote, local):
    return [
        pltpu.SemaphoreType.DMA((remote,)),
        pltpu.SemaphoreType.DMA((remote,)),
        pltpu.SemaphoreType.DMA((local,)),
    ]


def cost(us):
    return pl.CostEstimate(flops=0, bytes_accessed=us * 3_000_000, transcendentals=0)


def params(ident, mib=60):
    return pltpu.CompilerParams(
        collective_id=ident, has_side_effects=True, vmem_limit_bytes=mib * 2**20
    )


def begin_kernel(far, *refs):
    n = 3
    ws, blocks, marks, dy = refs[:n], refs[n], refs[n + 1], refs[n + 2]
    outs, blocks_out, marks_out, near = refs[n + 3 : 2 * n + 3], *refs[2 * n + 3 : 2 * n + 6]
    net = Net(far, *refs[2 * n + 6 :])
    me = net.group()
    mine = [net.load(w, o.at[me]) for w, o in zip(ws, outs)]
    mine.append(net.load(blocks.at[me], blocks_out.at[me]))
    mine.append(net.load(marks, marks_out.at[me]))
    net.greet(net.line() + [net.x, net.core])
    here = [near.at[net.at(0, 0, c, d)[1]] for c in range(2) for d in range(2)]
    dy_y = net.push(dy.at[net.at()[1]], here[0], net.y)
    tokens = {}
    others = [(r, b) for r in range(far) for b in range(2)][1:]
    for a, (w, o) in enumerate(zip(ws, outs)):
        for r in range(1, far):
            tokens[a, r] = net.push(w, o.at[me], net.at(r))
        tokens[a, 0, 1] = net.push(w, o.at[me], net.y)
    small = []
    for r, b in others:
        small.append((r, b, marks_out, net.push(marks, marks_out.at[me], net.at(r, b))))
    net.arrived(here[0], dy_y)
    dy_x = net.push(here[0], here[0], net.x)
    dy_core = net.push(here[0], here[0], net.core)
    for a, (w, o) in enumerate(zip(ws, outs)):
        for r in range(1, far):
            place = o.at[net.group(-r)]
            net.arrived(place, tokens[a, r])
            tokens[a, r, 1] = net.push(place, place, net.y)
    for r, b in others:
        to = net.at(r, b)
        small.append((r, b, blocks_out, net.push(blocks.at[to[0]], blocks_out.at[me], to)))
    net.arrived(here[2], dy_x)
    dy_both = net.push(here[2], here[2], net.core)
    for a, o in enumerate(outs):
        for r in range(far):
            net.arrived(o.at[net.group(-r, 1)], tokens[a, r, 1])
    net.arrived(here[1], dy_core)
    net.arrived(here[3], dy_both)
    for r, b, ref, k in small:
        net.arrived(ref.at[net.group(-r, b)], k)
    net.finish()
    for copy in mine:
        copy.wait()


def begin(ws, blocks, marks, dy, groups, tensors, ident):
    far = groups // 2
    outs = [jax.ShapeDtypeStruct((groups, *w.shape), w.dtype) for w in ws]
    outs.append(jax.ShapeDtypeStruct(blocks.shape, blocks.dtype))
    outs.append(jax.ShapeDtypeStruct((groups, *marks.shape), marks.dtype))
    outs.append(jax.ShapeDtypeStruct(dy.shape, dy.dtype))
    return pl.pallas_call(
        functools.partial(begin_kernel, far),
        out_shape=outs,
        in_specs=[ANY] * 6,
        out_specs=[ANY] * 6,
        scratch_shapes=semaphores(10 * far, 5),
        compiler_params=params(ident),
        cost_estimate=cost(100),
    )(*ws, blocks, marks, dy)


class ReduceGroups:
    def __init__(self, net, part, out, acc, from_y, from_z):
        self.net, self.part, self.out = net, part, out
        self.acc, self.from_y, self.from_z = acc, from_y, from_z
        self.turn = far_first(net.far)
        self.y, self.z = {}, {}

    def load(self):
        self.loads = {
            r: self.net.load(self.part.at[self.net.group(r)], self.acc.at[r]) for r in self.turn
        }

    def start(self, r):
        part = self.part.at[self.net.group(r, 1)]
        self.y[r] = self.net.push(part, self.from_y.at[r], self.net.y)

    def step(self, r):
        self.loads[r].wait()
        self.net.arrived(self.from_y.at[r], self.y[r])
        add_rows(self.acc.at[r], self.from_y.at[r])
        if r:
            self.z[r] = self.net.push(self.acc.at[r], self.from_z.at[r - 1], self.net.at(r))

    def end(self):
        for r in range(1, self.net.far):
            self.net.arrived(self.from_z.at[r - 1], self.z[r])

        @pl.loop(0, self.out.shape[0] // 16)
        def _(i):
            rows = pl.ds(pl.multiple_of(i * 16, 16), 16)
            total = self.acc[0, rows, :].astype(F32)
            for r in range(1, self.net.far):
                total = total + self.from_z[r - 1, rows, :].astype(F32)
            self.out[rows, :] = total

    @staticmethod
    def scratch(far, rows, width):
        return [
            pltpu.VMEM((far, rows, width), BF16),
            pltpu.VMEM((far, rows, width), BF16),
            pltpu.VMEM((far - 1, rows, width), BF16),
        ]


class GatherTensor:
    def __init__(self, net, own, out):
        self.net, self.own, self.out = net, own, out

    def place(self, c, d):
        return self.out.at[self.net.at(0, 0, c, d)[1]]

    def start(self):
        net = self.net
        self.mine = net.load(self.own, self.place(0, 0))
        self.x = net.push(self.own, self.place(0, 0), net.x)
        self.c0 = net.push(self.own, self.place(0, 0), net.core)

    def step(self):
        self.net.arrived(self.place(1, 0), self.x)
        self.c1 = self.net.push(self.place(1, 0), self.place(1, 0), self.net.core)

    def end(self):
        self.net.arrived(self.place(0, 1), self.c0)
        self.net.arrived(self.place(1, 1), self.c1)
        self.mine.wait()


class ReduceTensor:
    def __init__(self, net, part, acc, from_core, from_x):
        self.net, self.part = net, part
        self.acc, self.from_core, self.from_x = acc, from_core, from_x

    def at(self, c, d):
        return self.part.at[self.net.at(0, 0, c, d)[1]]

    def load(self):
        self.loads = [self.net.load(self.at(c, 0), self.acc.at[c]) for c in (1, 0)]

    def start(self):
        self.core = [
            self.net.push(self.at(c, 1), self.from_core.at[c], self.net.core) for c in (1, 0)
        ]

    def step(self):
        for i, c in enumerate((1, 0)):
            self.loads[i].wait()
            self.net.arrived(self.from_core.at[c], self.core[i])
            add_rows(self.acc.at[c], self.from_core.at[c])
            if c:
                self.x = self.net.push(self.acc.at[c], self.from_x, self.net.x)

    def end(self):
        self.net.arrived(self.from_x, self.x)

    def total(self, rows):
        return self.acc[0, rows, :].astype(F32) + self.from_x[rows, :].astype(F32)

    @staticmethod
    def scratch(rows, width):
        return [
            pltpu.VMEM((2, rows, width), BF16),
            pltpu.VMEM((2, rows, width), BF16),
            pltpu.VMEM((rows, width), BF16),
        ]


def sum_tensor_kernel(far, part, out, *scratch):
    net = Net(far, *scratch[-3:])
    rows_back = ReduceTensor(net, part, *scratch[:3])
    rows_back.load()
    net.greet([net.x, net.core])
    rows_back.start()
    rows_back.step()
    rows_back.end()

    @pl.loop(0, out.shape[0] // 16)
    def _(i):
        rows = pl.ds(pl.multiple_of(i * 16, 16), 16)
        out[rows, :] = rows_back.total(rows)

    net.finish()


def sum_tensor(part, groups, ident):
    _, m, width = part.shape
    return pl.pallas_call(
        functools.partial(sum_tensor_kernel, groups // 2),
        out_shape=jax.ShapeDtypeStruct((m, width), F32),
        in_specs=[ANY],
        out_specs=IN_VMEM,
        scratch_shapes=ReduceTensor.scratch(m, width) + semaphores(3, 2),
        compiler_params=params(ident, 16),
        cost_estimate=cost(16),
    )(part)


def gather_tensor_kernel(far, own, blocks, out, blocks_out, *scratch):
    net = Net(far, *scratch)
    give = GatherTensor(net, own, out)
    me = net.group()
    net.greet(net.line() + [net.x, net.core])
    give.start()
    mine = net.load(blocks.at[me], blocks_out.at[me])
    small = []
    for r in range(far):
        for b in range(2):
            if r or b:
                to = net.at(r, b)
                small.append((net.group(-r, b), net.push(blocks.at[to[0]], blocks_out.at[me], to)))
    give.step()
    give.end()
    for g, k in small:
        net.arrived(blocks_out.at[g], k)
    net.finish()
    mine.wait()


def gather_tensor(own, blocks, groups, tensors, ident):
    m, width = own.shape
    return pl.pallas_call(
        functools.partial(gather_tensor_kernel, groups // 2),
        out_shape=[
            jax.ShapeDtypeStruct((tensors, m, width), own.dtype),
            jax.ShapeDtypeStruct(blocks.shape, blocks.dtype),
        ],
        in_specs=[ANY] * 2,
        out_specs=[ANY] * 2,
        scratch_shapes=semaphores(2 + groups, 2),
        compiler_params=params(ident, 16),
        cost_estimate=cost(25),
    )(own, blocks)


def reduce_rows_kernel(far, part, out, *scratch):
    net = Net(far, *scratch[-3:])
    sums = ReduceAll(net, lambda s: part.at[s], *scratch[:5], "xy")
    sums.load()
    net.greet(net.near())
    sums.start()
    pipelined(far, [sums])
    sums.end()

    @pl.loop(0, out.shape[0] // 16)
    def _(i):
        rows = pl.ds(pl.multiple_of(i * 16, 16), 16)
        out[rows, :] = sums.total(rows)

    net.finish()


def reduce_rows(part, groups, ident):
    far = groups // 2
    return pl.pallas_call(
        functools.partial(reduce_rows_kernel, far),
        out_shape=jax.ShapeDtypeStruct(part.shape[1:], F32),
        in_specs=[ANY],
        out_specs=IN_VMEM,
        scratch_shapes=ReduceAll.scratch(far, *part.shape[1:]) + semaphores(12 * far, 4 * far),
        compiler_params=params(ident),
        cost_estimate=cost(90),
    )(part)


def cells(groups, tensors):
    across = 8 if groups * tensors <= 32 else 16
    return groups * tensors // across, across


def finish_kernel(far, *refs):
    (gq, gkv, gout, latent, misc, dxn, ffn, dresid, normed, scale, gain, resid, live) = refs[:13]
    (oq, okv, oout, osmall, otokens, ooutput) = refs[13:19]
    scratch = list(refs[19:])
    net = Net(far, *scratch[-3:])

    def take(n):
        got = scratch[:n]
        del scratch[:n]
        return got

    weights = [ReduceGroups(net, p, o, *take(3)) for p, o in ((gq, oq), (gkv, okv), (gout, oout))]
    down, across = cells(2 * far, 4)
    tall, wide = osmall.shape[0] // down, osmall.shape[1] // across
    tall_latent, tall_misc = latent.shape[0] // down, misc.shape[0] // down

    def cell(ref):
        def at(s):
            here = pl.ds(pl.multiple_of(s // across * tall, 16), tall)
            return ref.at[here, pl.ds(pl.multiple_of(s % across * wide, 128), wide)]

        return at

    summed = len(ffn.shape) == 2
    small, sum_own, tokens_own, output_own = scratch[-7:-3]
    sums = ReduceDirect(net, cell(small), *take(4), None, "xy")
    rows_back = ReduceTensor(net, dxn, *take(3))
    ffns = Summed(ffn) if summed else ReduceAll(net, lambda s: ffn.at[s], *take(5), "xy")
    give_output = GatherTensor(net, output_own, ooutput)
    every = GatherDirect(net, sum_own, cell(osmall))
    give_tokens = GatherTensor(net, tokens_own, otokens)
    moved = []
    for k in range(down):
        here = pl.ds(k * tall, tall_latent)
        moved.append(net.load(latent.at[pl.ds(k * tall_latent, tall_latent)], small.at[here]))
        here = pl.ds(k * tall + tall_latent, tall_misc)
        moved.append(net.load(misc.at[pl.ds(k * tall_misc, tall_misc)], small.at[here]))
    for part in (rows_back, *weights, ffns):
        part.load()
    mine = []
    net.greet(net.line() + [net.x, net.core])

    def send_weights(r):
        for part in weights:
            part.start(r)

    def step_weights(r):
        for part in weights:
            part.step(r)

    def each(count, body):
        @pl.loop(0, count // 16)
        def _(i):
            body(pl.ds(pl.multiple_of(i * 16, 16), 16))

    def tokens_rows(rows):
        n = normed[rows, :]
        weighted = rows_back.total(rows) * gain[...]
        mean = jnp.mean(weighted * n, axis=-1, keepdims=True)
        back = scale[rows, :] * (weighted - n * mean)
        tokens_own[rows, :] = (dresid[rows, :] + back).astype(BF16)

    def output_rows(rows):
        output_own[rows, :] = (resid[rows, :] + live[rows, :] * ffns.total(rows)).astype(BF16)

    def sum_rows(rows):
        sum_own[rows, :] = sums.total(rows).astype(BF16)

    turn = far_first(far)
    rows_back.start()
    for copy in moved:
        copy.wait()
    sums.load()
    sums.start()
    ffns.start()
    send_weights(turn[0])
    rows_back.step()
    for i in range(far):
        sums.stage_a(i)
    ffns.stage_a(0)
    for i in range(far):
        sums.stage_b(i)
    send_weights(turn[1])
    rows_back.end()
    each(tokens_own.shape[0], tokens_rows)
    give_tokens.start()
    ffns.stage_a(1)
    step_weights(turn[0])
    sums.end()
    each(sum_own.shape[0], sum_rows)
    mine.append(net.load(sum_own, cell(osmall)(net.slot())))
    every.start()
    every.stage_a(0)
    for k in range(far - 2):
        if k:
            step_weights(turn[k])
        send_weights(turn[k + 2])
        ffns.stage_b(k)
        ffns.stage_a(k + 2)
    give_tokens.step()
    for k in range(far - 2):
        ffns.stage_c(k)
    step_weights(turn[far - 2])
    for i in range(1, 2 * far):
        every.stage_a(i)
    ffns.stage_b(far - 2)
    step_weights(turn[far - 1])
    ffns.stage_c(far - 2)
    ffns.stage_b(far - 1)
    for i in range(2 * far):
        every.stage_b(i)
    ffns.stage_c(far - 1)
    ffns.end()
    each(output_own.shape[0], output_rows)
    give_output.start()
    for part in weights:
        part.end()
    give_output.step()
    for part in (give_tokens, every, give_output):
        part.end()
    net.finish()
    for copy in mine:
        copy.wait()


def finish(weights, latent, misc, dxn, ffn, rows, groups, tensors, ident):
    far = groups // 2
    m, width = rows[0].shape
    down, across = cells(groups, tensors)
    size = (latent.shape[0] + misc.shape[0], width)
    cell = (size[0] // down, width // across)
    outs = [jax.ShapeDtypeStruct(w.shape[1:], F32) for w in weights]
    outs.append(jax.ShapeDtypeStruct(size, BF16))
    outs += [jax.ShapeDtypeStruct((tensors, m, width), BF16)] * 2
    scratch = []
    for w in weights:
        scratch += ReduceGroups.scratch(far, *w.shape[1:])
    scratch += ReduceDirect.scratch(far, *cell)
    scratch += ReduceTensor.scratch(m, width)
    if len(ffn.shape) == 3:
        scratch += ReduceAll.scratch(far, *ffn.shape[1:])
    scratch += [pltpu.VMEM(size, BF16), pltpu.VMEM(cell, BF16)]
    scratch += [pltpu.VMEM((m, width), BF16)] * 2
    return pl.pallas_call(
        functools.partial(finish_kernel, far),
        out_shape=outs,
        in_specs=[ANY] * 6 + [ANY if len(ffn.shape) == 3 else IN_VMEM] + [IN_VMEM] * 6,
        out_specs=[IN_VMEM] * 3 + [ANY] * 3,
        scratch_shapes=scratch + semaphores(50 * far, 14 * far + 30),
        compiler_params=params(ident),
        cost_estimate=cost(110),
    )(*weights, latent, misc, dxn, ffn, *rows)


TILE = 32


def dot_nt(left, right):
    return lax.dot_general(left, right, (((1,), (1,)), ((), ())), preferred_element_type=F32)


def dot_nn(left, right):
    return lax.dot_general(left, right, (((1,), (0,)), ((), ())), preferred_element_type=F32)


def swap_halves(v):
    half = v.shape[1] // 2
    return jnp.concatenate([v[:, half:], v[:, :half]], axis=1)


def attend_kernel(
    heads,
    tokens, gain, w_query, w_latent, gain_lat, w_kv, w_out, cosine, sine,
    partial, xn1, qcat, kv, key_rope, probs, attended, normed_lat, scale_lat, compressed, scale_one,
    q_raw, latent,
):
    rows, width = tokens.shape
    blocks = w_out.shape[0]
    step = width // blocks

    @pl.loop(0, rows // 64)
    def _(i):
        at = pl.ds(pl.multiple_of(i * 64, 64), 64)
        v = tokens[at, :].astype(F32)
        scale = lax.rsqrt(jnp.mean(v * v, axis=-1, keepdims=True) + EPS)
        scale_one[at, :] = scale
        xn1[at, :] = (v * scale * gain[...]).astype(BF16)

    latent[...] = dot_nt(xn1[...], w_latent[...])
    q_raw[...] = dot_nn(xn1[...], w_query[...])

    @pl.loop(0, rows // 128)
    def _(i):
        at = pl.ds(pl.multiple_of(i * 128, 128), 128)
        v = latent[at, :KVR]
        scale = lax.rsqrt(jnp.mean(v * v, axis=-1, keepdims=True) + EPS)
        scale_lat[at, :] = scale
        normed = v * scale
        normed_lat[at, :] = normed
        compressed[at, :] = (normed * gain_lat[...]).astype(BF16)
        rope = latent[at, KVR:]
        c, s = cosine[at, :], sine[at, :]
        key_rope[at, :] = (rope * c + swap_halves(rope) * s).astype(BF16)
        for h in range(heads):
            base = h * (NOPE + ROPE)
            qcat[h, at, :NOPE] = q_raw[at, base : base + NOPE].astype(BF16)
            rope = q_raw[at, base + NOPE : base + NOPE + ROPE]
            qcat[h, at, NOPE:] = (rope * c + swap_halves(rope) * s).astype(BF16)

    kv[...] = dot_nn(compressed[...], w_kv[...]).astype(BF16)
    score_scale = (NOPE + ROPE) ** (-0.5)
    for h in range(heads):
        base = h * (NOPE + VD)

        @pl.loop(0, rows // 128)
        def _(i):
            at = pl.ds(pl.multiple_of(i * 128, 128), 128)
            score = dot_nt(qcat[h, at, :NOPE], kv[:, base : base + NOPE])
            score = (score + dot_nt(qcat[h, at, NOPE:], key_rope[...])) * score_scale
            mine = lax.broadcasted_iota(jnp.int32, score.shape, 0) + i * 128
            seen = lax.broadcasted_iota(jnp.int32, score.shape, 1) <= mine
            score = jnp.where(seen, score, -1e30)
            expo = jnp.exp(score - jnp.max(score, axis=-1, keepdims=True))
            prob = (expo / jnp.sum(expo, axis=-1, keepdims=True)).astype(BF16)
            probs[h, at, :] = prob
            out = dot_nn(prob, kv[:, base + NOPE : base + NOPE + VD])
            attended[at, h * VD : (h + 1) * VD] = out.astype(BF16)

    for e in range(blocks):
        partial[:, e * step : (e + 1) * step] = dot_nn(attended[...], w_out[e]).astype(BF16)


def attend(tokens, gain, w_query, w_latent, gain_lat, w_kv, w_out, cosine, sine):
    rows, width = tokens.shape
    heads = w_out.shape[1] // VD
    like = jax.ShapeDtypeStruct
    outs = [
        like((rows, width), BF16),
        like((rows, width), BF16),
        like((heads, rows, NOPE + ROPE), BF16),
        like((rows, w_kv.shape[1]), BF16),
        like((rows, ROPE), BF16),
        like((heads, rows, rows), BF16),
        like((rows, heads * VD), BF16),
        like((rows, KVR), F32),
        like((rows, 1), F32),
        like((rows, KVR), BF16),
        like((rows, 1), F32),
    ]
    return pl.pallas_call(
        functools.partial(attend_kernel, heads),
        out_shape=outs,
        in_specs=[IN_VMEM] * 9,
        out_specs=[IN_VMEM] * 11,
        scratch_shapes=[
            pltpu.VMEM((rows, w_query.shape[1]), F32),
            pltpu.VMEM((rows, w_latent.shape[0]), F32),
        ],
        compiler_params=pltpu.CompilerParams(vmem_limit_bytes=60 * 2**20),
        cost_estimate=cost(20),
    )(tokens, gain, w_query, w_latent, gain_lat, w_kv, w_out, cosine, sine)


def attend_back_kernel(
    heads,
    dattn, tokens, xn1, qcat, kv, key_rope, probs, attended, normed_lat, scale_lat, compressed, scale_one,
    w_query, w_latent, gain_lat, w_kv, w_out, cosine, sine,
    g_query, g_kv, g_out, g_latent, g_gain, g_gain_lat, dxn,
    dattended, dscore, dq, dkv, dkr, dlatent, turned, dcomp,
):
    rows, width = tokens.shape
    blocks = w_out.shape[0]
    step = width // blocks
    total = jnp.zeros((rows, heads * VD), F32)
    for e in range(blocks):
        total = total + dot_nt(dattn[:, e * step : (e + 1) * step], w_out[e])
    dattended[...] = total.astype(BF16)
    turned_att = attended[...].T
    for e in range(blocks):
        g_out[e] = dot_nn(turned_att, dattn[:, e * step : (e + 1) * step]).astype(BF16)
    score_scale = (NOPE + ROPE) ** (-0.5)
    for h in range(heads):
        base, qbase = h * (NOPE + VD), h * (NOPE + ROPE)

        @pl.loop(0, rows // 128)
        def _(i):
            at = pl.ds(pl.multiple_of(i * 128, 128), 128)
            dprob = dot_nt(dattended[at, h * VD : (h + 1) * VD], kv[:, base + NOPE : base + NOPE + VD])
            prob = probs[h, at, :].astype(F32)
            along = prob * dprob
            ds = (along - prob * jnp.sum(along, axis=-1, keepdims=True)) * score_scale
            dscore[at, :] = ds.astype(BF16)

        @pl.loop(0, rows // 128)
        def _(i):
            at = pl.ds(pl.multiple_of(i * 128, 128), 128)
            ds = dscore[at, :]
            dq[at, qbase : qbase + NOPE] = dot_nn(ds, kv[:, base : base + NOPE]).astype(BF16)
            rope = dot_nn(ds, key_rope[...])
            rope = rope * cosine[at, :] - swap_halves(rope) * sine[at, :]
            dq[at, qbase + NOPE : qbase + NOPE + ROPE] = rope.astype(BF16)

        turned_p = probs[h].T
        dv = dot_nn(turned_p, dattended[:, h * VD : (h + 1) * VD])
        dkv[:, base + NOPE : base + NOPE + VD] = dv.astype(BF16)
        turned_s = dscore[...].T
        dkv[:, base : base + NOPE] = dot_nn(turned_s, qcat[h, :, :NOPE]).astype(BF16)
        rope = dot_nn(turned_s, qcat[h, :, NOPE:])
        dkr[...] = rope if h == 0 else dkr[...] + rope

    turned_c = compressed[...].T
    g_kv[...] = dot_nn(turned_c, dkv[...]).astype(BF16)
    dcomp[...] = dot_nt(dkv[...], w_kv[...])
    dlatent[...] = jnp.zeros_like(dlatent)
    g_gain_lat[...] = jnp.zeros_like(g_gain_lat)

    @pl.loop(0, rows // 128)
    def _(i):
        at = pl.ds(pl.multiple_of(i * 128, 128), 128)
        d, n = dcomp[at, :], normed_lat[at, :]
        g_gain_lat[...] += jnp.sum(d * n, axis=0, keepdims=True)
        weighted = d * gain_lat[...]
        mean = jnp.mean(weighted * n, axis=-1, keepdims=True)
        dlatent[at, :KVR] = (scale_lat[at, :] * (weighted - n * mean)).astype(BF16)
        rope = dkr[at, :]
        rope = rope * cosine[at, :] - swap_halves(rope) * sine[at, :]
        dlatent[at, KVR : KVR + ROPE] = rope.astype(BF16)

    turned[...] = dlatent[...].T
    units = w_latent.shape[0]

    @pl.loop(0, width // 512)
    def _(c):
        at = pl.ds(pl.multiple_of(c * 512, 512), 512)
        g_query[at, :] = dot_nn(xn1[:, at].T, dq[...]).astype(BF16)
        g_latent[:, at] = dot_nn(turned[:units, :], xn1[:, at]).astype(BF16)
        d = dot_nt(dq[...], w_query[at, :]) + dot_nn(dlatent[:, :units], w_latent[:, at])
        dxn[:, at] = d.astype(BF16)
        normed = tokens[:, at].astype(F32) * scale_one[...]
        g_gain[:, at] = jnp.sum(d * normed, axis=0, keepdims=True)


def attend_back(dattn, tokens, kept, w_query, w_latent, gain_lat, w_kv, w_out, cosine, sine):
    rows, width = tokens.shape
    heads = w_out.shape[1] // VD
    like = jax.ShapeDtypeStruct
    units = w_latent.shape[0]
    padded = -(-units // 128) * 128
    outs = [
        like(w_query.shape, BF16),
        like(w_kv.shape, BF16),
        like(w_out.shape, BF16),
        like(w_latent.shape, BF16),
        like((1, width), F32),
        like((1, KVR), F32),
        like((rows, width), BF16),
    ]
    return pl.pallas_call(
        functools.partial(attend_back_kernel, heads),
        out_shape=outs,
        in_specs=[IN_VMEM] * 19,
        out_specs=[IN_VMEM] * 7,
        scratch_shapes=[
            pltpu.VMEM((rows, heads * VD), BF16),
            pltpu.VMEM((rows, rows), BF16),
            pltpu.VMEM((rows, w_query.shape[1]), BF16),
            pltpu.VMEM((rows, w_kv.shape[1]), BF16),
            pltpu.VMEM((rows, ROPE), F32),
            pltpu.VMEM((rows, padded), BF16),
            pltpu.VMEM((padded, rows), BF16),
            pltpu.VMEM((rows, KVR), F32),
        ],
        compiler_params=pltpu.CompilerParams(vmem_limit_bytes=62 * 2**20),
        cost_estimate=cost(40),
    )(dattn, tokens, *kept, w_query, w_latent, gain_lat, w_kv, w_out, cosine, sine)


def experts_kernel(sizes, *refs):
    far, experts, hidden, shared, total = sizes
    groups = 2 * far
    (x_own, dy_own, dy_near, picks, wg_hbm, wu_hbm, wd_hbm, ws_hbm, wr_hbm) = refs[:9]
    (outs_hbm, dg_out, gg_hbm, gu_hbm, gd_hbm, gs_hbm, x_all, dy_all, ffn_all) = refs[9:18]
    (core_in, x0_in, y1_in, y0_in, x1_in, z_in) = refs[18:24]
    (w_in, w_down, h, dh, hs, dgu, hsn, dgun, acc_in, acc_down, x, dy) = refs[24:36]
    (part, ffn_part, acc, own, stage1, stage2, stage3, stage4, dg, dg_in, dg_sum) = refs[36:47]
    (
        ag_s, ag_r, core_s, core_r, x0_s, x0_r, y1_s, y1_r, y0_s, y0_r, x1_s, x1_r, z_s, z_r,
        dg_s, dg_r, wsem, lsem, csem,
    ) = refs[47:]
    routed = experts * hidden
    units = routed + shared
    m, width = x_own.shape
    block, half = 4 * m, m // 2
    chunk = min(256, block)
    per = chunk // m
    low, high = pl.ds(0, half), pl.ds(half, half)
    net = Net(far, None, None, None)
    both, sums = range(2), range(1)

    def remote(src, dst, send, recv, to):
        return pltpu.make_async_remote_copy(
            src_ref=src, dst_ref=dst, send_sem=send, recv_sem=recv, device_id=to, device_id_type=MESH
        )

    def wait_for(ref, sem):
        pltpu.make_async_copy(ref, ref, sem).wait()

    links = ((net.y, net.x), (net.x, net.y))

    def place(q, r, u, v, d=0):
        p = q % 2
        b, c = (u, v) if p == 0 else (v, u)
        return (x_all, dy_all)[q // 2].at[net.slot(-r, b, c, d), (low, high)[p]]

    def pass_on(q, kind, r, u, v, to):
        ref = place(q, r, u, v)
        remote(ref, ref, ag_s.at[q, kind, r], ag_r.at[q, kind, r], to).start()

    def flows(r):
        return range(2 if isinstance(r, int) and r == 0 else 4)

    def rows_z(r):
        for q in range(4):
            ref = place(q, 0, 0, 0)
            src = ref if q < 2 else dy_own.at[net.at()[1], (low, high)[q % 2]]
            remote(src, ref, ag_s.at[q, 0, r], ag_r.at[q, 0, r], net.at(r)).start()

    def rows_a(r):
        for q in flows(r):
            if len(flows(r)) == 4:
                wait_for(place(q, r, 0, 0), ag_r.at[q, 0, r])
            pass_on(q, 1, r, 0, 0, links[q % 2][0])
            pass_on(q, 2, r, 0, 0, links[q % 2][1])
            pass_on(q, 4, r, 0, 0, net.core)

    def rows_b(r):
        for q in flows(r):
            wait_for(place(q, r, 1, 0), ag_r.at[q, 1, r])
            pass_on(q, 3, r, 1, 0, links[q % 2][1])
            pass_on(q, 6, r, 1, 0, net.core)

    def rows_c(r):
        for q in flows(r):
            for u in both:
                wait_for(place(q, r, u, 1), ag_r.at[q, 2 + u, r])
                pass_on(q, 5 + 2 * u, r, u, 1, net.core)

    def rows_d(r):
        for q in flows(r):
            for u in both:
                for v in both:
                    wait_for(place(q, r, u, v, 1), ag_r.at[q, 4 + 2 * u + v, r])

    def block_copies(s, dy_from):
        g = net.group(-(s // 2), 1 - s % 2)
        copies = []
        for t in range(4):
            here = pl.ds(t * m, m)
            copies.append(pltpu.make_async_copy(x_all.at[g * 4 + t], x.at[here], lsem.at[t]))
            source = dy_all.at[g * 4 + t] if dy_from is None else dy_from.at[t]
            copies.append(pltpu.make_async_copy(source, dy.at[here], lsem.at[4 + t]))
        return copies

    def load_block(s):
        pl.when(s == 1)(lambda: begin_all(block_copies(s, dy_own)))
        pl.when(s > 1)(lambda: begin_all(block_copies(s, None)))

    def mine(c, d):
        t = net.at(0, 0, c, d)[1]
        return pl.ds(pl.multiple_of(t * m, m), m)

    def ffn_copy(s):
        g = net.group(-(s // 2), 1 - s % 2)
        rows = pl.ds(pl.multiple_of(g * block, block), block)
        return pltpu.make_async_copy(ffn_part, ffn_all.at[rows], lsem.at[8])

    def core_push(s, a, c):
        return remote(
            part.at[a, mine(c, 1)], core_in.at[a, s, c], core_s.at[a, s, c], core_r.at[a, s, c], net.core
        )

    def x0_push(s, a):
        return remote(acc.at[a, s % 5, 1, low], x0_in.at[a, s], x0_s.at[a, s], x0_r.at[a, s], net.x)

    def y1_push(s, a, c):
        r = s // 2
        return remote(
            acc.at[a, s % 5, c, high], y1_in.at[a, r, c], y1_s.at[a, r, c], y1_r.at[a, r, c], net.y
        )

    def y0_push(s, a):
        r = s // 2
        return remote(acc.at[a, s % 5, 0, low], y0_in.at[a, r], y0_s.at[a, r], y0_r.at[a, r], net.y)

    def x1_push(s, a):
        r = s // 2
        return remote(acc.at[a, s % 5, 1, high], x1_in.at[a, r], x1_s.at[a, r], x1_r.at[a, r], net.x)

    def z_push(s, a):
        r = s // 2
        return remote(acc.at[a, s % 5, 0], z_in.at[a, r], z_s.at[a, r], z_r.at[a, r], net.at(-r))

    def copy_in(ref, buf, sem, k):
        return pltpu.make_async_copy(ref, buf, sem.at[k])

    def h1_loads(s):
        return [copy_in(core_in.at[a, s], stage1.at[a], csem, a) for a in sums]

    def h2_loads(s):
        return [copy_in(x0_in.at[a, s], stage2.at[a], csem, 2 + a) for a in sums]

    def h2_more(s):
        return [copy_in(y1_in.at[a, s // 2], stage3.at[a], csem, 4 + a) for a in sums]

    def h3_loads(s):
        return [copy_in(y0_in.at[a, s // 2], stage4.at[a, 0], csem, 6 + a) for a in sums] + [
            copy_in(x1_in.at[a, s // 2], stage4.at[a, 1], csem, 8 + a) for a in sums
        ]

    def begin_all(copies):
        for c in copies:
            c.start()

    def wait_all(copies):
        for c in copies:
            c.wait()

    def sends_done(s):
        for a in sums:
            x0_push(s, a).wait_send()

        @pl.when(s % 2 == 0)
        def _():
            for a in sums:
                for c in both:
                    y1_push(s, a, c).wait_send()
                y0_push(s, a).wait_send()

        @pl.when(s % 2 == 1)
        def _():
            for a in sums:
                x1_push(s, a).wait_send()
            pl.when(s > 1)(lambda: [z_push(s, a).wait_send() for a in sums] and None)

    def h1_pre(s):
        for a in sums:
            for c in both:
                wait_for(core_in.at[a, s, c], core_r.at[a, s, c])
        begin_all(h1_loads(s))

    def h1_post(s):
        wait_all(h1_loads(s))
        pl.when(s > 4)(lambda: sends_done(s - 5))
        for a in sums:
            for c in (1, 0):
                base = mine(c, 0).start

                @pl.loop(0, m // 16)
                def _(i):
                    rows = pl.ds(pl.multiple_of(i * 16, 16), 16)
                    there = pl.ds(pl.multiple_of(base + i * 16, 16), 16)
                    acc[a, s % 5, c, rows, :] = part[a, there, :] + stage1[a, c, rows, :]

            x0_push(s, a).start()

        @pl.when(s % 2 == 0)
        def _():
            for a in sums:
                for c in both:
                    y1_push(s, a, c).start()

    def add(a, s, c, base, buf):
        @pl.loop(0, half // 16)
        def _(i):
            rows = pl.ds(pl.multiple_of(base + i * 16, 16), 16)
            there = pl.ds(pl.multiple_of(i * 16, 16), 16)
            acc[a, s % 5, c, rows, :] = acc[a, s % 5, c, rows, :] + buf[there, :]

    def h2_pre(s):
        for a in sums:
            wait_for(x0_in.at[a, s], x0_r.at[a, s])
        begin_all(h2_loads(s))

        @pl.when(s % 2 == 1)
        def _():
            for a in sums:
                for c in both:
                    wait_for(y1_in.at[a, s // 2, c], y1_r.at[a, s // 2, c])
            begin_all(h2_more(s))

    def h2_post(s):
        wait_all(h2_loads(s))
        for a in sums:
            add(a, s, 0, 0, stage2.at[a])

        @pl.when(s % 2 == 0)
        def _():
            for a in sums:
                y0_push(s, a).start()

        @pl.when(s % 2 == 1)
        def _():
            wait_all(h2_more(s))
            for a in sums:
                for c in (1, 0):
                    add(a, s, c, half, stage3.at[a, c])
                x1_push(s, a).start()

    def h3_pre(s):
        for a in sums:
            wait_for(y0_in.at[a, s // 2], y0_r.at[a, s // 2])
            wait_for(x1_in.at[a, s // 2], x1_r.at[a, s // 2])
        begin_all(h3_loads(s))

    def h3_post(s):
        wait_all(h3_loads(s))
        for a in sums:
            for k in both:
                add(a, s, 0, k * half, stage4.at[a, k])

        @pl.when(s > 1)
        def _():
            for a in sums:
                z_push(s, a).start()

        @pl.when(s == 1)
        def _():
            for a in sums:
                own[a] = acc[a, 1, 0]

    def weights():
        pairs = []
        for e in range(experts):
            at = pl.ds(e * hidden, hidden)
            pairs.append((wg_hbm.at[e], w_in.at[at]))
            pairs.append((wu_hbm.at[e], w_in.at[pl.ds(units + e * hidden, hidden)]))
            pairs.append((wd_hbm.at[e], w_down.at[at]))
        some = ws_hbm.shape[2]
        for e in range(ws_hbm.shape[0]):
            across = pl.ds(e * some, some)
            for j, (ref, at) in enumerate(((w_in, routed), (w_in, units + routed), (w_down, routed))):
                part_j = ws_hbm.at[e, pl.ds(j * shared, shared)]
                pairs.append((part_j, ref.at[pl.ds(at, shared), across]))
        pairs.append((wr_hbm, w_in.at[pl.ds(2 * units, total)]))
        return [pltpu.make_async_copy(a, b, wsem.at[i]) for i, (a, b) in enumerate(pairs)]

    first = pltpu.make_async_copy(x_own, x_all.at[net.slot()], lsem.at[0])
    first.start()
    net.greet(net.line() + [net.at(c=c, d=d) for c, d in ((0, 1), (1, 0), (1, 1))])
    first.wait()
    rows_a(0)
    rows_z(1)
    begin_all(weights())
    acc_in[...] = jnp.zeros_like(acc_in)
    acc_down[...] = jnp.zeros_like(acc_down)
    dg[...] = jnp.zeros_like(dg)
    hs[units:, :] = jnp.zeros((hs.shape[0] - units, block), BF16)
    dgu[2 * units :, :] = jnp.zeros((dgu.shape[0] - 2 * units, block), BF16)
    rows_b(0)
    rows_c(0)
    rows_d(0)
    begin_all(block_copies(0, dy_near))
    wait_all(weights())

    last = groups - 1

    @pl.loop(0, groups)
    def _(s):
        r = s // 2
        g = net.group(-r, 1 - s % 2)
        more = r + 1 < far
        pl.when((s % 2 == 0) & more)(lambda: rows_a(r + 1))
        pl.when((s % 2 == 0) & (r + 2 < far))(lambda: rows_z(r + 2))
        pl.when(s > 0)(lambda: h1_pre(s - 1))
        pl.when(s > 2)(lambda: h2_pre(s - 3))
        wait_all(block_copies(s, None))

        @pl.loop(0, block // chunk)
        def _(n):
            at = pl.ds(pl.multiple_of(n * chunk, chunk), chunk)
            h[...] = dot_nt(w_in[...], x[at, :])
            dh[...] = dot_nt(w_down[...], dy[at, :])
            logits = h[2 * units :, :]
            expo = jnp.exp(logits - jnp.max(logits, axis=0, keepdims=True))
            marked = picks[:, pl.ds(pl.multiple_of(g * block + n * chunk, chunk), chunk)]
            gates = expo / jnp.sum(expo, axis=0, keepdims=True) * marked
            for e in range(experts + 1):
                base, count = (e * hidden, hidden) if e < experts else (routed, shared)
                gate = gates[e : e + 1, :] if e < experts else jnp.ones((1, chunk), F32)

                def body(i, total_):
                    a = pl.multiple_of(base + i * TILE, TILE)
                    here = pl.ds(a, TILE)
                    there = pl.ds(pl.multiple_of(units + a, TILE), TILE)
                    hg, hu, d = h[here, :], h[there, :], dh[here, :]
                    sig = 1.0 / (1.0 + jnp.exp(-hg))
                    act = hg * sig
                    dact = sig + act * (1.0 - sig)
                    hid = act * hu
                    hs[here, at] = (hid * gate).astype(BF16)
                    ds = d * gate
                    dgu[here, at] = (ds * hu * dact).astype(BF16)
                    dgu[there, at] = (ds * act).astype(BF16)
                    return total_ + jnp.sum(hid * d, axis=0, keepdims=True)

                row = lax.fori_loop(0, count // TILE, body, jnp.zeros((1, chunk), F32))
                if e < experts:
                    for j in range(per):
                        dg[n * per + j, g, e : e + 1, :] = row[:, j * m : (j + 1) * m]

        pl.when(s > 0)(lambda: h1_post(s - 1))
        pl.when(s > 2)(lambda: h2_post(s - 3))
        pl.when((s > 4) & (s % 2 == 0))(lambda: h3_pre(s - 5))
        pl.when(s == last)(lambda: h3_pre(last - 4))
        pl.when((s % 2 == 1) & more)(lambda: rows_c(r + 1))

        @pl.loop(0, width // 512)
        def _(c):
            at = pl.ds(pl.multiple_of(c * 512, 512), 512)
            acc_in[:, at] += dot_nn(dgu[: 2 * units, :], x[:, at])
            acc_down[:, at] += dot_nn(hs[:units, :], dy[:, at])

        pl.when((s > 4) & (s % 2 == 0))(lambda: h3_post(s - 5))

        @pl.when(s == last)
        def _():
            h3_post(last - 4)
            h2_pre(last - 2)

        pl.when((s % 2 == 1) & more)(lambda: rows_d(r + 1))
        pl.when(s + 1 < groups)(lambda: load_block(s + 1))
        hsn[...] = hs[...].T
        dgun[...] = dgu[...].T

        @pl.when(s > 0)
        def _():
            for c in both:
                core_push(s - 1, 0, c).wait_send()
            ffn_copy(s - 1).wait()

        @pl.loop(0, width // 512)
        def _(c):
            at = pl.ds(pl.multiple_of(c * 512, 512), 512)
            part[0, :, at] = dot_nn(dgun[:, : 2 * units], w_in[: 2 * units, at]).astype(BF16)

        for c in (1, 0):
            core_push(s, 0, c).start()

        @pl.loop(0, width // 512)
        def _(c):
            at = pl.ds(pl.multiple_of(c * 512, 512), 512)
            ffn_part[:, at] = dot_nn(hsn[:, :units], w_down[:, at]).astype(BF16)

        ffn_copy(s).start()
        pl.when(s == last)(lambda: h2_post(last - 2))
        pl.when((s % 2 == 0) & more)(lambda: rows_b(r + 1))

    def stores():
        pairs = []
        for e in range(experts):
            at = pl.ds(e * hidden, hidden)
            pairs.append((acc_in.at[at], gg_hbm.at[e]))
            pairs.append((acc_in.at[pl.ds(units + e * hidden, hidden)], gu_hbm.at[e]))
            pairs.append((acc_down.at[at], gd_hbm.at[e]))
        pairs.append((acc_in.at[pl.ds(routed, shared)], gs_hbm.at[0]))
        pairs.append((acc_in.at[pl.ds(units + routed, shared)], gs_hbm.at[1]))
        pairs.append((acc_down.at[pl.ds(routed, shared)], gs_hbm.at[2]))
        return [pltpu.make_async_copy(a, b, wsem.at[i]) for i, (a, b) in enumerate(pairs)]

    peers = [(c, d) for c in both for d in both][1:]

    def dg_push(k):
        c, d = peers[k]
        e, t = net.at(0, 0, c, d)
        return remote(dg.at[t], dg_in.at[k], dg_s.at[k], dg_r.at[k], (e, t))

    for k in range(3):
        dg_push(k).start()
    h2_pre(last - 1)
    h1_pre(last)
    h2_post(last - 1)
    h1_post(last)
    begin_all(stores())
    for a in sums:
        for c in both:
            wait_for(y1_in.at[a, last // 2, c], y1_r.at[a, last // 2, c])
    begin_all(h2_more(last))
    wait_all(h2_more(last))
    for a in sums:
        for c in (1, 0):
            add(a, last, c, half, stage3.at[a, c])
        x1_push(last, a).start()
    h3_pre(last - 2)
    h3_post(last - 2)
    for k in range(3):
        wait_for(dg_in.at[k], dg_r.at[k])
    dg_sum[...] = dg[net.at()[1]] + dg_in[0] + dg_in[1] + dg_in[2]
    me = net.group()
    dg_out[me] = dg_sum[me]
    others = [(r, b) for r in range(far) for b in both][1:]

    def dg_give(k):
        to = net.at(*others[k])
        return remote(dg_sum.at[to[0]], dg_out.at[me], dg_s.at[3 + k], dg_r.at[3 + k], to)

    for k in range(len(others)):
        dg_give(k).start()
    for a in sums:
        wait_for(x0_in.at[a, last], x0_r.at[a, last])
    begin_all(h2_loads(last))
    wait_all(h2_loads(last))
    for a in sums:
        add(a, last, 0, 0, stage2.at[a])
    h3_pre(last)
    h3_post(last)
    for r in range(1, far):
        for a in sums:
            wait_for(z_in.at[a, r], z_r.at[a, r])
            got = pltpu.make_async_copy(z_in.at[a, r], stage1.at[a, 0], csem.at[a])
            got.start()
            got.wait()

            @pl.loop(0, m // 16)
            def _(i):
                rows = pl.ds(pl.multiple_of(i * 16, 16), 16)
                own[a, rows, :] = own[a, rows, :] + stage1[a, 0, rows, :]

    give = pltpu.make_async_copy(own, outs_hbm, csem.at[0])
    give.start()
    for k in range(len(others)):
        r, b = others[k]
        wait_for(dg_out.at[net.group(-r, b)], dg_r.at[3 + k])
    for s in range(last - 4, last + 1):
        sends_done(s)
    for c in both:
        core_push(last, 0, c).wait_send()
    ffn_copy(last).wait()
    for q in range(4):
        for r in range(far):
            for kind in range(8):
                if r or (kind and q < 2):
                    wait_for(place(q, 0, 0, 0), ag_s.at[q, kind, r])
    for k in range(3):
        dg_push(k).wait_send()
    for k in range(len(others)):
        dg_give(k).wait_send()
    wait_all(stores())
    give.wait()


def experts_all(x, dy_own, dy_near, picks, wg, wu, wd, ws, wr, groups, tensors, ident):
    m, width = x.shape
    far = groups // 2
    experts, hidden, _ = wg.shape
    shared, total = ws.shape[1] // 3, wr.shape[0]
    units = experts * hidden + shared
    block, half = 4 * m, m // 2
    chunk = min(256, block)
    up = lambda v: -(-v // 128) * 128
    like = jax.ShapeDtypeStruct
    outs = [
        like((1, m, width), BF16),
        like((groups, 8, m), F32),
        like(wg.shape, F32),
        like(wu.shape, F32),
        like(wd.shape, F32),
        like((3, shared, width), F32),
        like((groups * tensors, m, width), BF16),
        like((groups * tensors, m, width), BF16),
        like((groups * block, width), BF16),
        like((1, groups, 2, m, width), BF16),
        like((1, groups, half, width), BF16),
        like((1, far, 2, half, width), BF16),
        like((1, far, half, width), BF16),
        like((1, far, half, width), BF16),
        like((1, far, m, width), BF16),
    ]
    dma = pltpu.SemaphoreType.DMA
    scratch = [
        pltpu.VMEM((2 * units + total, width), BF16),
        pltpu.VMEM((units, width), BF16),
        pltpu.VMEM((2 * units + total, chunk), F32),
        pltpu.VMEM((units, chunk), F32),
        pltpu.VMEM((up(units), block), BF16),
        pltpu.VMEM((up(2 * units), block), BF16),
        pltpu.VMEM((block, up(units)), BF16),
        pltpu.VMEM((block, up(2 * units)), BF16),
        pltpu.VMEM((2 * units, width), F32),
        pltpu.VMEM((units, width), F32),
        pltpu.VMEM((block, width), BF16),
        pltpu.VMEM((block, width), BF16),
        pltpu.VMEM((1, block, width), BF16),
        pltpu.VMEM((block, width), BF16),
        pltpu.VMEM((1, 5, 2, m, width), BF16),
        pltpu.VMEM((1, m, width), BF16),
        pltpu.VMEM((1, 2, m, width), BF16),
        pltpu.VMEM((1, half, width), BF16),
        pltpu.VMEM((1, 2, half, width), BF16),
        pltpu.VMEM((1, 2, half, width), BF16),
        pltpu.VMEM((tensors, groups, 8, m), F32),
        pltpu.VMEM((3, groups, 8, m), F32),
        pltpu.VMEM((groups, 8, m), F32),
    ]
    for shape in (
        (4, 8, far), (1, groups, 2), (1, groups), (1, far, 2), (1, far), (1, far), (1, far), (groups + 2,),
    ):
        scratch += [dma(shape), dma(shape)]
    scratch += [dma((3 * experts + 3 * ws.shape[0] + 1,)), dma((9,)), dma((10,))]
    got = pl.pallas_call(
        functools.partial(experts_kernel, (far, experts, hidden, shared, total)),
        out_shape=outs,
        in_specs=[ANY] * 3 + [IN_VMEM] + [ANY] * 5,
        out_specs=[ANY, IN_VMEM] + [ANY] * 13,
        scratch_shapes=scratch,
        compiler_params=params(ident, 63),
        cost_estimate=cost(280),
    )(x, dy_own, dy_near, picks, wg, wu, wd, ws, wr)
    return [*got[:6], got[8]]


BOTH = ("expert", "tensor")


def shards(
    tokens,
    lengths,
    routes,
    gain_attn,
    w_query,
    w_latent,
    gain_latent,
    w_kv,
    w_out,
    gain_ffn,
    w_router,
    w_shared_gate,
    w_shared_up,
    w_shared_down,
    w_gate,
    w_up,
    w_down,
    cotangent,
):
    groups = lax.axis_size("expert")
    tensors = lax.axis_size("tensor")
    eindex = lax.axis_index("expert")
    tindex = lax.axis_index("tensor")
    rows, width = tokens.shape
    quarter = rows // tensors
    experts_local, _, hidden_units = w_gate.shape
    total_experts = experts_local * groups
    every = groups * rows
    bf16, f32 = jnp.bfloat16, jnp.float32

    def own(v):
        return lax.dynamic_slice_in_dim(v, tindex * quarter, quarter, 0)

    live_int = (jnp.arange(rows) < lengths[0]).astype(jnp.int32)
    live = live_int.astype(f32)[:, None]
    live_own = own(live)
    cot_own = own(cotangent).astype(f32)
    dffn_group = (cotangent * live.astype(bf16)).reshape(tensors, quarter, width)

    part = w_shared_down.shape[0] // groups
    spare = -part % TILE

    def shared_units(v):
        v = jnp.pad(v.reshape(groups, part, v.shape[1]), ((0, 0), (0, spare), (0, 0)))
        return v

    shared_w = jnp.stack(
        [shared_units(v) for v in (w_shared_gate.T, w_shared_up.T, w_shared_down)], axis=1
    )
    choose = jnp.any(routes[..., None] == jnp.arange(total_experts), axis=1).astype(F32)
    picks = choose * live
    query_w, kv_up, out_proj, shared_w, marks, dffn_near = begin(
        (w_query, w_kv, w_out),
        shared_w.reshape(groups, -1, shared_w.shape[-1]),
        picks.T.astype(BF16),
        dffn_group,
        groups,
        tensors,
        0,
    )
    query_w = query_w.reshape(width, -1)
    kv_up = kv_up.reshape(KVR, -1)
    if (width // groups) % 128:
        shared_w = shared_w.transpose(1, 0, 2).reshape(1, -1, width)
    gate_t, up_t = w_gate.transpose(0, 2, 1), w_up.transpose(0, 2, 1)
    router_t = jnp.roll(w_router.T, -eindex * experts_local, axis=0)
    parts = max(1, every // 4096)
    some = quarter // parts

    def split(v):
        return v.reshape(parts, some, v.shape[1])

    marks = marks.reshape(groups, total_experts, tensors, parts, some).transpose(3, 1, 0, 2, 4)
    picks_all = marks.reshape(parts, total_experts, -1).astype(F32)
    picks_all = jnp.roll(picks_all, -eindex * experts_local, axis=1)
    xf = tokens.astype(f32)
    cosine, sine = rope_tables(rows, ROPE)
    cosine = jnp.concatenate([cosine, cosine], axis=1)
    sine = jnp.concatenate([-sine, sine], axis=1)
    attend_w = (query_w, w_latent.T, gain_latent[None], kv_up, out_proj, cosine, sine)
    partial, *kept = attend(tokens, gain_attn[None], *attend_w)
    scale_one = own(kept[-1])
    normed_one = own(xf) * scale_one
    partial = partial.reshape(tensors, quarter, width)
    attn = sum_tensor(partial, groups, parts + 2)
    resid = own(xf) + live_own * attn
    scale_two = inv_rms(resid)
    normed_two = resid * scale_two
    xn2_own = (normed_two * gain_ffn).astype(bf16)
    router = jax.nn.softmax(mat(xn2_own, w_router), axis=-1)
    outs = []
    for k in range(parts):
        dx, dgates, *grads, ffn = experts_all(
            split(xn2_own)[k],
            dffn_group[:, k * some : (k + 1) * some],
            dffn_near[:, k * some : (k + 1) * some],
            picks_all[k],
            gate_t,
            up_t,
            w_down,
            shared_w,
            router_t,
            groups,
            tensors,
            k + 1,
        )
        dx = dx[0].astype(F32)
        ffn = ffn.reshape(-1, some, width)
        if parts > 1:
            ffn = reduce_rows(ffn, groups, parts + 4 + k)
        dgates = dgates[:, :experts_local].reshape(total_experts, some).T
        outs.append((ffn, dx, dgates, *grads))
    dx, dgates = (jnp.concatenate(v, axis=0) for v in list(zip(*outs))[1:3])
    ffn = outs[0][0] if parts == 1 else jnp.concatenate([v[0] for v in outs], axis=0)
    grads = [functools.reduce(jnp.add, v) for v in list(zip(*outs))[3:]]
    drouter = own(picks) * dgates
    grad_gate, grad_up = (v.transpose(0, 2, 1) for v in grads[:2])
    grad_down = grads[2]
    dlogit = router * (drouter - jnp.sum(router * drouter, axis=-1, keepdims=True))
    grad_router = mat_tn(dlogit.astype(bf16), xn2_own)
    dnorm_two = dx + mat_nt(dlogit.astype(bf16), w_router)
    grad_gain_ffn = jnp.sum(dnorm_two * normed_two, axis=0)
    dresid = cot_own + norm_back(dnorm_two, normed_two, scale_two, gain_ffn)
    shared_g = grads[3].reshape(3, part + spare, groups, width // groups).astype(BF16)
    shared_g = shared_g.transpose(2, 0, 1, 3).reshape(groups, -1, width // groups)
    dattn, shared_g = gather_tensor((dresid * live_own).astype(bf16), shared_g, groups, tensors, parts + 3)
    dattn = dattn.reshape(rows, width)
    grad_query, grad_kv, grad_out, grad_latent, grad_gain_attn, grad_gain_latent, dnorm_one = (
        attend_back(dattn, tokens, kept, *attend_w)
    )
    down = cells(groups, tensors)[0]

    def whole_cells(v):
        return jnp.pad(v, ((0, -v.shape[0] % (16 * down)), (0, 0)))

    latent_g = whole_cells(grad_latent)
    misc = jnp.concatenate(
        [
            grad_router,
            grad_gain_attn,
            grad_gain_ffn[None],
            jnp.pad(grad_gain_latent, ((0, 0), (0, width - KVR))),
        ],
        axis=0,
    )
    misc = whole_cells(misc.astype(bf16))
    grad_query, grad_kv, grad_out, small, grad_tokens, output = finish(
        (
            grad_query.reshape(groups, -1, grad_query.shape[1]),
            grad_kv.reshape(groups, -1, grad_kv.shape[1]),
            grad_out,
        ),
        latent_g,
        misc,
        dnorm_one.reshape(tensors, quarter, width),
        ffn,
        (dresid, normed_one, scale_one, gain_attn[None], resid, live_own),
        groups,
        tensors,
        parts + 1,
    )
    grad_tokens = grad_tokens.reshape(rows, width)
    output = output.reshape(rows, width)
    small = small.reshape(down, -1, width)
    tall = latent_g.shape[0] // down
    grad_latent = small[:, :tall].reshape(-1, width)[: w_latent.shape[1]].astype(f32).T
    misc = small[:, tall:].reshape(-1, width).astype(f32)
    grad_router = misc[:total_experts].T
    grad_gain_attn = misc[total_experts]
    grad_gain_ffn = misc[total_experts + 1]
    grad_gain_latent = misc[total_experts + 2, :KVR]
    shared_g = shared_g.reshape(groups, 3, part + spare, -1)[:, :, :part].transpose(1, 0, 2, 3)
    shared_g = shared_g.reshape(3, groups * part, -1).astype(f32)
    grad_sgate, grad_sup, grad_sdown = shared_g[0].T, shared_g[1].T, shared_g[2]
    return (
        output,
        grad_tokens,
        grad_gain_attn,
        grad_query,
        grad_latent,
        grad_gain_latent,
        grad_kv,
        grad_out,
        grad_gain_ffn,
        grad_router,
        grad_sgate,
        grad_sup,
        grad_sdown,
        grad_gate,
        grad_up,
        grad_down,
    )


def solution(mesh):
    in_specs = (
        P("expert", None),
        P("expert"),
        P("expert", None),
        P(),
        P("expert", "tensor"),
        P(),
        P(),
        P("expert", "tensor"),
        P("tensor", "expert"),
        P(),
        P(),
        P("expert", "tensor"),
        P("expert", "tensor"),
        P("tensor", "expert"),
        P("expert", None, "tensor"),
        P("expert", None, "tensor"),
        P("expert", "tensor", None),
        P("expert", None),
    )
    out_specs = (
        P("expert", None),
        P("expert", None),
        P(),
        P("expert", "tensor"),
        P(),
        P(),
        P("expert", "tensor"),
        P("tensor", "expert"),
        P(),
        P(),
        P("expert", "tensor"),
        P("expert", "tensor"),
        P("tensor", "expert"),
        P("expert", None, "tensor"),
        P("expert", None, "tensor"),
        P("expert", "tensor", None),
    )
    return jax.shard_map(shards, mesh=mesh, in_specs=in_specs, out_specs=out_specs, check_vma=False)
```
